32 devices in a mesh: groups: 2 (over y), patch: 4 (over z), head: 2 (over x), sub: 2 (over core).
Axes of the slice: x: 2, y: 2, z: 4, core: 2. Of those that a mesh axis runs over, the one named last changes fastest.
Arguments:
- queries: bfloat16 [768, 1024], P(('groups', 'patch'), ('head', 'sub')), parts along dimension 0, may hold values from -112 to 112
- held_keys: bfloat16 [768, 1024], P('groups', ('head', 'sub')), parts along dimension 0, may hold values from -4 to 4
- held_values: bfloat16 [768, 1024], P('groups', ('head', 'sub')), parts along dimension 0, may hold values from -4 to 4
- key_change: float32 [768, 1024], P(('groups', 'patch'), ('head', 'sub')), parts along dimension 0, may hold values from -0.6 to 0.6
- value_change: float32 [768, 1024], P(('groups', 'patch'), ('head', 'sub')), parts along dimension 0, may hold values from -1.8 to 1.8
- out_weight: bfloat16 [1024, 5120], P(('head', 'sub')), may hold values from -0.25 to 0.25
- hidden_in: bfloat16 [768, 5120], P(('groups', 'patch'), ('head', 'sub')), parts along dimension 0, may hold values from -3 to 3
- gate: float32 [10240], P(('groups', 'head', 'sub')), parts along dimension 0, may hold values from 0.5 to 2.5
Outputs:
- block_out: bfloat16 [768, 5120], P(('groups', 'patch'), ('head', 'sub')), parts along dimension 0
The draws below stay inside these ranges and needn't reach their ends.
There are 2 independent parts, one for each index of `groups`. The reference program is written for one: setup_inputs(seed, part) draws one part's arguments, and reference() takes and returns one part's arrays. A program takes and returns all parts, laid end to end along the dimension named above; an argument that names none is the same for every part. Nothing has to cross between parts.
All inputs are finite; a program needn't handle non-finite values.
Results may differ from the reference program's by a relative error of at most 0.0044.
Values may be sent and summed in bfloat16 or wider, within the bound.
No kernel may reach another device: no remote copies, remote signals or barrier semaphores. Data moves between devices by JAX's collectives and lax.ppermute only.
A program may use at most 64 MiB of HBM per device.

```python
import math
import jax
import jax.numpy as jnp
from jax import lax

D = 5120
HD = 128
HEADS = 8
HW = 1024
TOKENS = 384


def shared_keys(key):
    return jnp.clip(jax.random.normal(key, (TOKENS, HW), jnp.float32), -4.0, 4.0)


def draw_held_keys(key, part):
    base = shared_keys(key)
    return base.astype(jnp.bfloat16)


def draw_queries(key, part):
    key = jax.random.fold_in(key, 23)
    drawn = 2.0 * jnp.clip(jax.random.normal(key, (TOKENS, HW), jnp.float32), -4.0, 4.0)
    return drawn.astype(jnp.bfloat16)


def spiked(entries, own_key, source, target, blocks, factor):
    def block_of(axis_at):
        return (jnp.arange(entries.shape[axis_at]) // (entries.shape[axis_at] // blocks)).reshape((-1,) + (1,) * (entries.ndim - 1 - axis_at))

    near = jax.random.permutation(own_key, blocks)[block_of(target)]
    far = (block_of(target) + blocks // 2) % blocks
    return jnp.where((block_of(source) == near) | (block_of(source) == far), factor * entries, entries)


def level_of(stream_key, dims, split, smallest, top_value):
    factor_of = 1.0
    for dim, blocks in split:
        steps = jax.random.uniform(jax.random.fold_in(jax.random.fold_in(stream_key, 6), dim), (blocks,), jnp.float32, smallest / len(split), top_value / len(split))
        factor_of = factor_of * jnp.repeat(jnp.exp(steps), dims[dim] // blocks).reshape((-1,) + (1,) * (len(dims) - 1 - dim))
    return factor_of


def noise(own_key, dims, deviation, bound, shards=(), kind=jnp.bfloat16):
    level = level_of(own_key, dims, shards, -0.22, 0.18) if shards else 1.0
    array = jax.random.normal(own_key, dims, jnp.float32) * deviation * level
    return jnp.minimum(jnp.maximum(array, -bound), bound).astype(kind)


def noise_with(stream_key, dims, scale, limit, cuts, heavy, kind=jnp.bfloat16):
    entries = scale * jax.random.normal(stream_key, dims, jnp.float32)
    if cuts:
        entries = entries * level_of(stream_key, dims, cuts, -0.22, 0.18)
    return jnp.clip(spiked(entries, jax.random.fold_in(stream_key, 3), *heavy), -limit, limit).astype(kind)


def setup_inputs(seed: int = 0, part: int = 0) -> dict:
    streams_of = jax.random.split(jax.random.key(seed), 9)
    part_keys = jax.random.split(jax.random.fold_in(streams_of[8], part), 9)
    return {
        "queries": draw_queries(jax.random.fold_in(jax.random.fold_in(streams_of[8], part), 71), part),
        "held_keys": draw_held_keys(jax.random.fold_in(jax.random.fold_in(streams_of[8], part), 71), part),
        "held_values": noise(part_keys[2], (TOKENS, HW), 1.0, 4.0, ((1, 4),)),
        "key_change": noise(part_keys[3], (TOKENS, HW), 0.1, 0.6, ((0, 4), (1, 4)), jnp.float32),
        "value_change": noise(part_keys[4], (TOKENS, HW), 0.3, 1.8, ((0, 4), (1, 4)), jnp.float32),
        "out_weight": noise_with(streams_of[5], (HW, D), HW ** -0.5, 0.25, ((0, 4),), (0, 1, 4, 2.0)),
        "hidden_in": noise(part_keys[6], (TOKENS, D), 0.5, 3.0, ((0, 4), (1, 4))),
        "gate": jnp.clip(0.5 + 2.0 * jax.random.uniform(part_keys[7], (D,), jnp.float32) ** level_of(part_keys[7], (D,), ((0, 4),), -0.2, 0.2), 0.5, 2.5),
    }


def reference(queries, held_keys, held_values, key_change, value_change, out_weight, hidden_in, gate):
    key_residual = key_change.astype(jnp.bfloat16)
    value_residual = value_change.astype(jnp.bfloat16)
    keys = held_keys.astype(jnp.float32) + key_residual.astype(jnp.float32)
    values = held_values.astype(jnp.float32) + value_residual.astype(jnp.float32)
    scale = 1.0 / math.sqrt(HD)
    query_heads = queries.astype(jnp.float32).reshape(TOKENS, HEADS, HD).transpose(1, 0, 2)
    key_heads = keys.reshape(TOKENS, HEADS, HD).transpose(1, 0, 2)
    value_heads = values.reshape(TOKENS, HEADS, HD).transpose(1, 0, 2)

    def one_head(triple):
        query_block, key_block, value_block = triple
        scores = jnp.dot(query_block, key_block.T, precision=lax.Precision.HIGHEST) * scale
        highest = lax.optimization_barrier(jnp.max(scores, axis=1, keepdims=True))
        weights = jnp.exp(scores - highest)
        totals = lax.optimization_barrier(jnp.sum(weights, axis=1, keepdims=True))
        return jnp.dot(weights, value_block, precision=lax.Precision.HIGHEST) / totals
    attended_heads = lax.map(one_head, (query_heads, key_heads, value_heads))
    attended = attended_heads.transpose(1, 0, 2).reshape(TOKENS, HW).astype(jnp.bfloat16)
    projected = jnp.dot(attended, out_weight, preferred_element_type=jnp.float32)
    return (hidden_in.astype(jnp.float32) + gate[None, :] * projected).astype(jnp.bfloat16)
```

```python
import functools
import math

import jax
import jax.numpy as jnp
from jax import lax
from jax.experimental import pallas as pl
from jax.experimental.pallas import tpu as pltpu
from jax.sharding import PartitionSpec as P

HD = 128


def shift(array, axis, size, step):
    pairs = [(i, (i + step) % size) for i in range(size)]
    return lax.ppermute(array, axis, pairs)


def attention_kernel(scale, patch, patches, q_ref, held_k_ref, held_v_ref, *refs):
    residual_refs, out_ref = refs[:-1], refs[-1]
    rows, width = q_ref.shape
    me = lax.axis_index(patch)
    starts = [
        pl.multiple_of(lax.rem(me + patches - i, patches) * rows, rows) for i in range(patches)
    ]
    for head in range(width // HD):
        cols = slice(head * HD, (head + 1) * HD)
        value_cols = slice(width + head * HD, width + (head + 1) * HD)
        keys = jnp.concatenate(
            [
                jnp.concatenate([held_k_ref[pl.ds(at, rows), cols], ref[:, cols]], axis=1)
                for at, ref in zip(starts, residual_refs)
            ],
            axis=0,
        )
        values = jnp.concatenate(
            [
                jnp.concatenate([held_v_ref[pl.ds(at, rows), cols], ref[:, value_cols]], axis=1)
                for at, ref in zip(starts, residual_refs)
            ],
            axis=0,
        )
        q = q_ref[:, cols]
        products = lax.dot_general(
            jnp.concatenate([q, q], axis=1),
            keys,
            (((1,), (1,)), ((), ())),
            preferred_element_type=jnp.float32,
        )
        scores = products * scale
        weights = jnp.exp(scores - jnp.max(scores, axis=1, keepdims=True))
        totals = jnp.sum(weights, axis=1, keepdims=True)
        high = weights.astype(jnp.bfloat16)
        low = (weights - high.astype(jnp.float32)).astype(jnp.bfloat16)
        sums = jnp.dot(
            jnp.concatenate([high, low], axis=0), values, preferred_element_type=jnp.float32
        )
        sums = sums[:rows] + sums[rows:]
        sums = sums[:, :HD] + sums[:, HD:]
        out_ref[:, cols] = (sums / totals).astype(jnp.bfloat16)


def solution(mesh):
    patches, heads, subs = mesh.shape["patch"], mesh.shape["head"], mesh.shape["sub"]

    def per_device(
        queries, held_keys, held_values, key_change, value_change, out_weight, hidden_in, gate
    ):
        rows, width = queries.shape
        columns = hidden_in.shape[1]
        sub = lax.axis_index("sub")
        head = lax.axis_index("head")

        with jax.named_scope("residual_gather"):
            residual = jnp.concatenate(
                [key_change.astype(jnp.bfloat16), value_change.astype(jnp.bfloat16)], axis=1
            )
            residuals = [residual] + [
                shift(residual, "patch", patches, i) for i in range(1, patches)
            ]

        def weight_block(weight, of_head, of_sub):
            at = (of_head * subs + of_sub) * columns
            return lax.dynamic_slice(weight, (0, at), (width, columns))

        with jax.named_scope("weight_swap"):
            weights = []
            for step in range(heads):
                of_head = lax.rem(head + step, heads)
                parts = [weight_block(out_weight, of_head, sub)]
                for i in range(1, subs):
                    away = weight_block(out_weight, of_head, lax.rem(sub + i, subs))
                    parts.append(shift(away, "sub", subs, i))
                weights.append(parts)

        with jax.named_scope("attention"):
            attended = pl.pallas_call(
                functools.partial(attention_kernel, 1.0 / math.sqrt(HD), "patch", patches),
                out_shape=jax.ShapeDtypeStruct((rows, width), jnp.bfloat16),
                in_specs=[pl.BlockSpec(memory_space=pltpu.VMEM)] * (3 + patches),
                out_specs=pl.BlockSpec(memory_space=pltpu.VMEM),
                compiler_params=pltpu.CompilerParams(vmem_limit_bytes=8 * 1024 * 1024),
            )(queries, held_keys, held_values, *residuals)

        with jax.named_scope("attended_swap"):
            attended_parts = [attended] + [
                shift(attended, "sub", subs, i) for i in range(1, subs)
            ]

        def project(parts):
            total = 0.0
            for rows_of, weight in zip(attended_parts, parts):
                total = total + jnp.dot(rows_of, weight, preferred_element_type=jnp.float32)
            return total

        with jax.named_scope("projection"):
            arrived = []
            for step in range(1, heads):
                term = project(weights[step]).astype(jnp.bfloat16)
                arrived.append(shift(term, "head", heads, step))
            total = project(weights[0])
            for term in arrived:
                total = total + term.astype(jnp.float32)
            return (hidden_in.astype(jnp.float32) + gate[None, :] * total).astype(jnp.bfloat16)

    in_specs = (
        P(("groups", "patch"), ("head", "sub")),
        P("groups", ("head", "sub")),
        P("groups", ("head", "sub")),
        P(("groups", "patch"), ("head", "sub")),
        P(("groups", "patch"), ("head", "sub")),
        P(("head", "sub"), None),
        P(("groups", "patch"), ("head", "sub")),
        P(("groups", "head", "sub")),
    )
    out_specs = P(("groups", "patch"), ("head", "sub"))
    return jax.shard_map(
        per_device, mesh=mesh, in_specs=in_specs, out_specs=out_specs, check_vma=False
    )
```

```python
import functools
import math

import jax
import jax.numpy as jnp
from jax import lax
from jax.experimental import pallas as pl
from jax.experimental.pallas import tpu as pltpu
from jax.sharding import PartitionSpec as P

HD = 128
LANES = 128
VMEM_LIMIT = 12 * 1024 * 1024

IN_VMEM = pl.BlockSpec(memory_space=pltpu.VMEM)
ANYWHERE = pl.BlockSpec(memory_space=pl.ANY)


def call(kernel, out_shape, in_specs, out_specs, name, flops=0, moved=0, scratch_shapes=()):
    return pl.pallas_call(
        kernel,
        out_shape=out_shape,
        in_specs=in_specs,
        out_specs=out_specs,
        scratch_shapes=scratch_shapes,
        name=name,
        cost_estimate=pl.CostEstimate(flops=flops, bytes_accessed=moved, transcendentals=0),
        compiler_params=pltpu.CompilerParams(vmem_limit_bytes=VMEM_LIMIT),
    )


def shift(array, axis, size, step):
    return lax.ppermute(array, axis, [(i, (i + step) % size) for i in range(size)])


def gather_line_of_four(own):
    first = lax.ppermute(own, "patch", [(0, 2), (2, 3), (3, 1), (1, 0)])
    second = lax.ppermute(own, "patch", [(0, 1), (1, 3), (3, 2), (2, 0)])
    middle = lax.ppermute(own, "patch", [(1, 2), (2, 1)])
    ends = lax.ppermute(first, "patch", [(2, 3), (1, 0)])
    return [own, first, second, middle, ends]


def line_of_four_sources(place):
    def table(*entries):
        value = jnp.int32(entries[0])
        for i, entry in enumerate(entries[1:], 1):
            value = jnp.where(place == i, jnp.int32(entry), value)
        return value

    return [place, table(1, 3, 0, 2), table(2, 0, 3, 1), table(3, 2, 1, 0)]


def attention_kernel(scale, patches, q_ref, held_k_ref, held_v_ref, *refs):
    block_refs, out_ref = refs[:-1], refs[-1]
    rows, width = q_ref.shape
    me = lax.axis_index("patch")
    if patches == 4:
        sources = line_of_four_sources(me)
        inner = jnp.logical_and(me > 0, me < 3)
        last = jnp.where(inner, block_refs[3][...], block_refs[4][...])
        blocks = [ref[...] for ref in block_refs[:3]] + [last]
    else:
        sources = [lax.rem(me + patches - i, patches) for i in range(patches)]
        blocks = [ref[...] for ref in block_refs]
    starts = [pl.multiple_of(source * rows, rows) for source in sources]
    for head in range(width // HD):
        cols = slice(head * HD, (head + 1) * HD)
        value_cols = slice(width + head * HD, width + (head + 1) * HD)
        keys = jnp.concatenate(
            [
                jnp.concatenate([held_k_ref[pl.ds(at, rows), cols], block[:, cols]], axis=1)
                for at, block in zip(starts, blocks)
            ],
            axis=0,
        )
        values = jnp.concatenate(
            [
                jnp.concatenate([held_v_ref[pl.ds(at, rows), cols], block[:, value_cols]], axis=1)
                for at, block in zip(starts, blocks)
            ],
            axis=0,
        )
        q = q_ref[:, cols]
        products = lax.dot_general(
            jnp.concatenate([q, q], axis=1),
            keys,
            (((1,), (1,)), ((), ())),
            preferred_element_type=jnp.float32,
        )
        scores = products * scale
        weights = jnp.exp(scores - jnp.max(scores, axis=1, keepdims=True))
        totals = jnp.sum(weights, axis=1, keepdims=True)
        high = weights.astype(jnp.bfloat16)
        low = (weights - high.astype(jnp.float32)).astype(jnp.bfloat16)
        sums = jnp.dot(
            jnp.concatenate([high, low], axis=0), values, preferred_element_type=jnp.float32
        )
        sums = sums[:rows] + sums[rows:]
        sums = sums[:, :HD] + sums[:, HD:]
        out_ref[:, cols] = (sums / totals).astype(jnp.bfloat16)


def slices_kernel(heads, subs, columns, weight_ref, after_1_ref, after_2_ref, *refs):
    out_refs, sems = refs[:-1], refs[-1]
    head, sub = lax.axis_index("head"), lax.axis_index("sub")
    copies = []
    for n, out_ref in enumerate(out_refs):
        step, i = n // subs, n % subs
        block = lax.rem(head + step, heads) * subs + lax.rem(sub + i, subs)
        at = pl.multiple_of(block * columns, LANES)
        copies.append(
            pltpu.make_async_copy(weight_ref.at[:, pl.ds(at, columns)], out_ref, sems.at[n])
        )
    for copy in copies:
        copy.start()
    for copy in copies:
        copy.wait()


def dot(a_ref, b_ref):
    return jnp.dot(a_ref[...], b_ref[...], preferred_element_type=jnp.float32)


def own_term_kernel(attended_ref, weight_ref, out_ref):
    out_ref[...] = dot(attended_ref, weight_ref)


def sent_term_kernel(total_ref, *refs):
    out_ref = refs[-1]
    total = total_ref[...]
    for attended_ref, weight_ref in zip(refs[:-1:2], refs[1:-1:2]):
        total = total + dot(attended_ref, weight_ref)
    out_ref[...] = total.astype(jnp.bfloat16)


def base_kernel(hidden_ref, gate_ref, *refs):
    out_ref = refs[-1]
    total = 0.0
    for attended_ref, weight_ref in zip(refs[:-1:2], refs[1:-1:2]):
        total = total + dot(attended_ref, weight_ref)
    out_ref[...] = hidden_ref[...].astype(jnp.float32) + gate_ref[...] * total


def final_kernel(base_ref, gate_ref, *refs):
    arrived_refs, out_ref = refs[:-1], refs[-1]
    total = 0.0
    for ref in arrived_refs:
        total = total + ref[...].astype(jnp.float32)
    out_ref[...] = (base_ref[...] + gate_ref[...] * total).astype(jnp.bfloat16)


def solution(mesh):
    patches, heads, subs = mesh.shape["patch"], mesh.shape["head"], mesh.shape["sub"]

    def per_device(
        queries, held_keys, held_values, key_change, value_change, out_weight, hidden_in, gate
    ):
        rows, width = queries.shape
        columns = hidden_in.shape[1]

        with jax.named_scope("residual_gather"):
            residual = jnp.concatenate(
                [key_change.astype(jnp.bfloat16), value_change.astype(jnp.bfloat16)], axis=1
            )
            if patches == 4:
                blocks = gather_line_of_four(residual)
            else:
                blocks = [residual] + [
                    shift(residual, "patch", patches, i) for i in range(1, patches)
                ]

        with jax.named_scope("weight_swap"):
            if columns % LANES == 0:
                block_shape = jax.ShapeDtypeStruct((width, columns), jnp.bfloat16)
                count = heads * subs
                slices = call(
                    functools.partial(slices_kernel, heads, subs, columns),
                    [block_shape] * count,
                    [pl.BlockSpec(memory_space=pltpu.HBM), ANYWHERE, ANYWHERE],
                    [IN_VMEM] * count,
                    "weight_slices",
                    moved=2 * 2 * width * columns * count,
                    scratch_shapes=[pltpu.SemaphoreType.DMA((count,))],
                )(out_weight, *blocks[2:4])
            else:
                head, sub = lax.axis_index("head"), lax.axis_index("sub")
                slices = []
                for step in range(heads):
                    for i in range(subs):
                        block = lax.rem(head + step, heads) * subs + lax.rem(sub + i, subs)
                        slices.append(
                            lax.dynamic_slice(out_weight, (0, block * columns), (width, columns))
                        )
            weights = [
                [
                    slices[step * subs + i] if i == 0
                    else shift(slices[step * subs + i], "sub", subs, i)
                    for i in range(subs)
                ]
                for step in range(heads)
            ]

        with jax.named_scope("attention"):
            attended = call(
                functools.partial(attention_kernel, 1.0 / math.sqrt(HD), patches),
                jax.ShapeDtypeStruct((rows, width), jnp.bfloat16),
                [IN_VMEM] * (3 + len(blocks)),
                IN_VMEM,
                "attention",
                flops=20_000_000_000,
            )(queries, held_keys, held_values, *blocks)

        with jax.named_scope("attended_swap"):
            attended_parts = [attended] + [
                shift(attended, "sub", subs, i) for i in range(1, subs)
            ]

        term = jax.ShapeDtypeStruct((rows, columns), jnp.float32)
        sent = jax.ShapeDtypeStruct((rows, columns), jnp.bfloat16)
        product_flops = 2 * rows * width * columns
        with jax.named_scope("projection"):
            arrived = []
            for step in range(1, heads):
                own = call(
                    own_term_kernel, term, [IN_VMEM] * 2, IN_VMEM, "own_term", product_flops
                )(attended, weights[step][0])
                pairs = [
                    x for i in range(1, subs) for x in (attended_parts[i], weights[step][i])
                ]
                total = call(
                    sent_term_kernel,
                    sent,
                    [IN_VMEM] * (1 + len(pairs)),
                    IN_VMEM,
                    "sent_term",
                    product_flops,
                )(own, *pairs)
                arrived.append(shift(total, "head", heads, step))
            gate_row = gate.reshape(1, columns)
            pairs = [x for i in range(subs) for x in (attended_parts[i], weights[0][i])]
            base = call(
                base_kernel,
                term,
                [IN_VMEM] * (2 + len(pairs)),
                IN_VMEM,
                "base",
                2 * product_flops,
            )(hidden_in, gate_row, *pairs)
            return call(
                final_kernel,
                sent,
                [IN_VMEM] * (2 + len(arrived)),
                IN_VMEM,
                "final",
                moved=rows * columns * 8,
            )(base, gate_row, *arrived)

    in_specs = (
        P(("groups", "patch"), ("head", "sub")),
        P("groups", ("head", "sub")),
        P("groups", ("head", "sub")),
        P(("groups", "patch"), ("head", "sub")),
        P(("groups", "patch"), ("head", "sub")),
        P(("head", "sub"), None),
        P(("groups", "patch"), ("head", "sub")),
        P(("groups", "head", "sub")),
    )
    out_specs = P(("groups", "patch"), ("head", "sub"))
    return jax.shard_map(
        per_device, mesh=mesh, in_specs=in_specs, out_specs=out_specs, check_vma=False
    )
```

```python
import functools
import math

import jax
import jax.numpy as jnp
from jax import lax
from jax.experimental import pallas as pl
from jax.experimental.pallas import tpu as pltpu
from jax.sharding import PartitionSpec as P

HD = 128
LANES = 128
VMEM_LIMIT = 12 * 1024 * 1024

IN_VMEM = pl.BlockSpec(memory_space=pltpu.VMEM)
ANYWHERE = pl.BlockSpec(memory_space=pl.ANY)


def call(
    kernel,
    out_shape,
    in_specs,
    out_specs,
    name,
    flops=0,
    moved=0,
    scratch_shapes=(),
    vmem=VMEM_LIMIT,
):
    return pl.pallas_call(
        kernel,
        out_shape=out_shape,
        in_specs=in_specs,
        out_specs=out_specs,
        scratch_shapes=scratch_shapes,
        name=name,
        cost_estimate=pl.CostEstimate(flops=flops, bytes_accessed=moved, transcendentals=0),
        compiler_params=pltpu.CompilerParams(vmem_limit_bytes=vmem),
    )


def shift(array, axis, size, step):
    return lax.ppermute(array, axis, [(i, (i + step) % size) for i in range(size)])


LINE_OF_FOUR = (
    ([(0, 2), (2, 3), (3, 1), (1, 0)], (1, 3, 0, 2)),
    ([(0, 1), (1, 3), (3, 2), (2, 0)], (2, 0, 3, 1)),
    ([(0, 3), (3, 0), (1, 2), (2, 1)], (3, 2, 1, 0)),
)


def gather_permutes(patches):
    if patches == 4:
        return [pairs for pairs, _ in LINE_OF_FOUR]
    return [
        [(i, (i + step) % patches) for i in range(patches)] for step in range(1, patches)
    ]


def gather_sources(patches, place):
    if patches == 4:
        sources = [place]
        for _, table in LINE_OF_FOUR:
            source = jnp.int32(table[0])
            for i in range(1, 4):
                source = jnp.where(place == i, jnp.int32(table[i]), source)
            sources.append(source)
        return sources
    return [lax.rem(place + patches - step, patches) for step in range(patches)]


def stage_kernel(patches, q_ref, held_k_ref, held_v_ref, products_ref, values_ref):
    rows, width = q_ref.shape
    sources = gather_sources(patches, lax.axis_index("patch"))
    starts = [pl.multiple_of(source * rows, rows) for source in sources]
    for i, at in enumerate(starts):
        values_ref[i * rows : (i + 1) * rows, :] = held_v_ref[pl.ds(at, rows), :]
    for head in range(width // HD):
        cols = slice(head * HD, (head + 1) * HD)
        keys = jnp.concatenate([held_k_ref[pl.ds(at, rows), cols] for at in starts], axis=0)
        products_ref[head] = dot_transposed(q_ref[:, cols], keys)


def dot_transposed(a, b):
    return lax.dot_general(
        a, b, (((1,), (1,)), ((), ())), preferred_element_type=jnp.float32
    )


def attention_kernel(scale, q_ref, products_ref, values_ref, *refs):
    block_refs, out_ref = refs[:-1], refs[-1]
    rows, width = q_ref.shape
    blocks = jnp.concatenate([ref[...] for ref in block_refs], axis=0)
    for head in range(width // HD):
        cols = slice(head * HD, (head + 1) * HD)
        value_cols = slice(width + head * HD, width + (head + 1) * HD)
        products = products_ref[head] + dot_transposed(q_ref[:, cols], blocks[:, cols])
        scores = products * scale
        weights = jnp.exp(scores - jnp.max(scores, axis=1, keepdims=True))
        totals = jnp.sum(weights, axis=1, keepdims=True)
        high = weights.astype(jnp.bfloat16)
        low = (weights - high.astype(jnp.float32)).astype(jnp.bfloat16)
        sums = jnp.dot(
            jnp.concatenate([high, low], axis=0),
            jnp.concatenate([values_ref[:, cols], blocks[:, value_cols]], axis=1),
            preferred_element_type=jnp.float32,
        )
        sums = sums[:rows] + sums[rows:]
        sums = sums[:, :HD] + sums[:, HD:]
        out_ref[:, cols] = (sums / totals).astype(jnp.bfloat16)


def block_dot(a_ref, weight_ref, block, columns):
    if block is None:
        weight = weight_ref[...]
    else:
        weight = weight_ref[:, pl.ds(pl.multiple_of(block * columns, LANES), columns)]
    return jnp.dot(a_ref[...], weight, preferred_element_type=jnp.float32)


def block_at(step, heads, subs):
    return lax.rem(lax.axis_index("head") + step, heads) * subs + lax.axis_index("sub")


def own_term_kernel(block_of, attended_ref, weight_ref, out_ref):
    out_ref[...] = block_dot(attended_ref, weight_ref, block_of(), out_ref.shape[1])


def sent_term_kernel(block_of, total_ref, *refs):
    out_ref = refs[-1]
    block, columns = block_of(), out_ref.shape[1]
    total = total_ref[...]
    for attended_ref, weight_ref in zip(refs[:-1:2], refs[1:-1:2]):
        total = total + block_dot(attended_ref, weight_ref, block, columns)
    out_ref[...] = total.astype(jnp.bfloat16)


def base_kernel(block_of, hidden_ref, gate_ref, *refs):
    out_ref = refs[-1]
    block, columns = block_of(), out_ref.shape[1]
    total = 0.0
    for attended_ref, weight_ref in zip(refs[:-1:2], refs[1:-1:2]):
        total = total + block_dot(attended_ref, weight_ref, block, columns)
    out_ref[...] = hidden_ref[...].astype(jnp.float32) + gate_ref[...] * total


def final_kernel(base_ref, gate_ref, *refs):
    arrived_refs, out_ref = refs[:-1], refs[-1]
    total = 0.0
    for ref in arrived_refs:
        total = total + ref[...].astype(jnp.float32)
    out_ref[...] = (base_ref[...] + gate_ref[...] * total).astype(jnp.bfloat16)


def solution(mesh):
    patches, heads, subs = mesh.shape["patch"], mesh.shape["head"], mesh.shape["sub"]

    def per_device(
        queries, held_keys, held_values, key_change, value_change, out_weight, hidden_in, gate
    ):
        rows, width = queries.shape
        columns = hidden_in.shape[1]

        with jax.named_scope("residual_gather"):
            low = jnp.float32(-jnp.inf)
            residual = jnp.maximum(
                lax.pad(key_change, low, ((0, 0, 0), (0, width, 0))),
                lax.pad(value_change, low, ((0, 0, 0), (width, 0, 0))),
            ).astype(jnp.bfloat16)
            blocks = [residual] + [
                lax.ppermute(residual, "patch", pairs) for pairs in gather_permutes(patches)
            ]

        with jax.named_scope("weight_swap"):
            weights = [out_weight] + [
                shift(out_weight, "sub", subs, i) for i in range(1, subs)
            ]

        def weight_and_block(i, step):
            if columns % LANES == 0:
                return weights[i], functools.partial(block_at, step, heads, subs)
            at = block_at(step, heads, subs) * columns
            return lax.dynamic_slice(weights[i], (0, at), (width, columns)), lambda: None

        tokens = rows * patches
        with jax.named_scope("attention"):
            products, values = call(
                functools.partial(stage_kernel, patches),
                [
                    jax.ShapeDtypeStruct((width // HD, rows, tokens), jnp.float32),
                    jax.ShapeDtypeStruct((tokens, width), jnp.bfloat16),
                ],
                [IN_VMEM] * 3,
                [IN_VMEM] * 2,
                "stage",
                flops=2_000_000_000,
            )(queries, held_keys, held_values)
            attended = call(
                functools.partial(attention_kernel, 1.0 / math.sqrt(HD)),
                jax.ShapeDtypeStruct((rows, width), jnp.bfloat16),
                [IN_VMEM] * (3 + len(blocks)),
                IN_VMEM,
                "attention",
                flops=2_000_000_000,
            )(queries, products, values, *blocks)

        with jax.named_scope("attended_swap"):
            attended_parts = [attended] + [
                shift(attended, "sub", subs, i) for i in range(1, subs)
            ]

        term = jax.ShapeDtypeStruct((rows, columns), jnp.float32)
        sent = jax.ShapeDtypeStruct((rows, columns), jnp.bfloat16)
        product_flops = 2 * rows * width * columns
        with jax.named_scope("projection"):
            arrived = []
            for step in range(1, heads):
                weight, block_of = weight_and_block(0, step)
                own = call(
                    functools.partial(own_term_kernel, block_of),
                    term,
                    [IN_VMEM] * 2,
                    IN_VMEM,
                    "own_term",
                    product_flops,
                )(attended, weight)
                pairs = [
                    x
                    for i in range(1, subs)
                    for x in (attended_parts[i], weight_and_block(i, step)[0])
                ]
                total = call(
                    functools.partial(sent_term_kernel, block_of),
                    sent,
                    [IN_VMEM] * (1 + len(pairs)),
                    IN_VMEM,
                    "sent_term",
                    product_flops,
                )(own, *pairs)
                arrived.append(shift(total, "head", heads, step))
            gate_row = gate.reshape(1, columns)
            pairs = [
                x for i in range(subs) for x in (attended_parts[i], weight_and_block(i, 0)[0])
            ]
            base = call(
                functools.partial(base_kernel, weight_and_block(0, 0)[1]),
                term,
                [IN_VMEM] * (2 + len(pairs)),
                IN_VMEM,
                "base",
                2 * product_flops,
            )(hidden_in, gate_row, *pairs)
            return call(
                final_kernel,
                sent,
                [IN_VMEM] * (2 + len(arrived)),
                IN_VMEM,
                "final",
                moved=rows * columns * 8,
            )(base, gate_row, *arrived)

    in_specs = (
        P(("groups", "patch"), ("head", "sub")),
        P("groups", ("head", "sub")),
        P("groups", ("head", "sub")),
        P(("groups", "patch"), ("head", "sub")),
        P(("groups", "patch"), ("head", "sub")),
        P(("head", "sub"), None),
        P(("groups", "patch"), ("head", "sub")),
        P(("groups", "head", "sub")),
    )
    out_specs = P(("groups", "patch"), ("head", "sub"))
    return jax.shard_map(
        per_device, mesh=mesh, in_specs=in_specs, out_specs=out_specs, check_vma=False
    )
```

```python
import functools
import math

import jax
import jax.numpy as jnp
from jax import lax
from jax.experimental import pallas as pl
from jax.experimental.pallas import tpu as pltpu
from jax.sharding import PartitionSpec as P

HD = 128
LANES = 128
VMEM_LIMIT = 12 * 1024 * 1024

IN_VMEM = pl.BlockSpec(memory_space=pltpu.VMEM)
ANYWHERE = pl.BlockSpec(memory_space=pl.ANY)


def call(
    kernel,
    out_shape,
    in_specs,
    out_specs,
    name,
    flops=0,
    moved=0,
    scratch_shapes=(),
    vmem=VMEM_LIMIT,
):
    return pl.pallas_call(
        kernel,
        out_shape=out_shape,
        in_specs=in_specs,
        out_specs=out_specs,
        scratch_shapes=scratch_shapes,
        name=name,
        cost_estimate=pl.CostEstimate(flops=flops, bytes_accessed=moved, transcendentals=0),
        compiler_params=pltpu.CompilerParams(vmem_limit_bytes=vmem),
    )


def shift(array, axis, size, step):
    return lax.ppermute(array, axis, [(i, (i + step) % size) for i in range(size)])


LINE_OF_FOUR = (
    [(2, 1), (1, 3)],
    [(1, 0), (0, 2), (3, 1)],
    [(2, 0), (3, 2), (0, 3)],
    [(0, 1), (1, 2), (2, 3), (3, 0)],
)


def gather_permutes(patches):
    if patches == 4:
        return LINE_OF_FOUR
    return [
        [(i, (i + step) % patches) for i in range(patches)] for step in range(1, patches)
    ]


def gather_slots(patches):
    slots = []
    for place in range(patches):
        found = []
        for n, pairs in enumerate(gather_permutes(patches)):
            found += [(n, source) for source, target in pairs if target == place]
        slots.append(found)
    return slots


def by_place(place, entries):
    if all(entry is entries[0] for entry in entries):
        return entries[0]
    value = entries[0]
    for i, entry in enumerate(entries[1:], 1):
        if entry is not value:
            value = jnp.where(place == i, entry, value)
    return value


def gather_sources(patches, place):
    if patches != 4:
        return [lax.rem(place + patches - step, patches) for step in range(patches)]
    slots = gather_slots(patches)
    return [place] + [
        by_place(place, [jnp.int32(found[i][1]) for found in slots]) for i in range(patches - 1)
    ]


def gathered_blocks(patches, refs):
    if patches != 4:
        return [ref[...] for ref in refs]
    place = lax.axis_index("patch")
    own, arrived = refs[0][...], [ref[...] for ref in refs[1:]]
    slots = gather_slots(patches)
    return [own] + [
        by_place(place, [arrived[found[i][0]] for found in slots]) for i in range(patches - 1)
    ]


def stage_kernel(patches, q_ref, held_k_ref, held_v_ref, products_ref, values_ref):
    rows, width = q_ref.shape
    sources = gather_sources(patches, lax.axis_index("patch"))
    starts = [pl.multiple_of(source * rows, rows) for source in sources]
    for i, at in enumerate(starts):
        values_ref[i * rows : (i + 1) * rows, :] = held_v_ref[pl.ds(at, rows), :]
    for head in range(width // HD):
        cols = slice(head * HD, (head + 1) * HD)
        keys = jnp.concatenate([held_k_ref[pl.ds(at, rows), cols] for at in starts], axis=0)
        products_ref[head] = dot_transposed(q_ref[:, cols], keys)


def dot_transposed(a, b):
    return lax.dot_general(
        a, b, (((1,), (1,)), ((), ())), preferred_element_type=jnp.float32
    )


def attention_kernel(scale, patches, q_ref, products_ref, values_ref, *refs):
    block_refs, out_ref = refs[:-1], refs[-1]
    rows, width = q_ref.shape
    blocks = jnp.concatenate(gathered_blocks(patches, block_refs), axis=0)
    for head in range(width // HD):
        cols = slice(head * HD, (head + 1) * HD)
        value_cols = slice(width + head * HD, width + (head + 1) * HD)
        products = products_ref[head] + dot_transposed(q_ref[:, cols], blocks[:, cols])
        scores = products * scale
        weights = jnp.exp(scores - jnp.max(scores, axis=1, keepdims=True))
        totals = jnp.sum(weights, axis=1, keepdims=True)
        high = weights.astype(jnp.bfloat16)
        low = (weights - high.astype(jnp.float32)).astype(jnp.bfloat16)
        sums = jnp.dot(
            jnp.concatenate([high, low], axis=0),
            jnp.concatenate([values_ref[:, cols], blocks[:, value_cols]], axis=1),
            preferred_element_type=jnp.float32,
        )
        sums = sums[:rows] + sums[rows:]
        sums = sums[:, :HD] + sums[:, HD:]
        out_ref[:, cols] = (sums / totals).astype(jnp.bfloat16)


def block_dot(a_ref, weight_ref, block, columns):
    if block is None:
        weight = weight_ref[...]
    else:
        weight = weight_ref[:, pl.ds(pl.multiple_of(block * columns, LANES), columns)]
    return jnp.dot(a_ref[...], weight, preferred_element_type=jnp.float32)


def block_at(step, heads, subs):
    return lax.rem(lax.axis_index("head") + step, heads) * subs + lax.axis_index("sub")


def own_term_kernel(block_of, attended_ref, weight_ref, out_ref):
    out_ref[...] = block_dot(attended_ref, weight_ref, block_of(), out_ref.shape[1])


def sent_term_kernel(block_of, total_ref, *refs):
    out_ref = refs[-1]
    block, columns = block_of(), out_ref.shape[1]
    total = total_ref[...]
    for attended_ref, weight_ref in zip(refs[:-1:2], refs[1:-1:2]):
        total = total + block_dot(attended_ref, weight_ref, block, columns)
    out_ref[...] = total.astype(jnp.bfloat16)


def base_kernel(block_of, hidden_ref, gate_ref, *refs):
    out_ref = refs[-1]
    block, columns = block_of(), out_ref.shape[1]
    total = 0.0
    for attended_ref, weight_ref in zip(refs[:-1:2], refs[1:-1:2]):
        total = total + block_dot(attended_ref, weight_ref, block, columns)
    out_ref[...] = hidden_ref[...].astype(jnp.float32) + gate_ref[...] * total


def final_kernel(base_ref, gate_ref, *refs):
    arrived_refs, out_ref = refs[:-1], refs[-1]
    total = 0.0
    for ref in arrived_refs:
        total = total + ref[...].astype(jnp.float32)
    out_ref[...] = (base_ref[...] + gate_ref[...] * total).astype(jnp.bfloat16)


def solution(mesh):
    patches, heads, subs = mesh.shape["patch"], mesh.shape["head"], mesh.shape["sub"]

    def per_device(
        queries, held_keys, held_values, key_change, value_change, out_weight, hidden_in, gate
    ):
        rows, width = queries.shape
        columns = hidden_in.shape[1]

        with jax.named_scope("residual_gather"):
            low = jnp.float32(-jnp.inf)
            residual = jnp.maximum(
                lax.pad(key_change, low, ((0, 0, 0), (0, width, 0))),
                lax.pad(value_change, low, ((0, 0, 0), (width, 0, 0))),
            ).astype(jnp.bfloat16)
            blocks = [residual] + [
                lax.ppermute(residual, "patch", pairs) for pairs in gather_permutes(patches)
            ]

        with jax.named_scope("weight_swap"):
            weights = [out_weight] + [
                shift(out_weight, "sub", subs, i) for i in range(1, subs)
            ]

        def weight_and_block(i, step):
            if columns % LANES == 0:
                return weights[i], functools.partial(block_at, step, heads, subs)
            at = block_at(step, heads, subs) * columns
            return lax.dynamic_slice(weights[i], (0, at), (width, columns)), lambda: None

        tokens = rows * patches
        with jax.named_scope("attention"):
            products, values = call(
                functools.partial(stage_kernel, patches),
                [
                    jax.ShapeDtypeStruct((width // HD, rows, tokens), jnp.float32),
                    jax.ShapeDtypeStruct((tokens, width), jnp.bfloat16),
                ],
                [IN_VMEM] * 3,
                [IN_VMEM] * 2,
                "stage",
                flops=2_000_000_000,
            )(queries, held_keys, held_values)
            attended = call(
                functools.partial(attention_kernel, 1.0 / math.sqrt(HD), patches),
                jax.ShapeDtypeStruct((rows, width), jnp.bfloat16),
                [IN_VMEM] * (3 + len(blocks)),
                IN_VMEM,
                "attention",
                flops=2_000_000_000,
            )(queries, products, values, *blocks)

        with jax.named_scope("attended_swap"):
            attended_parts = [attended] + [
                shift(attended, "sub", subs, i) for i in range(1, subs)
            ]

        term = jax.ShapeDtypeStruct((rows, columns), jnp.float32)
        sent = jax.ShapeDtypeStruct((rows, columns), jnp.bfloat16)
        product_flops = 2 * rows * width * columns
        with jax.named_scope("projection"):
            arrived = []
            for step in range(1, heads):
                weight, block_of = weight_and_block(0, step)
                own = call(
                    functools.partial(own_term_kernel, block_of),
                    term,
                    [IN_VMEM] * 2,
                    IN_VMEM,
                    "own_term",
                    product_flops,
                )(attended, weight)
                pairs = [
                    x
                    for i in range(1, subs)
                    for x in (attended_parts[i], weight_and_block(i, step)[0])
                ]
                total = call(
                    functools.partial(sent_term_kernel, block_of),
                    sent,
                    [IN_VMEM] * (1 + len(pairs)),
                    IN_VMEM,
                    "sent_term",
                    product_flops,
                )(own, *pairs)
                arrived.append(shift(total, "head", heads, step))
            gate_row = gate.reshape(1, columns)
            pairs = [
                x for i in range(subs) for x in (attended_parts[i], weight_and_block(i, 0)[0])
            ]
            base = call(
                functools.partial(base_kernel, weight_and_block(0, 0)[1]),
                term,
                [IN_VMEM] * (2 + len(pairs)),
                IN_VMEM,
                "base",
                2 * product_flops,
            )(hidden_in, gate_row, *pairs)
            return call(
                final_kernel,
                sent,
                [IN_VMEM] * (2 + len(arrived)),
                IN_VMEM,
                "final",
                moved=rows * columns * 8,
            )(base, gate_row, *arrived)

    in_specs = (
        P(("groups", "patch"), ("head", "sub")),
        P("groups", ("head", "sub")),
        P("groups", ("head", "sub")),
        P(("groups", "patch"), ("head", "sub")),
        P(("groups", "patch"), ("head", "sub")),
        P(("head", "sub"), None),
        P(("groups", "patch"), ("head", "sub")),
        P(("groups", "head", "sub")),
    )
    out_specs = P(("groups", "patch"), ("head", "sub"))
    return jax.shard_map(
        per_device, mesh=mesh, in_specs=in_specs, out_specs=out_specs, check_vma=False
    )
```

```python
import functools
import math

import jax
import jax.numpy as jnp
from jax import lax
from jax.experimental import pallas as pl
from jax.experimental.pallas import tpu as pltpu
from jax.sharding import PartitionSpec as P

HD = 128
LANES = 128
VMEM_LIMIT = 12 * 1024 * 1024

IN_VMEM = pl.BlockSpec(memory_space=pltpu.VMEM)
ANYWHERE = pl.BlockSpec(memory_space=pl.ANY)


def call(
    kernel,
    out_shape,
    in_specs,
    out_specs,
    name,
    flops=0,
    moved=0,
    scratch_shapes=(),
    vmem=VMEM_LIMIT,
):
    return pl.pallas_call(
        kernel,
        out_shape=out_shape,
        in_specs=in_specs,
        out_specs=out_specs,
        scratch_shapes=scratch_shapes,
        name=name,
        cost_estimate=pl.CostEstimate(flops=flops, bytes_accessed=moved, transcendentals=0),
        compiler_params=pltpu.CompilerParams(vmem_limit_bytes=vmem),
    )


def shift(array, axis, size, step):
    return lax.ppermute(array, axis, [(i, (i + step) % size) for i in range(size)])


def gather_steps(patches):
    return list(range(patches - 1, 0, -1))


def gather_sources(patches, place):
    return [place] + [lax.rem(place + patches - step, patches) for step in gather_steps(patches)]


def stage_kernel(patches, q_ref, held_k_ref, held_v_ref, products_ref, values_ref):
    rows, width = q_ref.shape
    sources = gather_sources(patches, lax.axis_index("patch"))
    starts = [pl.multiple_of(source * rows, rows) for source in sources]
    for i, at in enumerate(starts):
        values_ref[i * rows : (i + 1) * rows, :] = held_v_ref[pl.ds(at, rows), :]
    for head in range(width // HD):
        cols = slice(head * HD, (head + 1) * HD)
        keys = jnp.concatenate([held_k_ref[pl.ds(at, rows), cols] for at in starts], axis=0)
        products_ref[head] = dot_transposed(q_ref[:, cols], keys)


def dot_transposed(a, b):
    return lax.dot_general(
        a, b, (((1,), (1,)), ((), ())), preferred_element_type=jnp.float32
    )


def attention_kernel(scale, q_ref, products_ref, values_ref, *refs):
    block_refs, out_ref = refs[:-1], refs[-1]
    rows, width = q_ref.shape
    blocks = jnp.concatenate([ref[...] for ref in block_refs], axis=0)
    for head in range(width // HD):
        cols = slice(head * HD, (head + 1) * HD)
        value_cols = slice(width + head * HD, width + (head + 1) * HD)
        products = products_ref[head] + dot_transposed(q_ref[:, cols], blocks[:, cols])
        scores = products * scale
        weights = jnp.exp(scores - jnp.max(scores, axis=1, keepdims=True))
        totals = jnp.sum(weights, axis=1, keepdims=True)
        high = weights.astype(jnp.bfloat16)
        low = (weights - high.astype(jnp.float32)).astype(jnp.bfloat16)
        sums = jnp.dot(
            jnp.concatenate([high, low], axis=0),
            jnp.concatenate([values_ref[:, cols], blocks[:, value_cols]], axis=1),
            preferred_element_type=jnp.float32,
        )
        sums = sums[:rows] + sums[rows:]
        sums = sums[:, :HD] + sums[:, HD:]
        out_ref[:, cols] = (sums / totals).astype(jnp.bfloat16)


def block_dot(a_ref, weight_ref, block, columns):
    if block is None:
        weight = weight_ref[...]
    else:
        weight = weight_ref[:, pl.ds(pl.multiple_of(block * columns, LANES), columns)]
    return jnp.dot(a_ref[...], weight, preferred_element_type=jnp.float32)


def block_at(step, heads, subs):
    return lax.rem(lax.axis_index("head") + step, heads) * subs + lax.axis_index("sub")


def own_term_kernel(block_of, attended_ref, weight_ref, out_ref):
    out_ref[...] = block_dot(attended_ref, weight_ref, block_of(), out_ref.shape[1])


def sent_term_kernel(block_of, total_ref, *refs):
    out_ref = refs[-1]
    block, columns = block_of(), out_ref.shape[1]
    total = total_ref[...]
    for attended_ref, weight_ref in zip(refs[:-1:2], refs[1:-1:2]):
        total = total + block_dot(attended_ref, weight_ref, block, columns)
    out_ref[...] = total.astype(jnp.bfloat16)


def base_kernel(block_of, hidden_ref, gate_ref, *refs):
    out_ref = refs[-1]
    block, columns = block_of(), out_ref.shape[1]
    total = 0.0
    for attended_ref, weight_ref in zip(refs[:-1:2], refs[1:-1:2]):
        total = total + block_dot(attended_ref, weight_ref, block, columns)
    out_ref[...] = hidden_ref[...].astype(jnp.float32) + gate_ref[...] * total


def final_kernel(base_ref, gate_ref, *refs):
    arrived_refs, out_ref = refs[:-1], refs[-1]
    total = 0.0
    for ref in arrived_refs:
        total = total + ref[...].astype(jnp.float32)
    out_ref[...] = (base_ref[...] + gate_ref[...] * total).astype(jnp.bfloat16)


def solution(mesh):
    patches, heads, subs = mesh.shape["patch"], mesh.shape["head"], mesh.shape["sub"]

    def per_device(
        queries, held_keys, held_values, key_change, value_change, out_weight, hidden_in, gate
    ):
        rows, width = queries.shape
        columns = hidden_in.shape[1]

        with jax.named_scope("residual_gather"):
            low = jnp.float32(-jnp.inf)
            residual = jnp.maximum(
                lax.pad(key_change, low, ((0, 0, 0), (0, width, 0))),
                lax.pad(value_change, low, ((0, 0, 0), (width, 0, 0))),
            ).astype(jnp.bfloat16)
            blocks = [residual] + [
                shift(residual, "patch", patches, step) for step in gather_steps(patches)
            ]

        with jax.named_scope("weight_swap"):
            weights = [out_weight] + [
                shift(out_weight, "sub", subs, i) for i in range(1, subs)
            ]

        def weight_and_block(i, step):
            if columns % LANES == 0:
                return weights[i], functools.partial(block_at, step, heads, subs)
            at = block_at(step, heads, subs) * columns
            return lax.dynamic_slice(weights[i], (0, at), (width, columns)), lambda: None

        tokens = rows * patches
        with jax.named_scope("attention"):
            products, values = call(
                functools.partial(stage_kernel, patches),
                [
                    jax.ShapeDtypeStruct((width // HD, rows, tokens), jnp.float32),
                    jax.ShapeDtypeStruct((tokens, width), jnp.bfloat16),
                ],
                [IN_VMEM] * 3,
                [IN_VMEM] * 2,
                "stage",
                flops=2_000_000_000,
            )(queries, held_keys, held_values)
            attended = call(
                functools.partial(attention_kernel, 1.0 / math.sqrt(HD)),
                jax.ShapeDtypeStruct((rows, width), jnp.bfloat16),
                [IN_VMEM] * (3 + len(blocks)),
                IN_VMEM,
                "attention",
                flops=2_000_000_000,
            )(queries, products, values, *blocks)

        with jax.named_scope("attended_swap"):
            attended_parts = [attended] + [
                shift(attended, "sub", subs, i) for i in range(1, subs)
            ]

        term = jax.ShapeDtypeStruct((rows, columns), jnp.float32)
        sent = jax.ShapeDtypeStruct((rows, columns), jnp.bfloat16)
        product_flops = 2 * rows * width * columns
        with jax.named_scope("projection"):
            arrived = []
            for step in range(1, heads):
                weight, block_of = weight_and_block(0, step)
                own = call(
                    functools.partial(own_term_kernel, block_of),
                    term,
                    [IN_VMEM] * 2,
                    IN_VMEM,
                    "own_term",
                    product_flops,
                )(attended, weight)
                pairs = [
                    x
                    for i in range(1, subs)
                    for x in (attended_parts[i], weight_and_block(i, step)[0])
                ]
                total = call(
                    functools.partial(sent_term_kernel, block_of),
                    sent,
                    [IN_VMEM] * (1 + len(pairs)),
                    IN_VMEM,
                    "sent_term",
                    product_flops,
                )(own, *pairs)
                arrived.append(shift(total, "head", heads, step))
            gate_row = gate.reshape(1, columns)
            pairs = [
                x for i in range(subs) for x in (attended_parts[i], weight_and_block(i, 0)[0])
            ]
            base = call(
                functools.partial(base_kernel, weight_and_block(0, 0)[1]),
                term,
                [IN_VMEM] * (2 + len(pairs)),
                IN_VMEM,
                "base",
                2 * product_flops,
            )(hidden_in, gate_row, *pairs)
            return call(
                final_kernel,
                sent,
                [IN_VMEM] * (2 + len(arrived)),
                IN_VMEM,
                "final",
                moved=rows * columns * 8,
            )(base, gate_row, *arrived)

    in_specs = (
        P(("groups", "patch"), ("head", "sub")),
        P("groups", ("head", "sub")),
        P("groups", ("head", "sub")),
        P(("groups", "patch"), ("head", "sub")),
        P(("groups", "patch"), ("head", "sub")),
        P(("head", "sub"), None),
        P(("groups", "patch"), ("head", "sub")),
        P(("groups", "head", "sub")),
    )
    out_specs = P(("groups", "patch"), ("head", "sub"))
    return jax.shard_map(
        per_device, mesh=mesh, in_specs=in_specs, out_specs=out_specs, check_vma=False
    )
```

```python
import functools
import math

import jax
import jax.numpy as jnp
from jax import lax
from jax.experimental import pallas as pl
from jax.experimental.pallas import tpu as pltpu
from jax.sharding import PartitionSpec as P

HD = 128
LANES = 128
VMEM_LIMIT = 12 * 1024 * 1024

IN_VMEM = pl.BlockSpec(memory_space=pltpu.VMEM)
ANYWHERE = pl.BlockSpec(memory_space=pl.ANY)


def call(
    kernel,
    out_shape,
    in_specs,
    out_specs,
    name,
    flops=0,
    moved=0,
    scratch_shapes=(),
    aliases=None,
):
    return pl.pallas_call(
        kernel,
        out_shape=out_shape,
        in_specs=in_specs,
        out_specs=out_specs,
        scratch_shapes=scratch_shapes,
        input_output_aliases=aliases or {},
        name=name,
        cost_estimate=pl.CostEstimate(flops=flops, bytes_accessed=moved, transcendentals=0),
        compiler_params=pltpu.CompilerParams(vmem_limit_bytes=VMEM_LIMIT),
    )


def shift(array, axis, size, step):
    return lax.ppermute(array, axis, [(i, (i + step) % size) for i in range(size)])


RING_OF_FOUR = ((0, 1), (1, 3), (3, 2), (2, 0))


def gather(own, patches):
    if patches != 4:
        return [own] + [shift(own, "patch", patches, step) for step in range(1, patches)]
    forth = lax.ppermute(own, "patch", RING_OF_FOUR)
    back = lax.ppermute(own, "patch", [(target, source) for source, target in RING_OF_FOUR])
    across = lax.ppermute(forth, "patch", RING_OF_FOUR)
    return [own, across, back, forth]


def gather_sources(patches, place):
    if patches != 4:
        return [lax.rem(place + patches - step, patches) for step in range(patches)]
    before = {target: source for source, target in RING_OF_FOUR}
    after = dict(RING_OF_FOUR)
    return [place] + [
        by_place(place, [table(i) for i in range(4)])
        for table in (lambda i: before[before[i]], lambda i: after[i], lambda i: before[i])
    ]


def by_place(place, entries):
    value = jnp.int32(entries[0])
    for i, entry in enumerate(entries[1:], 1):
        value = jnp.where(place == i, jnp.int32(entry), value)
    return value


def stage_kernel(patches, q_ref, held_k_ref, held_v_ref, products_ref, values_ref):
    rows, width = q_ref.shape
    sources = gather_sources(patches, lax.axis_index("patch"))
    starts = [pl.multiple_of(source * rows, rows) for source in sources]
    for i, at in enumerate(starts):
        values_ref[i * rows : (i + 1) * rows, :] = held_v_ref[pl.ds(at, rows), :]
    for head in range(width // HD):
        cols = slice(head * HD, (head + 1) * HD)
        keys = jnp.concatenate([held_k_ref[pl.ds(at, rows), cols] for at in starts], axis=0)
        products_ref[head] = dot_transposed(q_ref[:, cols], keys)


def dot_transposed(a, b):
    return lax.dot_general(
        a, b, (((1,), (1,)), ((), ())), preferred_element_type=jnp.float32
    )


def attention_kernel(scale, q_ref, products_ref, values_ref, *refs):
    block_refs, out_ref = refs[:-1], refs[-1]
    rows, width = q_ref.shape
    blocks = jnp.concatenate([ref[...] for ref in block_refs], axis=0)
    for head in range(width // HD):
        cols = slice(head * HD, (head + 1) * HD)
        value_cols = slice(width + head * HD, width + (head + 1) * HD)
        products = products_ref[head] + dot_transposed(q_ref[:, cols], blocks[:, cols])
        scores = products * scale
        weights = jnp.exp(scores - jnp.max(scores, axis=1, keepdims=True))
        totals = jnp.sum(weights, axis=1, keepdims=True)
        high = weights.astype(jnp.bfloat16)
        low = (weights - high.astype(jnp.float32)).astype(jnp.bfloat16)
        sums = jnp.dot(
            jnp.concatenate([high, low], axis=0),
            jnp.concatenate([values_ref[:, cols], blocks[:, value_cols]], axis=1),
            preferred_element_type=jnp.float32,
        )
        sums = sums[:rows] + sums[rows:]
        sums = sums[:, :HD] + sums[:, HD:]
        out_ref[:, cols] = (sums / totals).astype(jnp.bfloat16)


def block_dot(a_ref, weight_ref, start, columns):
    if start is None:
        weight = weight_ref[...]
    else:
        weight = weight_ref[:, pl.ds(pl.multiple_of(start(), LANES), columns)]
    return jnp.dot(a_ref[...], weight, preferred_element_type=jnp.float32)


def own_term_kernel(starts, attended_ref, weight_ref, *out_refs):
    for start, out_ref in zip(starts, out_refs):
        out_ref[...] = block_dot(attended_ref, weight_ref, start, out_ref.shape[1])


def sent_term_kernel(start, total_ref, *refs):
    out_ref = refs[-1]
    total = total_ref[...]
    for attended_ref, weight_ref in zip(refs[:-1:2], refs[1:-1:2]):
        total = total + block_dot(attended_ref, weight_ref, start, out_ref.shape[1])
    out_ref[...] = total.astype(jnp.bfloat16)


def base_kernel(start, hidden_ref, gate_ref, *refs):
    out_ref = refs[-1]
    total = 0.0
    for attended_ref, weight_ref in zip(refs[:-1:2], refs[1:-1:2]):
        total = total + block_dot(attended_ref, weight_ref, start, out_ref.shape[1])
    out_ref[...] = hidden_ref[...].astype(jnp.float32) + gate_ref[...] * total


def final_kernel(at, base_ref, gate_ref, *refs):
    out_ref, result, sem = refs[-3:]
    size = result.shape[1]
    total = 0.0
    for ref in refs[:-3]:
        if ref.shape == result.shape:
            total = total + ref[...].astype(jnp.float32)
    cols = slice(at, at + size)
    result[...] = (base_ref[:, cols] + gate_ref[:, cols] * total).astype(jnp.bfloat16)
    copy = pltpu.make_async_copy(result, out_ref.at[:, pl.ds(at, size)], sem)
    copy.start()
    copy.wait()


def solution(mesh):
    patches, heads, subs = mesh.shape["patch"], mesh.shape["head"], mesh.shape["sub"]

    def per_device(
        queries, held_keys, held_values, key_change, value_change, out_weight, hidden_in, gate
    ):
        rows, width = queries.shape
        columns = hidden_in.shape[1]

        with jax.named_scope("residual_gather"):
            low = jnp.float32(-jnp.inf)
            residual = jnp.maximum(
                lax.pad(key_change, low, ((0, 0, 0), (0, width, 0))),
                lax.pad(value_change, low, ((0, 0, 0), (width, 0, 0))),
            ).astype(jnp.bfloat16)
            blocks = gather(residual, patches)

        with jax.named_scope("weight_swap"):
            weights = [out_weight] + [
                shift(out_weight, "sub", subs, i) for i in range(1, subs)
            ]

        chunks = 2 if columns % (2 * LANES) == 0 else 1
        size = columns // chunks

        def block_start(step, chunk):
            to = lax.rem(lax.axis_index("head") + step, heads) * subs + lax.axis_index("sub")
            return to * columns + chunk * size

        def weight_and_start(i, step, chunk=0, length=columns):
            start = functools.partial(block_start, step, chunk)
            if columns % LANES == 0:
                return weights[i], start
            return lax.dynamic_slice(weights[i], (0, start()), (width, length)), None

        tokens = rows * patches
        with jax.named_scope("attention"):
            products, values = call(
                functools.partial(stage_kernel, patches),
                [
                    jax.ShapeDtypeStruct((width // HD, rows, tokens), jnp.float32),
                    jax.ShapeDtypeStruct((tokens, width), jnp.bfloat16),
                ],
                [IN_VMEM] * 3,
                [IN_VMEM] * 2,
                "stage",
                flops=2_000_000_000,
            )(queries, held_keys, held_values)
            attended = call(
                functools.partial(attention_kernel, 1.0 / math.sqrt(HD)),
                jax.ShapeDtypeStruct((rows, width), jnp.bfloat16),
                [IN_VMEM] * (3 + len(blocks)),
                IN_VMEM,
                "attention",
                flops=2_000_000_000,
            )(queries, products, values, *blocks)

        with jax.named_scope("attended_swap"):
            attended_parts = [attended] + [
                shift(attended, "sub", subs, i) for i in range(1, subs)
            ]

        term = jax.ShapeDtypeStruct((rows, columns), jnp.float32)
        part = jax.ShapeDtypeStruct((rows, size), jnp.float32)
        sent = jax.ShapeDtypeStruct((rows, size), jnp.bfloat16)
        product_flops = 2 * rows * width * columns
        with jax.named_scope("projection"):
            arrived = [[] for _ in range(chunks)]
            for step in range(1, heads):
                own_weight = weight_and_start(0, step, 0, size)[0]
                own_terms = call(
                    functools.partial(
                        own_term_kernel,
                        [weight_and_start(0, step, n, size)[1] for n in range(chunks)],
                    ),
                    [part] * chunks,
                    [IN_VMEM] * 2,
                    [IN_VMEM] * chunks,
                    "own_term",
                    product_flops,
                )(attended, own_weight)
                for n in range(chunks):
                    pairs = [
                        x
                        for i in range(1, subs)
                        for x in (attended_parts[i], weight_and_start(i, step, n, size)[0])
                    ]
                    total = call(
                        functools.partial(
                            sent_term_kernel, weight_and_start(0, step, n, size)[1]
                        ),
                        sent,
                        [IN_VMEM] * (1 + len(pairs)),
                        IN_VMEM,
                        "sent_term",
                        product_flops // chunks,
                    )(own_terms[n], *pairs)
                    arrived[n].append(shift(total, "head", heads, step))
            gate_row = gate.reshape(1, columns)
            pairs = [
                x for i in range(subs) for x in (attended_parts[i], weight_and_start(i, 0)[0])
            ]
            base = call(
                functools.partial(base_kernel, weight_and_start(0, 0)[1]),
                term,
                [IN_VMEM] * (2 + len(pairs)),
                IN_VMEM,
                "base",
                2 * product_flops,
            )(hidden_in, gate_row, *pairs)
            out = None
            for n in range(chunks):
                before = [] if out is None else [out]
                inputs = [base, gate_row, *arrived[n], *before]
                out = call(
                    functools.partial(final_kernel, n * size),
                    jax.ShapeDtypeStruct((rows, columns), jnp.bfloat16),
                    [IN_VMEM] * (2 + len(arrived[n])) + [ANYWHERE] * len(before),
                    ANYWHERE,
                    "final",
                    moved=rows * size * 8,
                    scratch_shapes=[
                        pltpu.VMEM((rows, size), jnp.bfloat16),
                        pltpu.SemaphoreType.DMA,
                    ],
                    aliases={len(inputs) - 1: 0} if before else {},
                )(*inputs)
            return out

    in_specs = (
        P(("groups", "patch"), ("head", "sub")),
        P("groups", ("head", "sub")),
        P("groups", ("head", "sub")),
        P(("groups", "patch"), ("head", "sub")),
        P(("groups", "patch"), ("head", "sub")),
        P(("head", "sub"), None),
        P(("groups", "patch"), ("head", "sub")),
        P(("groups", "head", "sub")),
    )
    out_specs = P(("groups", "patch"), ("head", "sub"))
    return jax.shard_map(
        per_device, mesh=mesh, in_specs=in_specs, out_specs=out_specs, check_vma=False
    )
```

```python
import functools
import math

import jax
import jax.numpy as jnp
from jax import lax
from jax.experimental import pallas as pl
from jax.experimental.pallas import tpu as pltpu
from jax.sharding import PartitionSpec as P

HD = 128
LANES = 128
VMEM_LIMIT = 12 * 1024 * 1024

IN_VMEM = pl.BlockSpec(memory_space=pltpu.VMEM)
ANYWHERE = pl.BlockSpec(memory_space=pl.ANY)


def call(
    kernel,
    out_shape,
    in_specs,
    out_specs,
    name,
    flops=0,
    moved=0,
    scratch_shapes=(),
    vmem=VMEM_LIMIT,
):
    return pl.pallas_call(
        kernel,
        out_shape=out_shape,
        in_specs=in_specs,
        out_specs=out_specs,
        scratch_shapes=scratch_shapes,
        name=name,
        cost_estimate=pl.CostEstimate(flops=flops, bytes_accessed=moved, transcendentals=0),
        compiler_params=pltpu.CompilerParams(vmem_limit_bytes=vmem),
    )


def shift(array, axis, size, step):
    return lax.ppermute(array, axis, [(i, (i + step) % size) for i in range(size)])


def gather_steps(patches):
    return list(range(patches - 1, 0, -1))


def gather_sources(patches, place):
    return [place] + [lax.rem(place + patches - step, patches) for step in gather_steps(patches)]


def stage_kernel(patches, q_ref, held_k_ref, held_v_ref, products_ref, values_ref):
    rows, width = q_ref.shape
    sources = gather_sources(patches, lax.axis_index("patch"))
    starts = [pl.multiple_of(source * rows, rows) for source in sources]
    for i, at in enumerate(starts):
        values_ref[i * rows : (i + 1) * rows, :] = held_v_ref[pl.ds(at, rows), :]
    for head in range(width // HD):
        cols = slice(head * HD, (head + 1) * HD)
        keys = jnp.concatenate([held_k_ref[pl.ds(at, rows), cols] for at in starts], axis=0)
        products_ref[head] = dot_transposed(q_ref[:, cols], keys)


def dot_transposed(a, b):
    return lax.dot_general(
        a, b, (((1,), (1,)), ((), ())), preferred_element_type=jnp.float32
    )


def attention_kernel(scale, q_ref, products_ref, values_ref, *refs):
    block_refs, out_ref = refs[:-1], refs[-1]
    rows, width = q_ref.shape
    blocks = jnp.concatenate([ref[...] for ref in block_refs], axis=0)
    for head in range(width // HD):
        cols = slice(head * HD, (head + 1) * HD)
        value_cols = slice(width + head * HD, width + (head + 1) * HD)
        products = products_ref[head] + dot_transposed(q_ref[:, cols], blocks[:, cols])
        scores = products * scale
        weights = jnp.exp(scores - jnp.max(scores, axis=1, keepdims=True))
        totals = jnp.sum(weights, axis=1, keepdims=True)
        high = weights.astype(jnp.bfloat16)
        low = (weights - high.astype(jnp.float32)).astype(jnp.bfloat16)
        sums = jnp.dot(
            jnp.concatenate([high, low], axis=0),
            jnp.concatenate([values_ref[:, cols], blocks[:, value_cols]], axis=1),
            preferred_element_type=jnp.float32,
        )
        sums = sums[:rows] + sums[rows:]
        sums = sums[:, :HD] + sums[:, HD:]
        out_ref[:, cols] = (sums / totals).astype(jnp.bfloat16)


def block_dot(a_ref, weight_ref, start, columns):
    if start is None:
        weight = weight_ref[...]
    else:
        weight = weight_ref[:, pl.ds(pl.multiple_of(start, LANES), columns)]
    return jnp.dot(a_ref[...], weight, preferred_element_type=jnp.float32)


def products(start, columns, refs):
    total = 0.0
    for attended_ref, weight_ref in zip(refs[::2], refs[1::2]):
        total = total + block_dot(attended_ref, weight_ref, start, columns)
    return total


def sent_term_kernel(start, *refs):
    out_ref = refs[-1]
    total = products(start(), out_ref.shape[1], refs[:-1])
    out_ref[...] = total.astype(jnp.bfloat16)


def base_kernel(start, hidden_ref, gate_ref, *refs):
    out_ref = refs[-1]
    total = products(start(), out_ref.shape[1], refs[:-1])
    out_ref[...] = hidden_ref[...].astype(jnp.float32) + gate_ref[...] * total


def final_kernel(early, base_ref, gate_ref, *refs):
    arrived_refs, out_ref = refs[:-1], refs[-1]
    total = 0.0
    for ref in arrived_refs:
        total = total + ref[...].astype(jnp.float32)
    if early:
        out_ref[:, :early] = base_ref[:, :early].astype(jnp.bfloat16)
    out_ref[:, early:] = (base_ref[:, early:] + gate_ref[:, early:] * total).astype(jnp.bfloat16)


def early_weight_kernel(subs, columns, early, weight_ref, after_ref, out_ref, sems):
    chip = (1 - lax.axis_index("head")) * subs
    copies = []
    for sub in range(subs):
        at = pl.multiple_of((chip + sub) * columns, LANES)
        copies.append(
            pltpu.make_async_copy(
                weight_ref.at[:, pl.ds(at, early)],
                out_ref.at[:, pl.ds(sub * early, early)],
                sems.at[sub],
            )
        )
    for copy in copies:
        copy.start()
    for copy in copies:
        copy.wait()


def pack_kernel(early, attended_ref, weight_ref, out_ref):
    rows = attended_ref.shape[0]
    other = pl.multiple_of((1 - lax.axis_index("sub")) * early, LANES)
    out_ref[:rows, :] = attended_ref[...]
    out_ref[rows:, :] = weight_ref[:, pl.ds(other, early)]


def early_kernel(early, base_ref, gate_ref, attended_ref, weight_ref, packed_ref, out_ref):
    rows = attended_ref.shape[0]
    mine = pl.multiple_of(lax.axis_index("sub") * early, LANES)
    total = jnp.dot(
        attended_ref[...],
        weight_ref[:, pl.ds(mine, early)],
        preferred_element_type=jnp.float32,
    ) + jnp.dot(
        packed_ref[:rows, :], packed_ref[rows:, :], preferred_element_type=jnp.float32
    )
    out_ref[...] = base_ref[...]
    out_ref[:, :early] = base_ref[:, :early] + gate_ref[:, :early] * total


def solution(mesh):
    patches, heads, subs = mesh.shape["patch"], mesh.shape["head"], mesh.shape["sub"]

    def per_device(
        queries, held_keys, held_values, key_change, value_change, out_weight, hidden_in, gate
    ):
        rows, width = queries.shape
        columns = hidden_in.shape[1]

        with jax.named_scope("residual_gather"):
            low = jnp.float32(-jnp.inf)
            residual = jnp.maximum(
                lax.pad(key_change, low, ((0, 0, 0), (0, width, 0))),
                lax.pad(value_change, low, ((0, 0, 0), (width, 0, 0))),
            ).astype(jnp.bfloat16)
            blocks = [residual] + [
                shift(residual, "patch", patches, step) for step in gather_steps(patches)
            ]

        with jax.named_scope("weight_swap"):
            weights = [out_weight] + [
                shift(out_weight, "sub", subs, i) for i in range(1, subs)
            ]

        early = 2 * LANES if heads == 2 and columns % LANES == 0 and columns > 4 * LANES else 0
        if early:
            with jax.named_scope("early_weight"):
                early_weight = call(
                    functools.partial(early_weight_kernel, subs, columns, early),
                    jax.ShapeDtypeStruct((width, subs * early), jnp.bfloat16),
                    [ANYWHERE] * 2,
                    ANYWHERE,
                    "early_weight",
                    moved=4 * width * subs * early,
                    scratch_shapes=[pltpu.SemaphoreType.DMA((subs,))],
                    vmem=60 * 1024 * 1024,
                )(out_weight, residual)
                early_weight = shift(early_weight, "head", heads, 1)

        def weight_and_start(i, step, skip=0):
            def start():
                to = lax.rem(lax.axis_index("head") + step, heads) * subs + lax.axis_index("sub")
                return to * columns + skip

            if columns % LANES == 0:
                return weights[i], start
            return lax.dynamic_slice(weights[i], (0, start()), (width, columns)), lambda: None

        def pairs_and_start(step, skip=0):
            pairs = [
                x
                for i in range(subs)
                for x in (attended_parts[i], weight_and_start(i, step, skip)[0])
            ]
            return pairs, weight_and_start(0, step, skip)[1]

        tokens = rows * patches
        with jax.named_scope("attention"):
            products, values = call(
                functools.partial(stage_kernel, patches),
                [
                    jax.ShapeDtypeStruct((width // HD, rows, tokens), jnp.float32),
                    jax.ShapeDtypeStruct((tokens, width), jnp.bfloat16),
                ],
                [IN_VMEM] * 3,
                [IN_VMEM] * 2,
                "stage",
                flops=2_000_000_000,
            )(queries, held_keys, held_values)
            attended = call(
                functools.partial(attention_kernel, 1.0 / math.sqrt(HD)),
                jax.ShapeDtypeStruct((rows, width), jnp.bfloat16),
                [IN_VMEM] * (3 + len(blocks)),
                IN_VMEM,
                "attention",
                flops=2_000_000_000,
            )(queries, products, values, *blocks)

        with jax.named_scope("attended_swap"):
            attended_parts = [attended] + [
                shift(attended, "sub", subs, i) for i in range(1, subs)
            ]
            if early:
                other_attended = shift(attended, "head", heads, 1)

        term = jax.ShapeDtypeStruct((rows, columns), jnp.float32)
        sent = jax.ShapeDtypeStruct((rows, columns - early), jnp.bfloat16)
        product_flops = 2 * rows * width * columns
        with jax.named_scope("projection"):
            arrived = []
            for step in range(1, heads):
                pairs, start = pairs_and_start(step, early)
                total = call(
                    functools.partial(sent_term_kernel, start),
                    sent,
                    [IN_VMEM] * len(pairs),
                    IN_VMEM,
                    "sent_term",
                    2 * product_flops,
                )(*pairs)
                arrived.append(shift(total, "head", heads, step))
            gate_row = gate.reshape(1, columns)
            pairs, start = pairs_and_start(0)
            base = call(
                functools.partial(base_kernel, start),
                term,
                [IN_VMEM] * (2 + len(pairs)),
                IN_VMEM,
                "base",
                2 * product_flops,
            )(hidden_in, gate_row, *pairs)
            if early:
                packed = call(
                    functools.partial(pack_kernel, early),
                    jax.ShapeDtypeStruct((rows + width, early), jnp.bfloat16),
                    [IN_VMEM] * 2,
                    IN_VMEM,
                    "pack",
                )(other_attended, early_weight)
                packed = shift(packed, "sub", subs, 1)
                base = call(
                    functools.partial(early_kernel, early),
                    term,
                    [IN_VMEM] * 5,
                    IN_VMEM,
                    "early",
                    product_flops // 2,
                )(base, gate_row, other_attended, early_weight, packed)
            return call(
                functools.partial(final_kernel, early),
                jax.ShapeDtypeStruct((rows, columns), jnp.bfloat16),
                [IN_VMEM] * (2 + len(arrived)),
                IN_VMEM,
                "final",
                moved=rows * columns * 8,
            )(base, gate_row, *arrived)

    in_specs = (
        P(("groups", "patch"), ("head", "sub")),
        P("groups", ("head", "sub")),
        P("groups", ("head", "sub")),
        P(("groups", "patch"), ("head", "sub")),
        P(("groups", "patch"), ("head", "sub")),
        P(("head", "sub"), None),
        P(("groups", "patch"), ("head", "sub")),
        P(("groups", "head", "sub")),
    )
    out_specs = P(("groups", "patch"), ("head", "sub"))
    return jax.shard_map(
        per_device, mesh=mesh, in_specs=in_specs, out_specs=out_specs, check_vma=False
    )
```

```python
import functools
import math

import jax
import jax.numpy as jnp
from jax import lax
from jax.experimental import pallas as pl
from jax.experimental.pallas import tpu as pltpu
from jax.sharding import PartitionSpec as P

HD = 128
LANES = 128
VMEM_LIMIT = 12 * 1024 * 1024

IN_VMEM = pl.BlockSpec(memory_space=pltpu.VMEM)
ANYWHERE = pl.BlockSpec(memory_space=pl.ANY)


def call(
    kernel,
    out_shape,
    in_specs,
    out_specs,
    name,
    flops=0,
    moved=0,
    scratch_shapes=(),
    vmem=VMEM_LIMIT,
):
    return pl.pallas_call(
        kernel,
        out_shape=out_shape,
        in_specs=in_specs,
        out_specs=out_specs,
        scratch_shapes=scratch_shapes,
        name=name,
        cost_estimate=pl.CostEstimate(flops=flops, bytes_accessed=moved, transcendentals=0),
        compiler_params=pltpu.CompilerParams(vmem_limit_bytes=vmem),
    )


def shift(array, axis, size, step):
    return lax.ppermute(array, axis, [(i, (i + step) % size) for i in range(size)])


def gather_steps(patches):
    return list(range(patches - 1, 0, -1))


def gather_sources(patches, place):
    return [place] + [lax.rem(place + patches - step, patches) for step in gather_steps(patches)]


def stage_kernel(patches, q_ref, held_k_ref, held_v_ref, products_ref, values_ref):
    rows, width = q_ref.shape
    sources = gather_sources(patches, lax.axis_index("patch"))
    starts = [pl.multiple_of(source * rows, rows) for source in sources]
    for i, at in enumerate(starts):
        values_ref[i * rows : (i + 1) * rows, :] = held_v_ref[pl.ds(at, rows), :]
    for head in range(width // HD):
        cols = slice(head * HD, (head + 1) * HD)
        keys = jnp.concatenate([held_k_ref[pl.ds(at, rows), cols] for at in starts], axis=0)
        products_ref[head] = dot_transposed(q_ref[:, cols], keys)


def dot_transposed(a, b):
    return lax.dot_general(
        a, b, (((1,), (1,)), ((), ())), preferred_element_type=jnp.float32
    )


def attention_kernel(scale, q_ref, products_ref, values_ref, *refs):
    block_refs, out_ref = refs[:-1], refs[-1]
    rows, width = q_ref.shape
    blocks = jnp.concatenate([ref[...] for ref in block_refs], axis=0)
    for head in range(width // HD):
        cols = slice(head * HD, (head + 1) * HD)
        value_cols = slice(width + head * HD, width + (head + 1) * HD)
        products = products_ref[head] + dot_transposed(q_ref[:, cols], blocks[:, cols])
        scores = products * scale
        weights = jnp.exp(scores - jnp.max(scores, axis=1, keepdims=True))
        totals = jnp.sum(weights, axis=1, keepdims=True)
        high = weights.astype(jnp.bfloat16)
        low = (weights - high.astype(jnp.float32)).astype(jnp.bfloat16)
        sums = jnp.dot(
            jnp.concatenate([high, low], axis=0),
            jnp.concatenate([values_ref[:, cols], blocks[:, value_cols]], axis=1),
            preferred_element_type=jnp.float32,
        )
        sums = sums[:rows] + sums[rows:]
        sums = sums[:, :HD] + sums[:, HD:]
        out_ref[:, cols] = (sums / totals).astype(jnp.bfloat16)


def block_dot(a_ref, weight_ref, start, columns):
    if start is None:
        weight = weight_ref[...]
    else:
        weight = weight_ref[:, pl.ds(pl.multiple_of(start, LANES), columns)]
    return jnp.dot(a_ref[...], weight, preferred_element_type=jnp.float32)


def products(start, columns, refs):
    total = 0.0
    for attended_ref, weight_ref in zip(refs[::2], refs[1::2]):
        total = total + block_dot(attended_ref, weight_ref, start, columns)
    return total


def sent_term_kernel(start, *refs):
    out_ref = refs[-1]
    total = products(start(), out_ref.shape[1], refs[:-1])
    out_ref[...] = total.astype(jnp.bfloat16)


def base_kernel(start, hidden_ref, gate_ref, *refs):
    out_ref = refs[-1]
    total = products(start(), out_ref.shape[1], refs[:-1])
    out_ref[...] = hidden_ref[...].astype(jnp.float32) + gate_ref[...] * total


def final_kernel(early, base_ref, gate_ref, *refs):
    arrived_refs, out_ref = refs[:-1], refs[-1]
    total = 0.0
    for ref in arrived_refs:
        total = total + ref[...].astype(jnp.float32)
    if early:
        out_ref[:, :early] = base_ref[:, :early].astype(jnp.bfloat16)
    out_ref[:, early:] = (base_ref[:, early:] + gate_ref[:, early:] * total).astype(jnp.bfloat16)


def early_weight_kernel(subs, columns, early, weight_ref, after_ref, out_ref, sems):
    chip = (1 - lax.axis_index("head")) * subs
    copies = []
    for sub in range(subs):
        at = pl.multiple_of((chip + sub) * columns, LANES)
        copies.append(
            pltpu.make_async_copy(
                weight_ref.at[:, pl.ds(at, early)],
                out_ref.at[:, pl.ds(sub * early, early)],
                sems.at[sub],
            )
        )
    for copy in copies:
        copy.start()
    for copy in copies:
        copy.wait()


def pack_kernel(early, attended_ref, weight_ref, out_ref):
    rows, width = attended_ref.shape
    for i in range(width // early):
        out_ref[i * rows : (i + 1) * rows, :] = attended_ref[:, i * early : (i + 1) * early]
    other = pl.multiple_of((1 - lax.axis_index("sub")) * early, LANES)
    out_ref[rows * (width // early) :, :] = weight_ref[:, pl.ds(other, early)]


def early_kernel(early, base_ref, gate_ref, attended_ref, weight_ref, packed_ref, out_ref):
    rows, width = attended_ref.shape
    pieces = width // early
    mine = pl.multiple_of(lax.axis_index("sub") * early, LANES)
    total = jnp.dot(
        attended_ref[...],
        weight_ref[:, pl.ds(mine, early)],
        preferred_element_type=jnp.float32,
    ) + jnp.dot(
        jnp.concatenate(
            [packed_ref[i * rows : (i + 1) * rows, :] for i in range(pieces)], axis=1
        ),
        packed_ref[pieces * rows :, :],
        preferred_element_type=jnp.float32,
    )
    out_ref[...] = base_ref[...]
    out_ref[:, :early] = base_ref[:, :early] + gate_ref[:, :early] * total


def solution(mesh):
    patches, heads, subs = mesh.shape["patch"], mesh.shape["head"], mesh.shape["sub"]

    def per_device(
        queries, held_keys, held_values, key_change, value_change, out_weight, hidden_in, gate
    ):
        rows, width = queries.shape
        columns = hidden_in.shape[1]

        with jax.named_scope("residual_gather"):
            low = jnp.float32(-jnp.inf)
            residual = jnp.maximum(
                lax.pad(key_change, low, ((0, 0, 0), (0, width, 0))),
                lax.pad(value_change, low, ((0, 0, 0), (width, 0, 0))),
            ).astype(jnp.bfloat16)
            blocks = [residual] + [
                shift(residual, "patch", patches, step) for step in gather_steps(patches)
            ]

        with jax.named_scope("weight_swap"):
            weights = [out_weight] + [
                shift(out_weight, "sub", subs, i) for i in range(1, subs)
            ]

        early = LANES if heads == 2 and columns % LANES == 0 and columns > 4 * LANES else 0
        if early:
            with jax.named_scope("early_weight"):
                early_weight = call(
                    functools.partial(early_weight_kernel, subs, columns, early),
                    jax.ShapeDtypeStruct((width, subs * early), jnp.bfloat16),
                    [ANYWHERE] * 2,
                    IN_VMEM,
                    "early_weight",
                    moved=4 * width * subs * early,
                    scratch_shapes=[pltpu.SemaphoreType.DMA((subs,))],
                    vmem=60 * 1024 * 1024,
                )(out_weight, residual)
                early_weight = shift(early_weight, "head", heads, 1)

        def weight_and_start(i, step, skip=0):
            def start():
                to = lax.rem(lax.axis_index("head") + step, heads) * subs + lax.axis_index("sub")
                return to * columns + skip

            if columns % LANES == 0:
                return weights[i], start
            return lax.dynamic_slice(weights[i], (0, start()), (width, columns)), lambda: None

        def pairs_and_start(step, skip=0):
            pairs = [
                x
                for i in range(subs)
                for x in (attended_parts[i], weight_and_start(i, step, skip)[0])
            ]
            return pairs, weight_and_start(0, step, skip)[1]

        tokens = rows * patches
        with jax.named_scope("attention"):
            products, values = call(
                functools.partial(stage_kernel, patches),
                [
                    jax.ShapeDtypeStruct((width // HD, rows, tokens), jnp.float32),
                    jax.ShapeDtypeStruct((tokens, width), jnp.bfloat16),
                ],
                [IN_VMEM] * 3,
                [IN_VMEM] * 2,
                "stage",
                flops=2_000_000_000,
            )(queries, held_keys, held_values)
            attended = call(
                functools.partial(attention_kernel, 1.0 / math.sqrt(HD)),
                jax.ShapeDtypeStruct((rows, width), jnp.bfloat16),
                [IN_VMEM] * (3 + len(blocks)),
                IN_VMEM,
                "attention",
                flops=2_000_000_000,
            )(queries, products, values, *blocks)

        with jax.named_scope("attended_swap"):
            attended_parts = [attended] + [
                shift(attended, "sub", subs, i) for i in range(1, subs)
            ]
            if early:
                other_attended = shift(attended, "head", heads, 1)

        term = jax.ShapeDtypeStruct((rows, columns), jnp.float32)
        sent = jax.ShapeDtypeStruct((rows, columns - early), jnp.bfloat16)
        product_flops = 2 * rows * width * columns
        with jax.named_scope("projection"):
            arrived = []
            for step in range(1, heads):
                pairs, start = pairs_and_start(step, early)
                total = call(
                    functools.partial(sent_term_kernel, start),
                    sent,
                    [IN_VMEM] * len(pairs),
                    IN_VMEM,
                    "sent_term",
                    2 * product_flops,
                )(*pairs)
                arrived.append(shift(total, "head", heads, step))
            gate_row = gate.reshape(1, columns)
            pairs, start = pairs_and_start(0)
            base = call(
                functools.partial(base_kernel, start),
                term,
                [IN_VMEM] * (2 + len(pairs)),
                IN_VMEM,
                "base",
                2 * product_flops,
            )(hidden_in, gate_row, *pairs)
            if early:
                packed = call(
                    functools.partial(pack_kernel, early),
                    jax.ShapeDtypeStruct((rows * (width // early) + width, early), jnp.bfloat16),
                    [IN_VMEM] * 2,
                    IN_VMEM,
                    "pack",
                )(other_attended, early_weight)
                packed = shift(packed, "sub", subs, 1)
                base = call(
                    functools.partial(early_kernel, early),
                    term,
                    [IN_VMEM] * 5,
                    IN_VMEM,
                    "early",
                    product_flops // 2,
                )(base, gate_row, other_attended, early_weight, packed)
            return call(
                functools.partial(final_kernel, early),
                jax.ShapeDtypeStruct((rows, columns), jnp.bfloat16),
                [IN_VMEM] * (2 + len(arrived)),
                IN_VMEM,
                "final",
                moved=rows * columns * 8,
            )(base, gate_row, *arrived)

    in_specs = (
        P(("groups", "patch"), ("head", "sub")),
        P("groups", ("head", "sub")),
        P("groups", ("head", "sub")),
        P(("groups", "patch"), ("head", "sub")),
        P(("groups", "patch"), ("head", "sub")),
        P(("head", "sub"), None),
        P(("groups", "patch"), ("head", "sub")),
        P(("groups", "head", "sub")),
    )
    out_specs = P(("groups", "patch"), ("head", "sub"))
    return jax.shard_map(
        per_device, mesh=mesh, in_specs=in_specs, out_specs=out_specs, check_vma=False
    )
```

```python
import functools
import math

import jax
import jax.numpy as jnp
from jax import lax
from jax.experimental import pallas as pl
from jax.experimental.pallas import tpu as pltpu
from jax.sharding import PartitionSpec as P

HD = 128
LANES = 128
VMEM_LIMIT = 12 * 1024 * 1024
EARLY = 256

IN_VMEM = pl.BlockSpec(memory_space=pltpu.VMEM)
ANYWHERE = pl.BlockSpec(memory_space=pl.ANY)


def call(
    kernel,
    out_shape,
    in_specs,
    out_specs,
    name,
    flops=0,
    moved=0,
    scratch_shapes=(),
    vmem=VMEM_LIMIT,
):
    return pl.pallas_call(
        kernel,
        out_shape=out_shape,
        in_specs=in_specs,
        out_specs=out_specs,
        scratch_shapes=scratch_shapes,
        name=name,
        cost_estimate=pl.CostEstimate(flops=flops, bytes_accessed=moved, transcendentals=0),
        compiler_params=pltpu.CompilerParams(vmem_limit_bytes=vmem),
    )


def shift(array, axis, size, step):
    return lax.ppermute(array, axis, [(i, (i + step) % size) for i in range(size)])


def gather_steps(patches):
    return list(range(patches - 1, 0, -1))


def gather_sources(patches, place):
    return [place] + [lax.rem(place + patches - step, patches) for step in gather_steps(patches)]


def stage_kernel(patches, q_ref, held_k_ref, held_v_ref, products_ref, values_ref):
    rows, width = q_ref.shape
    sources = gather_sources(patches, lax.axis_index("patch"))
    starts = [pl.multiple_of(source * rows, rows) for source in sources]
    for i, at in enumerate(starts):
        values_ref[i * rows : (i + 1) * rows, :] = held_v_ref[pl.ds(at, rows), :]
    for head in range(width // HD):
        cols = slice(head * HD, (head + 1) * HD)
        keys = jnp.concatenate([held_k_ref[pl.ds(at, rows), cols] for at in starts], axis=0)
        products_ref[head] = dot_transposed(q_ref[:, cols], keys)


def dot_transposed(a, b):
    return lax.dot_general(
        a, b, (((1,), (1,)), ((), ())), preferred_element_type=jnp.float32
    )


def attention_kernel(scale, q_ref, products_ref, values_ref, *refs):
    block_refs, out_ref = refs[:-1], refs[-1]
    rows, width = q_ref.shape
    blocks = jnp.concatenate([ref[...] for ref in block_refs], axis=0)
    for head in range(width // HD):
        cols = slice(head * HD, (head + 1) * HD)
        value_cols = slice(width + head * HD, width + (head + 1) * HD)
        products = products_ref[head] + dot_transposed(q_ref[:, cols], blocks[:, cols])
        scores = products * scale
        weights = jnp.exp(scores - jnp.max(scores, axis=1, keepdims=True))
        totals = jnp.sum(weights, axis=1, keepdims=True)
        high = weights.astype(jnp.bfloat16)
        low = (weights - high.astype(jnp.float32)).astype(jnp.bfloat16)
        sums = jnp.dot(
            jnp.concatenate([high, low], axis=0),
            jnp.concatenate([values_ref[:, cols], blocks[:, value_cols]], axis=1),
            preferred_element_type=jnp.float32,
        )
        sums = sums[:rows] + sums[rows:]
        sums = sums[:, :HD] + sums[:, HD:]
        out_ref[:, cols] = (sums / totals).astype(jnp.bfloat16)


def block_dot(a_ref, weight_ref, start, columns):
    if start is None:
        weight = weight_ref[...]
    else:
        weight = weight_ref[:, pl.ds(pl.multiple_of(start, LANES), columns)]
    return jnp.dot(a_ref[...], weight, preferred_element_type=jnp.float32)


def products(start, columns, refs):
    total = 0.0
    for attended_ref, weight_ref in zip(refs[::2], refs[1::2]):
        total = total + block_dot(attended_ref, weight_ref, start, columns)
    return total


def sent_term_kernel(start, *refs):
    out_ref = refs[-1]
    total = products(start(), out_ref.shape[1], refs[:-1])
    out_ref[...] = total.astype(jnp.bfloat16)


def base_kernel(start, hidden_ref, gate_ref, *refs):
    out_ref = refs[-1]
    total = products(start(), out_ref.shape[1], refs[:-1])
    out_ref[...] = hidden_ref[...].astype(jnp.float32) + gate_ref[...] * total


def final_kernel(early, base_ref, gate_ref, *refs):
    arrived_refs, out_ref = refs[:-1], refs[-1]
    total = 0.0
    for ref in arrived_refs:
        total = total + ref[...].astype(jnp.float32)
    if early:
        out_ref[:, :early] = base_ref[:, :early].astype(jnp.bfloat16)
    out_ref[:, early:] = (base_ref[:, early:] + gate_ref[:, early:] * total).astype(jnp.bfloat16)


def pack_kernel(early, attended_ref, weight_ref, out_ref):
    rows, width = attended_ref.shape
    for i in range(width // early):
        out_ref[i * rows : (i + 1) * rows, :] = attended_ref[:, i * early : (i + 1) * early]
    other = pl.multiple_of((1 - lax.axis_index("sub")) * early, LANES)
    out_ref[rows * (width // early) :, :] = weight_ref[:, pl.ds(other, early)]


def early_kernel(early, base_ref, gate_ref, attended_ref, weight_ref, packed_ref, out_ref):
    rows, width = attended_ref.shape
    pieces = width // early
    mine = pl.multiple_of(lax.axis_index("sub") * early, LANES)
    total = jnp.dot(
        attended_ref[...],
        weight_ref[:, pl.ds(mine, early)],
        preferred_element_type=jnp.float32,
    ) + jnp.dot(
        jnp.concatenate(
            [packed_ref[i * rows : (i + 1) * rows, :] for i in range(pieces)], axis=1
        ),
        packed_ref[pieces * rows :, :],
        preferred_element_type=jnp.float32,
    )
    out_ref[...] = base_ref[...]
    out_ref[:, :early] = base_ref[:, :early] + gate_ref[:, :early] * total


def solution(mesh):
    patches, heads, subs = mesh.shape["patch"], mesh.shape["head"], mesh.shape["sub"]

    def per_device(
        queries, held_keys, held_values, key_change, value_change, out_weight, hidden_in, gate
    ):
        rows, width = queries.shape
        columns = hidden_in.shape[1]

        with jax.named_scope("residual_gather"):
            low = jnp.float32(-jnp.inf)
            residual = jnp.maximum(
                lax.pad(key_change, low, ((0, 0, 0), (0, width, 0))),
                lax.pad(value_change, low, ((0, 0, 0), (width, 0, 0))),
            ).astype(jnp.bfloat16)
            blocks = [residual] + [
                shift(residual, "patch", patches, step) for step in gather_steps(patches)
            ]

        with jax.named_scope("weight_swap"):
            weights = [out_weight] + [
                shift(out_weight, "sub", subs, i) for i in range(1, subs)
            ]

        early = EARLY if heads == 2 and columns % LANES == 0 and columns > 4 * LANES else 0
        if early:
            with jax.named_scope("early_weight"):
                chip = (1 - lax.axis_index("head")) * subs
                slices = [
                    lax.dynamic_slice(out_weight, (0, (chip + i) * columns), (width, early))
                    for i in range(subs)
                ]
                low = jnp.bfloat16(-jnp.inf)
                early_weight = functools.reduce(
                    jnp.maximum,
                    [
                        lax.pad(piece, low, ((0, 0, 0), (i * early, (subs - 1 - i) * early, 0)))
                        for i, piece in enumerate(slices)
                    ],
                )
                early_weight = shift(early_weight, "head", heads, 1)

        def weight_and_start(i, step, skip=0):
            def start():
                to = lax.rem(lax.axis_index("head") + step, heads) * subs + lax.axis_index("sub")
                return to * columns + skip

            if columns % LANES == 0:
                return weights[i], start
            return lax.dynamic_slice(weights[i], (0, start()), (width, columns)), lambda: None

        def pairs_and_start(step, skip=0):
            pairs = [
                x
                for i in range(subs)
                for x in (attended_parts[i], weight_and_start(i, step, skip)[0])
            ]
            return pairs, weight_and_start(0, step, skip)[1]

        tokens = rows * patches
        with jax.named_scope("attention"):
            products, values = call(
                functools.partial(stage_kernel, patches),
                [
                    jax.ShapeDtypeStruct((width // HD, rows, tokens), jnp.float32),
                    jax.ShapeDtypeStruct((tokens, width), jnp.bfloat16),
                ],
                [IN_VMEM] * 3,
                [IN_VMEM] * 2,
                "stage",
                flops=2_000_000_000,
            )(queries, held_keys, held_values)
            attended = call(
                functools.partial(attention_kernel, 1.0 / math.sqrt(HD)),
                jax.ShapeDtypeStruct((rows, width), jnp.bfloat16),
                [IN_VMEM] * (3 + len(blocks)),
                IN_VMEM,
                "attention",
                flops=2_000_000_000,
            )(queries, products, values, *blocks)

        with jax.named_scope("attended_swap"):
            attended_parts = [attended] + [
                shift(attended, "sub", subs, i) for i in range(1, subs)
            ]
            if early:
                other_attended = shift(attended, "head", heads, 1)

        term = jax.ShapeDtypeStruct((rows, columns), jnp.float32)
        sent = jax.ShapeDtypeStruct((rows, columns - early), jnp.bfloat16)
        product_flops = 2 * rows * width * columns
        with jax.named_scope("projection"):
            arrived = []
            for step in range(1, heads):
                pairs, start = pairs_and_start(step, early)
                total = call(
                    functools.partial(sent_term_kernel, start),
                    sent,
                    [IN_VMEM] * len(pairs),
                    IN_VMEM,
                    "sent_term",
                    2 * product_flops,
                )(*pairs)
                arrived.append(shift(total, "head", heads, step))
            gate_row = gate.reshape(1, columns)
            pairs, start = pairs_and_start(0)
            base = call(
                functools.partial(base_kernel, start),
                term,
                [IN_VMEM] * (2 + len(pairs)),
                IN_VMEM,
                "base",
                2 * product_flops,
            )(hidden_in, gate_row, *pairs)
            if early:
                packed = call(
                    functools.partial(pack_kernel, early),
                    jax.ShapeDtypeStruct((rows * (width // early) + width, early), jnp.bfloat16),
                    [IN_VMEM] * 2,
                    IN_VMEM,
                    "pack",
                )(other_attended, early_weight)
                packed = shift(packed, "sub", subs, 1)
                base = call(
                    functools.partial(early_kernel, early),
                    term,
                    [IN_VMEM] * 5,
                    IN_VMEM,
                    "early",
                    product_flops // 2,
                )(base, gate_row, other_attended, early_weight, packed)
            return call(
                functools.partial(final_kernel, early),
                jax.ShapeDtypeStruct((rows, columns), jnp.bfloat16),
                [IN_VMEM] * (2 + len(arrived)),
                IN_VMEM,
                "final",
                moved=rows * columns * 8,
            )(base, gate_row, *arrived)

    in_specs = (
        P(("groups", "patch"), ("head", "sub")),
        P("groups", ("head", "sub")),
        P("groups", ("head", "sub")),
        P(("groups", "patch"), ("head", "sub")),
        P(("groups", "patch"), ("head", "sub")),
        P(("head", "sub"), None),
        P(("groups", "patch"), ("head", "sub")),
        P(("groups", "head", "sub")),
    )
    out_specs = P(("groups", "patch"), ("head", "sub"))
    return jax.shard_map(
        per_device, mesh=mesh, in_specs=in_specs, out_specs=out_specs, check_vma=False
    )
```

```python
import functools
import math

import jax
import jax.numpy as jnp
from jax import lax
from jax.experimental import pallas as pl
from jax.experimental.pallas import tpu as pltpu
from jax.sharding import PartitionSpec as P

HD = 128
LANES = 128
VMEM_LIMIT = 12 * 1024 * 1024
EARLY = 256

IN_VMEM = pl.BlockSpec(memory_space=pltpu.VMEM)
ANYWHERE = pl.BlockSpec(memory_space=pl.ANY)


def call(
    kernel,
    out_shape,
    in_specs,
    out_specs,
    name,
    flops=0,
    moved=0,
    scratch_shapes=(),
    vmem=VMEM_LIMIT,
):
    return pl.pallas_call(
        kernel,
        out_shape=out_shape,
        in_specs=in_specs,
        out_specs=out_specs,
        scratch_shapes=scratch_shapes,
        name=name,
        cost_estimate=pl.CostEstimate(flops=flops, bytes_accessed=moved, transcendentals=0),
        compiler_params=pltpu.CompilerParams(vmem_limit_bytes=vmem),
    )


def shift(array, axis, size, step):
    return lax.ppermute(array, axis, [(i, (i + step) % size) for i in range(size)])


def gather_steps(patches):
    return list(range(1, patches))


def gather_sources(patches, place):
    return [place] + [lax.rem(place + patches - step, patches) for step in gather_steps(patches)]


def stage_kernel(patches, q_ref, held_k_ref, held_v_ref, products_ref, values_ref):
    rows, width = q_ref.shape
    sources = gather_sources(patches, lax.axis_index("patch"))
    starts = [pl.multiple_of(source * rows, rows) for source in sources]
    for i, at in enumerate(starts):
        values_ref[i * rows : (i + 1) * rows, :] = held_v_ref[pl.ds(at, rows), :]
    for head in range(width // HD):
        cols = slice(head * HD, (head + 1) * HD)
        keys = jnp.concatenate([held_k_ref[pl.ds(at, rows), cols] for at in starts], axis=0)
        products_ref[head] = dot_transposed(q_ref[:, cols], keys)


def dot_transposed(a, b):
    return lax.dot_general(
        a, b, (((1,), (1,)), ((), ())), preferred_element_type=jnp.float32
    )


def attention_kernel(scale, q_ref, products_ref, values_ref, *refs):
    block_refs, out_ref = refs[:-1], refs[-1]
    rows, width = q_ref.shape
    blocks = jnp.concatenate([ref[...] for ref in block_refs], axis=0)
    for head in range(width // HD):
        cols = slice(head * HD, (head + 1) * HD)
        value_cols = slice(width + head * HD, width + (head + 1) * HD)
        products = products_ref[head] + dot_transposed(q_ref[:, cols], blocks[:, cols])
        scores = products * scale
        weights = jnp.exp(scores - jnp.max(scores, axis=1, keepdims=True))
        totals = jnp.sum(weights, axis=1, keepdims=True)
        high = weights.astype(jnp.bfloat16)
        low = (weights - high.astype(jnp.float32)).astype(jnp.bfloat16)
        sums = jnp.dot(
            jnp.concatenate([high, low], axis=0),
            jnp.concatenate([values_ref[:, cols], blocks[:, value_cols]], axis=1),
            preferred_element_type=jnp.float32,
        )
        sums = sums[:rows] + sums[rows:]
        sums = sums[:, :HD] + sums[:, HD:]
        out_ref[:, cols] = (sums / totals).astype(jnp.bfloat16)


def block_dot(a_ref, weight_ref, start, columns):
    if start is None:
        weight = weight_ref[...]
    else:
        weight = weight_ref[:, pl.ds(pl.multiple_of(start, LANES), columns)]
    return jnp.dot(a_ref[...], weight, preferred_element_type=jnp.float32)


def products(start, columns, refs):
    total = 0.0
    for attended_ref, weight_ref in zip(refs[::2], refs[1::2]):
        total = total + block_dot(attended_ref, weight_ref, start, columns)
    return total


def sent_term_kernel(start, *refs):
    out_ref = refs[-1]
    total = products(start(), out_ref.shape[1], refs[:-1])
    out_ref[...] = total.astype(jnp.bfloat16)


def base_kernel(start, hidden_ref, gate_ref, *refs):
    out_ref = refs[-1]
    total = products(start(), out_ref.shape[1], refs[:-1])
    out_ref[...] = hidden_ref[...].astype(jnp.float32) + gate_ref[...] * total


def final_kernel(early, base_ref, gate_ref, *refs):
    arrived_refs, out_ref = refs[:-1], refs[-1]
    total = 0.0
    for ref in arrived_refs:
        total = total + ref[...].astype(jnp.float32)
    if early:
        out_ref[:, :early] = base_ref[:, :early].astype(jnp.bfloat16)
    out_ref[:, early:] = (base_ref[:, early:] + gate_ref[:, early:] * total).astype(jnp.bfloat16)


def pack_kernel(early, attended_ref, weight_ref, out_ref):
    rows, width = attended_ref.shape
    for i in range(width // early):
        out_ref[i * rows : (i + 1) * rows, :] = attended_ref[:, i * early : (i + 1) * early]
    other = pl.multiple_of((1 - lax.axis_index("sub")) * early, LANES)
    out_ref[rows * (width // early) :, :] = weight_ref[:, pl.ds(other, early)]


def early_kernel(early, base_ref, gate_ref, attended_ref, weight_ref, packed_ref, out_ref):
    rows, width = attended_ref.shape
    pieces = width // early
    mine = pl.multiple_of(lax.axis_index("sub") * early, LANES)
    total = jnp.dot(
        attended_ref[...],
        weight_ref[:, pl.ds(mine, early)],
        preferred_element_type=jnp.float32,
    ) + jnp.dot(
        jnp.concatenate(
            [packed_ref[i * rows : (i + 1) * rows, :] for i in range(pieces)], axis=1
        ),
        packed_ref[pieces * rows :, :],
        preferred_element_type=jnp.float32,
    )
    out_ref[...] = base_ref[...]
    out_ref[:, :early] = base_ref[:, :early] + gate_ref[:, :early] * total


def solution(mesh):
    patches, heads, subs = mesh.shape["patch"], mesh.shape["head"], mesh.shape["sub"]

    def per_device(
        queries, held_keys, held_values, key_change, value_change, out_weight, hidden_in, gate
    ):
        rows, width = queries.shape
        columns = hidden_in.shape[1]

        with jax.named_scope("residual_gather"):
            low = jnp.float32(-jnp.inf)
            residual = jnp.maximum(
                lax.pad(key_change, low, ((0, 0, 0), (0, width, 0))),
                lax.pad(value_change, low, ((0, 0, 0), (width, 0, 0))),
            ).astype(jnp.bfloat16)

        early = EARLY if heads == 2 and columns % LANES == 0 and columns > 4 * LANES else 0
        if early:
            with jax.named_scope("early_weight"):
                chip = (1 - lax.axis_index("head")) * subs
                slices = [
                    lax.dynamic_slice(out_weight, (0, (chip + i) * columns), (width, early))
                    for i in range(subs)
                ]
                low = jnp.bfloat16(-jnp.inf)
                early_weight = functools.reduce(
                    jnp.maximum,
                    [
                        lax.pad(piece, low, ((0, 0, 0), (i * early, (subs - 1 - i) * early, 0)))
                        for i, piece in enumerate(slices)
                    ],
                )

        with jax.named_scope("residual_gather"):
            last = residual
            if early:
                last, early_weight = lax.optimization_barrier((residual, early_weight))
            blocks = [residual] + [
                shift(last if step == patches - 1 else residual, "patch", patches, step)
                for step in gather_steps(patches)
            ]

        with jax.named_scope("weight_swap"):
            weights = [out_weight] + [
                shift(out_weight, "sub", subs, i) for i in range(1, subs)
            ]

        if early:
            with jax.named_scope("early_weight"):
                early_weight = shift(early_weight, "head", heads, 1)

        def weight_and_start(i, step, skip=0):
            def start():
                to = lax.rem(lax.axis_index("head") + step, heads) * subs + lax.axis_index("sub")
                return to * columns + skip

            if columns % LANES == 0:
                return weights[i], start
            return lax.dynamic_slice(weights[i], (0, start()), (width, columns)), lambda: None

        def pairs_and_start(step, skip=0):
            pairs = [
                x
                for i in range(subs)
                for x in (attended_parts[i], weight_and_start(i, step, skip)[0])
            ]
            return pairs, weight_and_start(0, step, skip)[1]

        tokens = rows * patches
        with jax.named_scope("attention"):
            products, values = call(
                functools.partial(stage_kernel, patches),
                [
                    jax.ShapeDtypeStruct((width // HD, rows, tokens), jnp.float32),
                    jax.ShapeDtypeStruct((tokens, width), jnp.bfloat16),
                ],
                [IN_VMEM] * 3,
                [IN_VMEM] * 2,
                "stage",
                flops=2_000_000_000,
            )(queries, held_keys, held_values)
            attended = call(
                functools.partial(attention_kernel, 1.0 / math.sqrt(HD)),
                jax.ShapeDtypeStruct((rows, width), jnp.bfloat16),
                [IN_VMEM] * (3 + len(blocks)),
                IN_VMEM,
                "attention",
                flops=2_000_000_000,
            )(queries, products, values, *blocks)

        with jax.named_scope("attended_swap"):
            attended_parts = [attended] + [
                shift(attended, "sub", subs, i) for i in range(1, subs)
            ]
            if early:
                other_attended = shift(attended, "head", heads, 1)

        term = jax.ShapeDtypeStruct((rows, columns), jnp.float32)
        sent = jax.ShapeDtypeStruct((rows, columns - early), jnp.bfloat16)
        product_flops = 2 * rows * width * columns
        with jax.named_scope("projection"):
            arrived = []
            for step in range(1, heads):
                pairs, start = pairs_and_start(step, early)
                total = call(
                    functools.partial(sent_term_kernel, start),
                    sent,
                    [IN_VMEM] * len(pairs),
                    IN_VMEM,
                    "sent_term",
                    2 * product_flops,
                )(*pairs)
                arrived.append(shift(total, "head", heads, step))
            gate_row = gate.reshape(1, columns)
            pairs, start = pairs_and_start(0)
            base = call(
                functools.partial(base_kernel, start),
                term,
                [IN_VMEM] * (2 + len(pairs)),
                IN_VMEM,
                "base",
                2 * product_flops,
            )(hidden_in, gate_row, *pairs)
            if early:
                packed = call(
                    functools.partial(pack_kernel, early),
                    jax.ShapeDtypeStruct((rows * (width // early) + width, early), jnp.bfloat16),
                    [IN_VMEM] * 2,
                    IN_VMEM,
                    "pack",
                )(other_attended, early_weight)
                packed = shift(packed, "sub", subs, 1)
                base = call(
                    functools.partial(early_kernel, early),
                    term,
                    [IN_VMEM] * 5,
                    IN_VMEM,
                    "early",
                    product_flops // 2,
                )(base, gate_row, other_attended, early_weight, packed)
            return call(
                functools.partial(final_kernel, early),
                jax.ShapeDtypeStruct((rows, columns), jnp.bfloat16),
                [IN_VMEM] * (2 + len(arrived)),
                IN_VMEM,
                "final",
                moved=rows * columns * 8,
            )(base, gate_row, *arrived)

    in_specs = (
        P(("groups", "patch"), ("head", "sub")),
        P("groups", ("head", "sub")),
        P("groups", ("head", "sub")),
        P(("groups", "patch"), ("head", "sub")),
        P(("groups", "patch"), ("head", "sub")),
        P(("head", "sub"), None),
        P(("groups", "patch"), ("head", "sub")),
        P(("groups", "head", "sub")),
    )
    out_specs = P(("groups", "patch"), ("head", "sub"))
    return jax.shard_map(
        per_device, mesh=mesh, in_specs=in_specs, out_specs=out_specs, check_vma=False
    )
```

```python
import functools
import math

import jax
import jax.numpy as jnp
from jax import lax
from jax.experimental import pallas as pl
from jax.experimental.pallas import tpu as pltpu
from jax.sharding import PartitionSpec as P

HD = 128
LANES = 128
VMEM_LIMIT = 12 * 1024 * 1024
EARLY = 256

IN_VMEM = pl.BlockSpec(memory_space=pltpu.VMEM)
ANYWHERE = pl.BlockSpec(memory_space=pl.ANY)


def call(
    kernel,
    out_shape,
    in_specs,
    out_specs,
    name,
    flops=0,
    moved=0,
    scratch_shapes=(),
    vmem=VMEM_LIMIT,
):
    return pl.pallas_call(
        kernel,
        out_shape=out_shape,
        in_specs=in_specs,
        out_specs=out_specs,
        scratch_shapes=scratch_shapes,
        name=name,
        cost_estimate=pl.CostEstimate(flops=flops, bytes_accessed=moved, transcendentals=0),
        compiler_params=pltpu.CompilerParams(vmem_limit_bytes=vmem),
    )


def shift(array, axis, size, step):
    return lax.ppermute(array, axis, [(i, (i + step) % size) for i in range(size)])


def gather_steps(patches):
    return list(range(patches - 1, 0, -1))


def gather_sources(patches, place):
    return [place] + [lax.rem(place + patches - step, patches) for step in gather_steps(patches)]


def prepare_kernel(subs, columns, early, *refs):
    changes, weights = refs[:2], refs[2:3] if early else ()
    residual_ref, early_refs = refs[2 + len(weights)], refs[3 + len(weights) : -3]
    buffers, sems = refs[-3:-1], refs[-1]
    width = buffers[0].shape[1]
    copies = [
        pltpu.make_async_copy(change, buffer, sems.at[i])
        for i, (change, buffer) in enumerate(zip(changes, buffers))
    ]
    if early:
        chip = (1 - lax.axis_index("head")) * subs
        for sub in range(subs):
            at = pl.multiple_of((chip + sub) * columns, LANES)
            copies.append(
                pltpu.make_async_copy(
                    weights[0].at[:, pl.ds(at, early)],
                    early_refs[0].at[:, pl.ds(sub * early, early)],
                    sems.at[2 + sub],
                )
            )
    for copy in copies:
        copy.start()
    for i, buffer in enumerate(buffers):
        copies[i].wait()
        residual_ref[:, i * width : (i + 1) * width] = buffer[...].astype(jnp.bfloat16)
    for copy in copies[2:]:
        copy.wait()


def stage_kernel(patches, q_ref, held_k_ref, held_v_ref, products_ref, values_ref):
    rows, width = q_ref.shape
    sources = gather_sources(patches, lax.axis_index("patch"))
    starts = [pl.multiple_of(source * rows, rows) for source in sources]
    for i, at in enumerate(starts):
        values_ref[i * rows : (i + 1) * rows, :] = held_v_ref[pl.ds(at, rows), :]
    for head in range(width // HD):
        cols = slice(head * HD, (head + 1) * HD)
        keys = jnp.concatenate([held_k_ref[pl.ds(at, rows), cols] for at in starts], axis=0)
        products_ref[head] = dot_transposed(q_ref[:, cols], keys)


def dot_transposed(a, b):
    return lax.dot_general(
        a, b, (((1,), (1,)), ((), ())), preferred_element_type=jnp.float32
    )


def attention_kernel(scale, q_ref, products_ref, values_ref, *refs):
    block_refs, out_ref = refs[:-1], refs[-1]
    rows, width = q_ref.shape
    blocks = jnp.concatenate([ref[...] for ref in block_refs], axis=0)
    for head in range(width // HD):
        cols = slice(head * HD, (head + 1) * HD)
        value_cols = slice(width + head * HD, width + (head + 1) * HD)
        products = products_ref[head] + dot_transposed(q_ref[:, cols], blocks[:, cols])
        scores = products * scale
        weights = jnp.exp(scores - jnp.max(scores, axis=1, keepdims=True))
        totals = jnp.sum(weights, axis=1, keepdims=True)
        high = weights.astype(jnp.bfloat16)
        low = (weights - high.astype(jnp.float32)).astype(jnp.bfloat16)
        sums = jnp.dot(
            jnp.concatenate([high, low], axis=0),
            jnp.concatenate([values_ref[:, cols], blocks[:, value_cols]], axis=1),
            preferred_element_type=jnp.float32,
        )
        sums = sums[:rows] + sums[rows:]
        sums = sums[:, :HD] + sums[:, HD:]
        out_ref[:, cols] = (sums / totals).astype(jnp.bfloat16)


def block_dot(a_ref, weight_ref, start, columns):
    if start is None:
        weight = weight_ref[...]
    else:
        weight = weight_ref[:, pl.ds(pl.multiple_of(start, LANES), columns)]
    return jnp.dot(a_ref[...], weight, preferred_element_type=jnp.float32)


def products(start, columns, refs):
    total = 0.0
    for attended_ref, weight_ref in zip(refs[::2], refs[1::2]):
        total = total + block_dot(attended_ref, weight_ref, start, columns)
    return total


def sent_term_kernel(start, *refs):
    out_ref = refs[-1]
    total = products(start(), out_ref.shape[1], refs[:-1])
    out_ref[...] = total.astype(jnp.bfloat16)


def base_kernel(start, hidden_ref, gate_ref, *refs):
    out_ref = refs[-1]
    total = products(start(), out_ref.shape[1], refs[:-1])
    out_ref[...] = hidden_ref[...].astype(jnp.float32) + gate_ref[...] * total


def final_kernel(early, base_ref, gate_ref, *refs):
    arrived_refs, out_ref = refs[:-1], refs[-1]
    total = 0.0
    for ref in arrived_refs:
        total = total + ref[...].astype(jnp.float32)
    if early:
        out_ref[:, :early] = base_ref[:, :early].astype(jnp.bfloat16)
    out_ref[:, early:] = (base_ref[:, early:] + gate_ref[:, early:] * total).astype(jnp.bfloat16)


def pack_kernel(early, attended_ref, weight_ref, out_ref):
    rows, width = attended_ref.shape
    for i in range(width // early):
        out_ref[i * rows : (i + 1) * rows, :] = attended_ref[:, i * early : (i + 1) * early]
    other = pl.multiple_of((1 - lax.axis_index("sub")) * early, LANES)
    out_ref[rows * (width // early) :, :] = weight_ref[:, pl.ds(other, early)]


def early_kernel(early, base_ref, gate_ref, attended_ref, weight_ref, packed_ref, out_ref):
    rows, width = attended_ref.shape
    pieces = width // early
    mine = pl.multiple_of(lax.axis_index("sub") * early, LANES)
    total = jnp.dot(
        attended_ref[...],
        weight_ref[:, pl.ds(mine, early)],
        preferred_element_type=jnp.float32,
    ) + jnp.dot(
        jnp.concatenate(
            [packed_ref[i * rows : (i + 1) * rows, :] for i in range(pieces)], axis=1
        ),
        packed_ref[pieces * rows :, :],
        preferred_element_type=jnp.float32,
    )
    out_ref[...] = base_ref[...]
    out_ref[:, :early] = base_ref[:, :early] + gate_ref[:, :early] * total


def solution(mesh):
    patches, heads, subs = mesh.shape["patch"], mesh.shape["head"], mesh.shape["sub"]

    def per_device(
        queries, held_keys, held_values, key_change, value_change, out_weight, hidden_in, gate
    ):
        rows, width = queries.shape
        columns = hidden_in.shape[1]

        early = EARLY if heads == 2 and columns % LANES == 0 and columns > 4 * LANES else 0
        with jax.named_scope("residual_gather"):
            operands = [key_change, value_change] + ([out_weight] if early else [])
            shapes = [jax.ShapeDtypeStruct((rows, 2 * width), jnp.bfloat16)]
            if early:
                shapes.append(jax.ShapeDtypeStruct((width, subs * early), jnp.bfloat16))
            residual, *early_weights = call(
                functools.partial(prepare_kernel, subs, columns, early),
                shapes,
                [ANYWHERE] * len(operands),
                [IN_VMEM] * len(shapes),
                "prepare",
                scratch_shapes=[
                    pltpu.VMEM((rows, width), jnp.float32),
                    pltpu.VMEM((rows, width), jnp.float32),
                    pltpu.SemaphoreType.DMA((2 + subs,)),
                ],
            )(*[pltpu.with_memory_space_constraint(x, pltpu.HBM) for x in operands])
            blocks = [residual] + [
                shift(residual, "patch", patches, step) for step in gather_steps(patches)
            ]

        with jax.named_scope("weight_swap"):
            weights = [out_weight] + [
                shift(out_weight, "sub", subs, i) for i in range(1, subs)
            ]

        if early:
            with jax.named_scope("early_weight"):
                early_weight = shift(early_weights[0], "head", heads, 1)

        def weight_and_start(i, step, skip=0):
            def start():
                to = lax.rem(lax.axis_index("head") + step, heads) * subs + lax.axis_index("sub")
                return to * columns + skip

            if columns % LANES == 0:
                return weights[i], start
            return lax.dynamic_slice(weights[i], (0, start()), (width, columns)), lambda: None

        def pairs_and_start(step, skip=0):
            pairs = [
                x
                for i in range(subs)
                for x in (attended_parts[i], weight_and_start(i, step, skip)[0])
            ]
            return pairs, weight_and_start(0, step, skip)[1]

        tokens = rows * patches
        with jax.named_scope("attention"):
            products, values = call(
                functools.partial(stage_kernel, patches),
                [
                    jax.ShapeDtypeStruct((width // HD, rows, tokens), jnp.float32),
                    jax.ShapeDtypeStruct((tokens, width), jnp.bfloat16),
                ],
                [IN_VMEM] * 3,
                [IN_VMEM] * 2,
                "stage",
                flops=2_000_000_000,
            )(queries, held_keys, held_values)
            attended = call(
                functools.partial(attention_kernel, 1.0 / math.sqrt(HD)),
                jax.ShapeDtypeStruct((rows, width), jnp.bfloat16),
                [IN_VMEM] * (3 + len(blocks)),
                IN_VMEM,
                "attention",
                flops=2_000_000_000,
            )(queries, products, values, *blocks)

        with jax.named_scope("attended_swap"):
            attended_parts = [attended] + [
                shift(attended, "sub", subs, i) for i in range(1, subs)
            ]
            if early:
                other_attended = shift(attended, "head", heads, 1)

        term = jax.ShapeDtypeStruct((rows, columns), jnp.float32)
        sent = jax.ShapeDtypeStruct((rows, columns - early), jnp.bfloat16)
        product_flops = 2 * rows * width * columns
        with jax.named_scope("projection"):
            arrived = []
            for step in range(1, heads):
                pairs, start = pairs_and_start(step, early)
                total = call(
                    functools.partial(sent_term_kernel, start),
                    sent,
                    [IN_VMEM] * len(pairs),
                    IN_VMEM,
                    "sent_term",
                    2 * product_flops,
                )(*pairs)
                arrived.append(shift(total, "head", heads, step))
            gate_row = gate.reshape(1, columns)
            pairs, start = pairs_and_start(0)
            base = call(
                functools.partial(base_kernel, start),
                term,
                [IN_VMEM] * (2 + len(pairs)),
                IN_VMEM,
                "base",
                2 * product_flops,
            )(hidden_in, gate_row, *pairs)
            if early:
                packed = call(
                    functools.partial(pack_kernel, early),
                    jax.ShapeDtypeStruct((rows * (width // early) + width, early), jnp.bfloat16),
                    [IN_VMEM] * 2,
                    IN_VMEM,
                    "pack",
                )(other_attended, early_weight)
                packed = shift(packed, "sub", subs, 1)
                base = call(
                    functools.partial(early_kernel, early),
                    term,
                    [IN_VMEM] * 5,
                    IN_VMEM,
                    "early",
                    product_flops // 2,
                )(base, gate_row, other_attended, early_weight, packed)
            return call(
                functools.partial(final_kernel, early),
                jax.ShapeDtypeStruct((rows, columns), jnp.bfloat16),
                [IN_VMEM] * (2 + len(arrived)),
                IN_VMEM,
                "final",
                moved=rows * columns * 8,
            )(base, gate_row, *arrived)

    in_specs = (
        P(("groups", "patch"), ("head", "sub")),
        P("groups", ("head", "sub")),
        P("groups", ("head", "sub")),
        P(("groups", "patch"), ("head", "sub")),
        P(("groups", "patch"), ("head", "sub")),
        P(("head", "sub"), None),
        P(("groups", "patch"), ("head", "sub")),
        P(("groups", "head", "sub")),
    )
    out_specs = P(("groups", "patch"), ("head", "sub"))
    return jax.shard_map(
        per_device, mesh=mesh, in_specs=in_specs, out_specs=out_specs, check_vma=False
    )
```

```python
import functools
import math

import jax
import jax.numpy as jnp
from jax import lax
from jax.experimental import pallas as pl
from jax.experimental.pallas import tpu as pltpu
from jax.sharding import PartitionSpec as P

HD = 128
LANES = 128
ROW_TILE = 16
VMEM_LIMIT = 12 * 1024 * 1024
EARLY = 256

IN_VMEM = pl.BlockSpec(memory_space=pltpu.VMEM)
ANYWHERE = pl.BlockSpec(memory_space=pl.ANY)


def call(
    kernel,
    out_shape,
    in_specs,
    out_specs,
    name,
    flops=0,
    moved=0,
    scratch_shapes=(),
    vmem=VMEM_LIMIT,
):
    return pl.pallas_call(
        kernel,
        out_shape=out_shape,
        in_specs=in_specs,
        out_specs=out_specs,
        scratch_shapes=scratch_shapes,
        name=name,
        cost_estimate=pl.CostEstimate(flops=flops, bytes_accessed=moved, transcendentals=0),
        compiler_params=pltpu.CompilerParams(vmem_limit_bytes=vmem),
    )


def in_hbm(array):
    return pltpu.with_memory_space_constraint(array, pltpu.HBM)


def shift(array, axis, size, step):
    return lax.ppermute(array, axis, [(i, (i + step) % size) for i in range(size)])


def gather_steps(patches):
    return list(range(patches - 1, 0, -1))


def gather_sources(patches, place):
    return [place] + [lax.rem(place + patches - step, patches) for step in gather_steps(patches)]


def prepare_kernel(*refs):
    changes, out_ref, buffers, sems = refs[:2], refs[2], refs[3:5], refs[5]
    width = buffers[0].shape[1]
    copies = [
        pltpu.make_async_copy(change, buffer, sems.at[i])
        for i, (change, buffer) in enumerate(zip(changes, buffers))
    ]
    for copy in copies:
        copy.start()
    for i, (copy, buffer) in enumerate(zip(copies, buffers)):
        copy.wait()
        out_ref[:, i * width : (i + 1) * width] = buffer[...].astype(jnp.bfloat16)


def early_weight_kernel(subs, columns, early, weight_ref, out_ref, sems):
    chip = (1 - lax.axis_index("head")) * subs
    copies = []
    for sub in range(subs):
        at = pl.multiple_of((chip + sub) * columns, LANES)
        copies.append(
            pltpu.make_async_copy(
                weight_ref.at[:, pl.ds(at, early)],
                out_ref.at[:, pl.ds(sub * early, early)],
                sems.at[sub],
            )
        )
    for copy in copies:
        copy.start()
    for copy in copies:
        copy.wait()


def stage_kernel(patches, q_ref, held_k_ref, held_v_ref, products_ref, values_ref):
    rows, width = q_ref.shape
    sources = gather_sources(patches, lax.axis_index("patch"))
    starts = [pl.multiple_of(source * rows, rows) for source in sources]
    for i, at in enumerate(starts):
        values_ref[i * rows : (i + 1) * rows, :] = held_v_ref[pl.ds(at, rows), :]
    for head in range(width // HD):
        cols = slice(head * HD, (head + 1) * HD)
        keys = jnp.concatenate([held_k_ref[pl.ds(at, rows), cols] for at in starts], axis=0)
        products_ref[head] = dot_transposed(q_ref[:, cols], keys)


def dot_transposed(a, b):
    return lax.dot_general(
        a, b, (((1,), (1,)), ((), ())), preferred_element_type=jnp.float32
    )


def attention_kernel(scale, q_ref, products_ref, values_ref, *refs):
    block_refs, out_ref = refs[:-1], refs[-1]
    rows, width = q_ref.shape
    blocks = jnp.concatenate([ref[...] for ref in block_refs], axis=0)
    for head in range(width // HD):
        cols = slice(head * HD, (head + 1) * HD)
        value_cols = slice(width + head * HD, width + (head + 1) * HD)
        products = products_ref[head] + dot_transposed(q_ref[:, cols], blocks[:, cols])
        scores = products * scale
        weights = jnp.exp(scores - jnp.max(scores, axis=1, keepdims=True))
        totals = jnp.sum(weights, axis=1, keepdims=True)
        high = weights.astype(jnp.bfloat16)
        low = (weights - high.astype(jnp.float32)).astype(jnp.bfloat16)
        sums = jnp.dot(
            jnp.concatenate([high, low], axis=0),
            jnp.concatenate([values_ref[:, cols], blocks[:, value_cols]], axis=1),
            preferred_element_type=jnp.float32,
        )
        sums = sums[:rows] + sums[rows:]
        sums = sums[:, :HD] + sums[:, HD:]
        out_ref[:, cols] = (sums / totals).astype(jnp.bfloat16)


def block_dot(a_ref, weight_ref, start, columns):
    if start is None:
        weight = weight_ref[...]
    else:
        weight = weight_ref[:, pl.ds(pl.multiple_of(start, LANES), columns)]
    return jnp.dot(a_ref[...], weight, preferred_element_type=jnp.float32)


def products(start, columns, refs):
    total = 0.0
    for attended_ref, weight_ref in zip(refs[::2], refs[1::2]):
        total = total + block_dot(attended_ref, weight_ref, start, columns)
    return total


def sent_term_kernel(start, *refs):
    out_ref = refs[-1]
    total = products(start(), out_ref.shape[1], refs[:-1])
    out_ref[...] = total.astype(jnp.bfloat16)


def base_kernel(start, hidden_ref, gate_ref, *refs):
    out_ref = refs[-1]
    total = products(start(), out_ref.shape[1], refs[:-1])
    out_ref[...] = hidden_ref[...].astype(jnp.float32) + gate_ref[...] * total


def final_kernel(early, blocks, base_ref, gate_ref, *refs):
    arrived_refs, (out_ref, result, sems) = refs[:-3], refs[-3:]
    rows = base_ref.shape[0] // blocks
    copies = []
    for n in range(blocks):
        at = slice(n * rows, (n + 1) * rows)
        total = 0.0
        for ref in arrived_refs:
            total = total + ref[at, :].astype(jnp.float32)
        if early:
            result[at, :early] = base_ref[at, :early].astype(jnp.bfloat16)
        total = base_ref[at, early:] + gate_ref[:, early:] * total
        result[at, early:] = total.astype(jnp.bfloat16)
        copies.append(pltpu.make_async_copy(result.at[at, :], out_ref.at[at, :], sems.at[n]))
        copies[n].start()
    for copy in copies:
        copy.wait()


def pack_kernel(early, attended_ref, weight_ref, out_ref):
    rows, width = attended_ref.shape
    for i in range(width // early):
        out_ref[i * rows : (i + 1) * rows, :] = attended_ref[:, i * early : (i + 1) * early]
    other = pl.multiple_of((1 - lax.axis_index("sub")) * early, LANES)
    out_ref[rows * (width // early) :, :] = weight_ref[:, pl.ds(other, early)]


def early_kernel(early, base_ref, gate_ref, attended_ref, weight_ref, packed_ref, out_ref):
    rows, width = attended_ref.shape
    pieces = width // early
    mine = pl.multiple_of(lax.axis_index("sub") * early, LANES)
    total = jnp.dot(
        attended_ref[...],
        weight_ref[:, pl.ds(mine, early)],
        preferred_element_type=jnp.float32,
    ) + jnp.dot(
        jnp.concatenate(
            [packed_ref[i * rows : (i + 1) * rows, :] for i in range(pieces)], axis=1
        ),
        packed_ref[pieces * rows :, :],
        preferred_element_type=jnp.float32,
    )
    out_ref[...] = base_ref[...]
    out_ref[:, :early] = base_ref[:, :early] + gate_ref[:, :early] * total


def solution(mesh):
    patches, heads, subs = mesh.shape["patch"], mesh.shape["head"], mesh.shape["sub"]

    def per_device(
        queries, held_keys, held_values, key_change, value_change, out_weight, hidden_in, gate
    ):
        rows, width = queries.shape
        columns = hidden_in.shape[1]

        early = EARLY if heads == 2 and columns % LANES == 0 and columns > 4 * LANES else 0
        with jax.named_scope("residual_gather"):
            residual = call(
                prepare_kernel,
                jax.ShapeDtypeStruct((rows, 2 * width), jnp.bfloat16),
                [ANYWHERE] * 2,
                IN_VMEM,
                "prepare",
                scratch_shapes=[
                    pltpu.VMEM((rows, width), jnp.float32),
                    pltpu.VMEM((rows, width), jnp.float32),
                    pltpu.SemaphoreType.DMA((2,)),
                ],
            )(in_hbm(key_change), in_hbm(value_change))
            blocks = [residual] + [
                shift(residual, "patch", patches, step) for step in gather_steps(patches)
            ]

        with jax.named_scope("weight_swap"):
            weights = [out_weight] + [
                shift(out_weight, "sub", subs, i) for i in range(1, subs)
            ]

        if early:
            with jax.named_scope("early_weight"):
                early_weight = call(
                    functools.partial(early_weight_kernel, subs, columns, early),
                    jax.ShapeDtypeStruct((width, subs * early), jnp.bfloat16),
                    [ANYWHERE],
                    IN_VMEM,
                    "early_weight",
                    moved=4 * width * subs * early,
                    scratch_shapes=[pltpu.SemaphoreType.DMA((subs,))],
                )(in_hbm(out_weight))
                early_weight = shift(early_weight, "head", heads, 1)

        def weight_and_start(i, step, skip=0):
            def start():
                to = lax.rem(lax.axis_index("head") + step, heads) * subs + lax.axis_index("sub")
                return to * columns + skip

            if columns % LANES == 0:
                return weights[i], start
            return lax.dynamic_slice(weights[i], (0, start()), (width, columns)), lambda: None

        def pairs_and_start(step, skip=0):
            pairs = [
                x
                for i in range(subs)
                for x in (attended_parts[i], weight_and_start(i, step, skip)[0])
            ]
            return pairs, weight_and_start(0, step, skip)[1]

        tokens = rows * patches
        with jax.named_scope("attention"):
            products, values = call(
                functools.partial(stage_kernel, patches),
                [
                    jax.ShapeDtypeStruct((width // HD, rows, tokens), jnp.float32),
                    jax.ShapeDtypeStruct((tokens, width), jnp.bfloat16),
                ],
                [IN_VMEM] * 3,
                [IN_VMEM] * 2,
                "stage",
                flops=2_000_000_000,
            )(queries, held_keys, held_values)
            attended = call(
                functools.partial(attention_kernel, 1.0 / math.sqrt(HD)),
                jax.ShapeDtypeStruct((rows, width), jnp.bfloat16),
                [IN_VMEM] * (3 + len(blocks)),
                IN_VMEM,
                "attention",
                flops=2_000_000_000,
            )(queries, products, values, *blocks)

        with jax.named_scope("attended_swap"):
            attended_parts = [attended] + [
                shift(attended, "sub", subs, i) for i in range(1, subs)
            ]
            if early:
                other_attended = shift(attended, "head", heads, 1)

        term = jax.ShapeDtypeStruct((rows, columns), jnp.float32)
        sent = jax.ShapeDtypeStruct((rows, columns - early), jnp.bfloat16)
        product_flops = 2 * rows * width * columns
        with jax.named_scope("projection"):
            arrived = []
            for step in range(1, heads):
                pairs, start = pairs_and_start(step, early)
                total = call(
                    functools.partial(sent_term_kernel, start),
                    sent,
                    [IN_VMEM] * len(pairs),
                    IN_VMEM,
                    "sent_term",
                    2 * product_flops,
                )(*pairs)
                arrived.append(shift(total, "head", heads, step))
            gate_row = gate.reshape(1, columns)
            pairs, start = pairs_and_start(0)
            base = call(
                functools.partial(base_kernel, start),
                term,
                [IN_VMEM] * (2 + len(pairs)),
                IN_VMEM,
                "base",
                2 * product_flops,
            )(hidden_in, gate_row, *pairs)
            if early:
                packed = call(
                    functools.partial(pack_kernel, early),
                    jax.ShapeDtypeStruct((rows * (width // early) + width, early), jnp.bfloat16),
                    [IN_VMEM] * 2,
                    IN_VMEM,
                    "pack",
                )(other_attended, early_weight)
                packed = shift(packed, "sub", subs, 1)
                base = call(
                    functools.partial(early_kernel, early),
                    term,
                    [IN_VMEM] * 5,
                    IN_VMEM,
                    "early",
                    product_flops // 2,
                )(base, gate_row, other_attended, early_weight, packed)
            row_blocks = 3 if rows % (3 * ROW_TILE) == 0 else 1
            return call(
                functools.partial(final_kernel, early, row_blocks),
                jax.ShapeDtypeStruct((rows, columns), jnp.bfloat16),
                [IN_VMEM] * (2 + len(arrived)),
                ANYWHERE,
                "final",
                moved=rows * columns * 8,
                scratch_shapes=[
                    pltpu.VMEM((rows, columns), jnp.bfloat16),
                    pltpu.SemaphoreType.DMA((row_blocks,)),
                ],
            )(base, gate_row, *arrived)

    in_specs = (
        P(("groups", "patch"), ("head", "sub")),
        P("groups", ("head", "sub")),
        P("groups", ("head", "sub")),
        P(("groups", "patch"), ("head", "sub")),
        P(("groups", "patch"), ("head", "sub")),
        P(("head", "sub"), None),
        P(("groups", "patch"), ("head", "sub")),
        P(("groups", "head", "sub")),
    )
    out_specs = P(("groups", "patch"), ("head", "sub"))
    return jax.shard_map(
        per_device, mesh=mesh, in_specs=in_specs, out_specs=out_specs, check_vma=False
    )
```

```python
import functools
import math

import jax
import jax.numpy as jnp
from jax import lax
from jax.experimental import pallas as pl
from jax.experimental.pallas import tpu as pltpu
from jax.sharding import PartitionSpec as P

HD = 128
LANES = 128
ROW_TILE = 16
VMEM_LIMIT = 12 * 1024 * 1024
EARLY = 256

IN_VMEM = pl.BlockSpec(memory_space=pltpu.VMEM)
ANYWHERE = pl.BlockSpec(memory_space=pl.ANY)


def call(
    kernel,
    out_shape,
    in_specs,
    out_specs,
    name,
    flops=0,
    moved=0,
    scratch_shapes=(),
    vmem=VMEM_LIMIT,
):
    return pl.pallas_call(
        kernel,
        out_shape=out_shape,
        in_specs=in_specs,
        out_specs=out_specs,
        scratch_shapes=scratch_shapes,
        name=name,
        cost_estimate=pl.CostEstimate(flops=flops, bytes_accessed=moved, transcendentals=0),
        compiler_params=pltpu.CompilerParams(vmem_limit_bytes=vmem),
    )


def in_hbm(array):
    return pltpu.with_memory_space_constraint(array, pltpu.HBM)


def shift(array, axis, size, step):
    return lax.ppermute(array, axis, [(i, (i + step) % size) for i in range(size)])


def gather_steps(patches):
    return list(range(patches - 1, 0, -1))


def gather_sources(patches, place):
    return [place] + [lax.rem(place + patches - step, patches) for step in gather_steps(patches)]


def early_weight_kernel(subs, columns, early, weight_ref, out_ref, sems):
    chip = (1 - lax.axis_index("head")) * subs
    copies = []
    for sub in range(subs):
        at = pl.multiple_of((chip + sub) * columns, LANES)
        copies.append(
            pltpu.make_async_copy(
                weight_ref.at[:, pl.ds(at, early)],
                out_ref.at[:, pl.ds(sub * early, early)],
                sems.at[sub],
            )
        )
    for copy in copies:
        copy.start()
    for copy in copies:
        copy.wait()


def stage_kernel(patches, q_ref, held_k_ref, held_v_ref, products_ref, values_ref):
    rows, width = q_ref.shape
    sources = gather_sources(patches, lax.axis_index("patch"))
    starts = [pl.multiple_of(source * rows, rows) for source in sources]
    for i, at in enumerate(starts):
        values_ref[i * rows : (i + 1) * rows, :] = held_v_ref[pl.ds(at, rows), :]
    for head in range(width // HD):
        cols = slice(head * HD, (head + 1) * HD)
        keys = jnp.concatenate([held_k_ref[pl.ds(at, rows), cols] for at in starts], axis=0)
        products_ref[head] = dot_transposed(q_ref[:, cols], keys)


def dot_transposed(a, b):
    return lax.dot_general(
        a, b, (((1,), (1,)), ((), ())), preferred_element_type=jnp.float32
    )


def attention_kernel(scale, q_ref, products_ref, values_ref, *refs):
    block_refs, out_ref = refs[:-1], refs[-1]
    rows, width = q_ref.shape
    blocks = jnp.concatenate([ref[...] for ref in block_refs], axis=0)
    for head in range(width // HD):
        cols = slice(head * HD, (head + 1) * HD)
        value_cols = slice(width + head * HD, width + (head + 1) * HD)
        products = products_ref[head] + dot_transposed(q_ref[:, cols], blocks[:, cols])
        scores = products * scale
        weights = jnp.exp(scores - jnp.max(scores, axis=1, keepdims=True))
        totals = jnp.sum(weights, axis=1, keepdims=True)
        high = weights.astype(jnp.bfloat16)
        low = (weights - high.astype(jnp.float32)).astype(jnp.bfloat16)
        sums = jnp.dot(
            jnp.concatenate([high, low], axis=0),
            jnp.concatenate([values_ref[:, cols], blocks[:, value_cols]], axis=1),
            preferred_element_type=jnp.float32,
        )
        sums = sums[:rows] + sums[rows:]
        sums = sums[:, :HD] + sums[:, HD:]
        out_ref[:, cols] = (sums / totals).astype(jnp.bfloat16)


def block_dot(a_ref, weight_ref, start, columns):
    if start is None:
        weight = weight_ref[...]
    else:
        weight = weight_ref[:, pl.ds(pl.multiple_of(start, LANES), columns)]
    return jnp.dot(a_ref[...], weight, preferred_element_type=jnp.float32)


def products(start, columns, refs):
    total = 0.0
    for attended_ref, weight_ref in zip(refs[::2], refs[1::2]):
        total = total + block_dot(attended_ref, weight_ref, start, columns)
    return total


def sent_term_kernel(start, *refs):
    out_ref = refs[-1]
    total = products(start(), out_ref.shape[1], refs[:-1])
    out_ref[...] = total.astype(jnp.bfloat16)


def base_kernel(start, hidden_ref, gate_ref, *refs):
    out_ref = refs[-1]
    total = products(start(), out_ref.shape[1], refs[:-1])
    out_ref[...] = hidden_ref[...].astype(jnp.float32) + gate_ref[...] * total


def pack_kernel(early, attended_ref, weight_ref, out_ref):
    rows, width = attended_ref.shape
    for i in range(width // early):
        out_ref[i * rows : (i + 1) * rows, :] = attended_ref[:, i * early : (i + 1) * early]
    other = pl.multiple_of((1 - lax.axis_index("sub")) * early, LANES)
    out_ref[rows * (width // early) :, :] = weight_ref[:, pl.ds(other, early)]


def early_kernel(early, base_ref, gate_ref, attended_ref, weight_ref, packed_ref, out_ref):
    rows, width = attended_ref.shape
    pieces = width // early
    mine = pl.multiple_of(lax.axis_index("sub") * early, LANES)
    total = jnp.dot(
        attended_ref[...],
        weight_ref[:, pl.ds(mine, early)],
        preferred_element_type=jnp.float32,
    ) + jnp.dot(
        jnp.concatenate(
            [packed_ref[i * rows : (i + 1) * rows, :] for i in range(pieces)], axis=1
        ),
        packed_ref[pieces * rows :, :],
        preferred_element_type=jnp.float32,
    )
    out_ref[...] = base_ref[...]
    out_ref[:, :early] = base_ref[:, :early] + gate_ref[:, :early] * total


def solution(mesh):
    patches, heads, subs = mesh.shape["patch"], mesh.shape["head"], mesh.shape["sub"]

    def per_device(
        queries, held_keys, held_values, key_change, value_change, out_weight, hidden_in, gate
    ):
        rows, width = queries.shape
        columns = hidden_in.shape[1]

        early = EARLY if heads == 2 and columns % LANES == 0 and columns > 4 * LANES else 0
        with jax.named_scope("residual_gather"):
            low = jnp.float32(-jnp.inf)
            residual = jnp.maximum(
                lax.pad(key_change, low, ((0, 0, 0), (0, width, 0))),
                lax.pad(value_change, low, ((0, 0, 0), (width, 0, 0))),
            ).astype(jnp.bfloat16)
            blocks = [residual] + [
                shift(residual, "patch", patches, step) for step in gather_steps(patches)
            ]

        with jax.named_scope("weight_swap"):
            weights = [out_weight] + [
                shift(out_weight, "sub", subs, i) for i in range(1, subs)
            ]

        if early:
            with jax.named_scope("early_weight"):
                early_weight = call(
                    functools.partial(early_weight_kernel, subs, columns, early),
                    jax.ShapeDtypeStruct((width, subs * early), jnp.bfloat16),
                    [ANYWHERE],
                    IN_VMEM,
                    "early_weight",
                    moved=4 * width * subs * early,
                    scratch_shapes=[pltpu.SemaphoreType.DMA((subs,))],
                )(in_hbm(out_weight))
                early_weight = shift(early_weight, "head", heads, 1)

        def weight_and_start(i, step, skip=0):
            def start():
                to = lax.rem(lax.axis_index("head") + step, heads) * subs + lax.axis_index("sub")
                return to * columns + skip

            if columns % LANES == 0:
                return weights[i], start
            return lax.dynamic_slice(weights[i], (0, start()), (width, columns)), lambda: None

        def pairs_and_start(step, skip=0):
            pairs = [
                x
                for i in range(subs)
                for x in (attended_parts[i], weight_and_start(i, step, skip)[0])
            ]
            return pairs, weight_and_start(0, step, skip)[1]

        tokens = rows * patches
        with jax.named_scope("attention"):
            products, values = call(
                functools.partial(stage_kernel, patches),
                [
                    jax.ShapeDtypeStruct((width // HD, rows, tokens), jnp.float32),
                    jax.ShapeDtypeStruct((tokens, width), jnp.bfloat16),
                ],
                [IN_VMEM] * 3,
                [IN_VMEM] * 2,
                "stage",
                flops=2_000_000_000,
            )(queries, held_keys, held_values)
            attended = call(
                functools.partial(attention_kernel, 1.0 / math.sqrt(HD)),
                jax.ShapeDtypeStruct((rows, width), jnp.bfloat16),
                [IN_VMEM] * (3 + len(blocks)),
                IN_VMEM,
                "attention",
                flops=2_000_000_000,
            )(queries, products, values, *blocks)

        with jax.named_scope("attended_swap"):
            attended_parts = [attended] + [
                shift(attended, "sub", subs, i) for i in range(1, subs)
            ]
            if early:
                other_attended = shift(attended, "head", heads, 1)

        term = jax.ShapeDtypeStruct((rows, columns), jnp.float32)
        sent = jax.ShapeDtypeStruct((rows, columns - early), jnp.bfloat16)
        product_flops = 2 * rows * width * columns
        with jax.named_scope("projection"):
            arrived = []
            for step in range(1, heads):
                pairs, start = pairs_and_start(step, early)
                total = call(
                    functools.partial(sent_term_kernel, start),
                    sent,
                    [IN_VMEM] * len(pairs),
                    IN_VMEM,
                    "sent_term",
                    2 * product_flops,
                )(*pairs)
                arrived.append(shift(total, "head", heads, step))
            gate_row = gate.reshape(1, columns)
            pairs, start = pairs_and_start(0)
            base = call(
                functools.partial(base_kernel, start),
                term,
                [IN_VMEM] * (2 + len(pairs)),
                IN_VMEM,
                "base",
                2 * product_flops,
            )(hidden_in, gate_row, *pairs)
            if early:
                packed = call(
                    functools.partial(pack_kernel, early),
                    jax.ShapeDtypeStruct((rows * (width // early) + width, early), jnp.bfloat16),
                    [IN_VMEM] * 2,
                    IN_VMEM,
                    "pack",
                )(other_attended, early_weight)
                packed = shift(packed, "sub", subs, 1)
                base = call(
                    functools.partial(early_kernel, early),
                    term,
                    [IN_VMEM] * 5,
                    IN_VMEM,
                    "early",
                    product_flops // 2,
                )(base, gate_row, other_attended, early_weight, packed)
            total = functools.reduce(jnp.add, [x.astype(jnp.float32) for x in arrived])
            total = lax.pad(total, jnp.float32(0), ((0, 0, 0), (early, 0, 0)))
            return (base + gate_row * total).astype(jnp.bfloat16)

    in_specs = (
        P(("groups", "patch"), ("head", "sub")),
        P("groups", ("head", "sub")),
        P("groups", ("head", "sub")),
        P(("groups", "patch"), ("head", "sub")),
        P(("groups", "patch"), ("head", "sub")),
        P(("head", "sub"), None),
        P(("groups", "patch"), ("head", "sub")),
        P(("groups", "head", "sub")),
    )
    out_specs = P(("groups", "patch"), ("head", "sub"))
    return jax.shard_map(
        per_device, mesh=mesh, in_specs=in_specs, out_specs=out_specs, check_vma=False
    )
```

```python
import functools
import math

import jax
import jax.numpy as jnp
from jax import lax
from jax.experimental import pallas as pl
from jax.experimental.pallas import tpu as pltpu
from jax.sharding import PartitionSpec as P

HD = 128
LANES = 128
ROW_TILE = 16
VMEM_LIMIT = 12 * 1024 * 1024
EARLY = 256

IN_VMEM = pl.BlockSpec(memory_space=pltpu.VMEM)
ANYWHERE = pl.BlockSpec(memory_space=pl.ANY)


def call(
    kernel,
    out_shape,
    in_specs,
    out_specs,
    name,
    flops=0,
    moved=0,
    scratch_shapes=(),
    vmem=VMEM_LIMIT,
):
    return pl.pallas_call(
        kernel,
        out_shape=out_shape,
        in_specs=in_specs,
        out_specs=out_specs,
        scratch_shapes=scratch_shapes,
        name=name,
        cost_estimate=pl.CostEstimate(flops=flops, bytes_accessed=moved, transcendentals=0),
        compiler_params=pltpu.CompilerParams(vmem_limit_bytes=vmem),
    )


def in_hbm(array):
    return pltpu.with_memory_space_constraint(array, pltpu.HBM)


def shift(array, axis, size, step):
    return lax.ppermute(array, axis, [(i, (i + step) % size) for i in range(size)])


def gather_steps(patches):
    return list(range(patches - 1, 0, -1))


def gather_sources(patches, place):
    return [place] + [lax.rem(place + patches - step, patches) for step in gather_steps(patches)]


def early_weight_kernel(subs, columns, early, weight_ref, out_ref, sems):
    chip = (1 - lax.axis_index("head")) * subs
    copies = []
    for sub in range(subs):
        at = pl.multiple_of((chip + sub) * columns, LANES)
        copies.append(
            pltpu.make_async_copy(
                weight_ref.at[:, pl.ds(at, early)],
                out_ref.at[:, pl.ds(sub * early, early)],
                sems.at[sub],
            )
        )
    for copy in copies:
        copy.start()
    for copy in copies:
        copy.wait()


def stage_kernel(
    patches, q_hbm, held_k_hbm, held_v_hbm, q_ref, products_ref, values_ref, keys_ref, sems
):
    rows, width = q_ref.shape
    sources = gather_sources(patches, lax.axis_index("patch"))
    copies = [pltpu.make_async_copy(q_hbm, q_ref, sems.at[0])]
    for i, source in enumerate(sources):
        at = pl.multiple_of(source * rows, rows)
        for n, (held, ref) in enumerate(((held_k_hbm, keys_ref), (held_v_hbm, values_ref))):
            copies.append(
                pltpu.make_async_copy(
                    held.at[pl.ds(at, rows), :],
                    ref.at[i * rows : (i + 1) * rows, :],
                    sems.at[1 + 2 * i + n],
                )
            )
    for copy in copies:
        copy.start()
    for copy in copies:
        copy.wait()
    for head in range(width // HD):
        cols = slice(head * HD, (head + 1) * HD)
        products_ref[head] = dot_transposed(q_ref[:, cols], keys_ref[:, cols])


def dot_transposed(a, b):
    return lax.dot_general(
        a, b, (((1,), (1,)), ((), ())), preferred_element_type=jnp.float32
    )


def attention_kernel(scale, q_ref, products_ref, values_ref, *refs):
    block_refs, out_ref = refs[:-1], refs[-1]
    rows, width = q_ref.shape
    blocks = jnp.concatenate([ref[...] for ref in block_refs], axis=0)
    for head in range(width // HD):
        cols = slice(head * HD, (head + 1) * HD)
        value_cols = slice(width + head * HD, width + (head + 1) * HD)
        products = products_ref[head] + dot_transposed(q_ref[:, cols], blocks[:, cols])
        scores = products * scale
        weights = jnp.exp(scores - jnp.max(scores, axis=1, keepdims=True))
        totals = jnp.sum(weights, axis=1, keepdims=True)
        high = weights.astype(jnp.bfloat16)
        low = (weights - high.astype(jnp.float32)).astype(jnp.bfloat16)
        sums = jnp.dot(
            jnp.concatenate([high, low], axis=0),
            jnp.concatenate([values_ref[:, cols], blocks[:, value_cols]], axis=1),
            preferred_element_type=jnp.float32,
        )
        sums = sums[:rows] + sums[rows:]
        sums = sums[:, :HD] + sums[:, HD:]
        out_ref[:, cols] = (sums / totals).astype(jnp.bfloat16)


def block_dot(a_ref, weight_ref, start, columns):
    if start is None:
        weight = weight_ref[...]
    else:
        weight = weight_ref[:, pl.ds(pl.multiple_of(start, LANES), columns)]
    return jnp.dot(a_ref[...], weight, preferred_element_type=jnp.float32)


def products(start, columns, refs):
    total = 0.0
    for attended_ref, weight_ref in zip(refs[::2], refs[1::2]):
        total = total + block_dot(attended_ref, weight_ref, start, columns)
    return total


def sent_term_kernel(start, *refs):
    out_ref = refs[-1]
    total = products(start(), out_ref.shape[1], refs[:-1])
    out_ref[...] = total.astype(jnp.bfloat16)


def base_kernel(start, hidden_ref, gate_ref, *refs):
    out_ref = refs[-1]
    total = products(start(), out_ref.shape[1], refs[:-1])
    out_ref[...] = hidden_ref[...].astype(jnp.float32) + gate_ref[...] * total


def final_kernel(early, blocks, base_ref, gate_ref, *refs):
    arrived_refs, (out_ref, result, sems) = refs[:-3], refs[-3:]
    rows = base_ref.shape[0] // blocks
    copies = []
    for n in range(blocks):
        at = slice(n * rows, (n + 1) * rows)
        total = 0.0
        for ref in arrived_refs:
            total = total + ref[at, :].astype(jnp.float32)
        if early:
            result[at, :early] = base_ref[at, :early].astype(jnp.bfloat16)
        total = base_ref[at, early:] + gate_ref[:, early:] * total
        result[at, early:] = total.astype(jnp.bfloat16)
        copies.append(pltpu.make_async_copy(result.at[at, :], out_ref.at[at, :], sems.at[n]))
        copies[n].start()
    for copy in copies:
        copy.wait()


def pack_kernel(early, attended_ref, weight_ref, out_ref):
    rows, width = attended_ref.shape
    for i in range(width // early):
        out_ref[i * rows : (i + 1) * rows, :] = attended_ref[:, i * early : (i + 1) * early]
    other = pl.multiple_of((1 - lax.axis_index("sub")) * early, LANES)
    out_ref[rows * (width // early) :, :] = weight_ref[:, pl.ds(other, early)]


def early_kernel(early, base_ref, gate_ref, attended_ref, weight_ref, packed_ref, out_ref):
    rows, width = attended_ref.shape
    pieces = width // early
    mine = pl.multiple_of(lax.axis_index("sub") * early, LANES)
    total = jnp.dot(
        attended_ref[...],
        weight_ref[:, pl.ds(mine, early)],
        preferred_element_type=jnp.float32,
    ) + jnp.dot(
        jnp.concatenate(
            [packed_ref[i * rows : (i + 1) * rows, :] for i in range(pieces)], axis=1
        ),
        packed_ref[pieces * rows :, :],
        preferred_element_type=jnp.float32,
    )
    out_ref[...] = base_ref[...]
    out_ref[:, :early] = base_ref[:, :early] + gate_ref[:, :early] * total


def solution(mesh):
    patches, heads, subs = mesh.shape["patch"], mesh.shape["head"], mesh.shape["sub"]

    def per_device(
        queries, held_keys, held_values, key_change, value_change, out_weight, hidden_in, gate
    ):
        rows, width = queries.shape
        columns = hidden_in.shape[1]

        early = EARLY if heads == 2 and columns % LANES == 0 and columns > 4 * LANES else 0
        with jax.named_scope("residual_gather"):
            low = jnp.float32(-jnp.inf)
            residual = jnp.maximum(
                lax.pad(key_change, low, ((0, 0, 0), (0, width, 0))),
                lax.pad(value_change, low, ((0, 0, 0), (width, 0, 0))),
            ).astype(jnp.bfloat16)
            blocks = [residual] + [
                shift(residual, "patch", patches, step) for step in gather_steps(patches)
            ]

        with jax.named_scope("weight_swap"):
            swapped, _ = lax.optimization_barrier((out_weight, residual))
            weights = [out_weight] + [shift(swapped, "sub", subs, i) for i in range(1, subs)]

        if early:
            with jax.named_scope("early_weight"):
                early_weight = call(
                    functools.partial(early_weight_kernel, subs, columns, early),
                    jax.ShapeDtypeStruct((width, subs * early), jnp.bfloat16),
                    [ANYWHERE],
                    IN_VMEM,
                    "early_weight",
                    moved=4 * width * subs * early,
                    scratch_shapes=[pltpu.SemaphoreType.DMA((subs,))],
                )(in_hbm(out_weight))
                early_weight = shift(early_weight, "head", heads, 1)

        def weight_and_start(i, step, skip=0):
            def start():
                to = lax.rem(lax.axis_index("head") + step, heads) * subs + lax.axis_index("sub")
                return to * columns + skip

            if columns % LANES == 0:
                return weights[i], start
            return lax.dynamic_slice(weights[i], (0, start()), (width, columns)), lambda: None

        def pairs_and_start(step, skip=0):
            pairs = [
                x
                for i in range(subs)
                for x in (attended_parts[i], weight_and_start(i, step, skip)[0])
            ]
            return pairs, weight_and_start(0, step, skip)[1]

        tokens = rows * patches
        with jax.named_scope("attention"):
            staged_queries, products, values = call(
                functools.partial(stage_kernel, patches),
                [
                    jax.ShapeDtypeStruct((rows, width), jnp.bfloat16),
                    jax.ShapeDtypeStruct((width // HD, rows, tokens), jnp.float32),
                    jax.ShapeDtypeStruct((tokens, width), jnp.bfloat16),
                ],
                [ANYWHERE] * 3,
                [IN_VMEM] * 3,
                "stage",
                flops=2_000_000_000,
                scratch_shapes=[
                    pltpu.VMEM((tokens, width), jnp.bfloat16),
                    pltpu.SemaphoreType.DMA((1 + 2 * patches,)),
                ],
            )(in_hbm(queries), in_hbm(held_keys), in_hbm(held_values))
            attended = call(
                functools.partial(attention_kernel, 1.0 / math.sqrt(HD)),
                jax.ShapeDtypeStruct((rows, width), jnp.bfloat16),
                [IN_VMEM] * (3 + len(blocks)),
                IN_VMEM,
                "attention",
                flops=2_000_000_000,
            )(staged_queries, products, values, *blocks)

        with jax.named_scope("attended_swap"):
            attended_parts = [attended] + [
                shift(attended, "sub", subs, i) for i in range(1, subs)
            ]
            if early:
                other_attended = shift(attended, "head", heads, 1)

        term = jax.ShapeDtypeStruct((rows, columns), jnp.float32)
        sent = jax.ShapeDtypeStruct((rows, columns - early), jnp.bfloat16)
        product_flops = 2 * rows * width * columns
        with jax.named_scope("projection"):
            arrived = []
            for step in range(1, heads):
                pairs, start = pairs_and_start(step, early)
                total = call(
                    functools.partial(sent_term_kernel, start),
                    sent,
                    [IN_VMEM] * len(pairs),
                    IN_VMEM,
                    "sent_term",
                    2 * product_flops,
                )(*pairs)
                arrived.append(shift(total, "head", heads, step))
            gate_row = gate.reshape(1, columns)
            pairs, start = pairs_and_start(0)
            base = call(
                functools.partial(base_kernel, start),
                term,
                [IN_VMEM] * (2 + len(pairs)),
                IN_VMEM,
                "base",
                2 * product_flops,
            )(hidden_in, gate_row, *pairs)
            if early:
                packed = call(
                    functools.partial(pack_kernel, early),
                    jax.ShapeDtypeStruct((rows * (width // early) + width, early), jnp.bfloat16),
                    [IN_VMEM] * 2,
                    IN_VMEM,
                    "pack",
                )(other_attended, early_weight)
                packed = shift(packed, "sub", subs, 1)
                base = call(
                    functools.partial(early_kernel, early),
                    term,
                    [IN_VMEM] * 5,
                    IN_VMEM,
                    "early",
                    product_flops // 2,
                )(base, gate_row, other_attended, early_weight, packed)
            row_blocks = 3 if rows % (3 * ROW_TILE) == 0 else 1
            return call(
                functools.partial(final_kernel, early, row_blocks),
                jax.ShapeDtypeStruct((rows, columns), jnp.bfloat16),
                [IN_VMEM] * (2 + len(arrived)),
                ANYWHERE,
                "final",
                moved=rows * columns * 8,
                scratch_shapes=[
                    pltpu.VMEM((rows, columns), jnp.bfloat16),
                    pltpu.SemaphoreType.DMA((row_blocks,)),
                ],
            )(base, gate_row, *arrived)

    in_specs = (
        P(("groups", "patch"), ("head", "sub")),
        P("groups", ("head", "sub")),
        P("groups", ("head", "sub")),
        P(("groups", "patch"), ("head", "sub")),
        P(("groups", "patch"), ("head", "sub")),
        P(("head", "sub"), None),
        P(("groups", "patch"), ("head", "sub")),
        P(("groups", "head", "sub")),
    )
    out_specs = P(("groups", "patch"), ("head", "sub"))
    return jax.shard_map(
        per_device, mesh=mesh, in_specs=in_specs, out_specs=out_specs, check_vma=False
    )
```

```python
import functools
import math

import jax
import jax.numpy as jnp
from jax import lax
from jax.experimental import pallas as pl
from jax.experimental.pallas import tpu as pltpu
from jax.sharding import PartitionSpec as P

HD = 128
LANES = 128
ROW_TILE = 16
VMEM_LIMIT = 12 * 1024 * 1024
EARLY = 256

IN_VMEM = pl.BlockSpec(memory_space=pltpu.VMEM)
ANYWHERE = pl.BlockSpec(memory_space=pl.ANY)


def call(
    kernel,
    out_shape,
    in_specs,
    out_specs,
    name,
    flops=0,
    moved=0,
    scratch_shapes=(),
    vmem=VMEM_LIMIT,
):
    return pl.pallas_call(
        kernel,
        out_shape=out_shape,
        in_specs=in_specs,
        out_specs=out_specs,
        scratch_shapes=scratch_shapes,
        name=name,
        cost_estimate=pl.CostEstimate(flops=flops, bytes_accessed=moved, transcendentals=0),
        compiler_params=pltpu.CompilerParams(vmem_limit_bytes=vmem),
    )


def in_hbm(array):
    return pltpu.with_memory_space_constraint(array, pltpu.HBM)


def shift(array, axis, size, step):
    return lax.ppermute(array, axis, [(i, (i + step) % size) for i in range(size)])


def gather_steps(patches):
    return [3, 1, 2] if patches == 4 else list(range(patches - 1, 0, -1))


def gather_sources(patches, place):
    return [place] + [lax.rem(place + patches - step, patches) for step in gather_steps(patches)]


def early_weight_kernel(subs, columns, early, weight_ref, out_ref, sems):
    chip = (1 - lax.axis_index("head")) * subs
    copies = []
    for sub in range(subs):
        at = pl.multiple_of((chip + sub) * columns, LANES)
        copies.append(
            pltpu.make_async_copy(
                weight_ref.at[:, pl.ds(at, early)],
                out_ref.at[:, pl.ds(sub * early, early)],
                sems.at[sub],
            )
        )
    for copy in copies:
        copy.start()
    for copy in copies:
        copy.wait()


def stage_kernel(
    patches, q_hbm, held_k_hbm, held_v_hbm, q_ref, products_ref, values_ref, keys_ref, sems
):
    rows, width = q_ref.shape
    sources = gather_sources(patches, lax.axis_index("patch"))
    copies = [pltpu.make_async_copy(q_hbm, q_ref, sems.at[0])]
    for i, source in enumerate(sources):
        at = pl.multiple_of(source * rows, rows)
        for n, (held, ref) in enumerate(((held_k_hbm, keys_ref), (held_v_hbm, values_ref))):
            copies.append(
                pltpu.make_async_copy(
                    held.at[pl.ds(at, rows), :],
                    ref.at[i * rows : (i + 1) * rows, :],
                    sems.at[1 + 2 * i + n],
                )
            )
    for copy in copies:
        copy.start()
    for copy in copies:
        copy.wait()
    for head in range(width // HD):
        cols = slice(head * HD, (head + 1) * HD)
        products_ref[head] = dot_transposed(q_ref[:, cols], keys_ref[:, cols])


def dot_transposed(a, b):
    return lax.dot_general(
        a, b, (((1,), (1,)), ((), ())), preferred_element_type=jnp.float32
    )


def attention_kernel(scale, q_ref, products_ref, values_ref, *refs):
    block_refs, out_ref = refs[:-1], refs[-1]
    rows, width = q_ref.shape
    blocks = jnp.concatenate([ref[...] for ref in block_refs], axis=0)
    for head in range(width // HD):
        cols = slice(head * HD, (head + 1) * HD)
        value_cols = slice(width + head * HD, width + (head + 1) * HD)
        products = products_ref[head] + dot_transposed(q_ref[:, cols], blocks[:, cols])
        scores = products * scale
        weights = jnp.exp(scores - jnp.max(scores, axis=1, keepdims=True))
        totals = jnp.sum(weights, axis=1, keepdims=True)
        high = weights.astype(jnp.bfloat16)
        low = (weights - high.astype(jnp.float32)).astype(jnp.bfloat16)
        sums = jnp.dot(
            jnp.concatenate([high, low], axis=0),
            jnp.concatenate([values_ref[:, cols], blocks[:, value_cols]], axis=1),
            preferred_element_type=jnp.float32,
        )
        sums = sums[:rows] + sums[rows:]
        sums = sums[:, :HD] + sums[:, HD:]
        out_ref[:, cols] = (sums / totals).astype(jnp.bfloat16)


def block_dot(a_ref, weight_ref, start, columns):
    if start is None:
        weight = weight_ref[...]
    else:
        weight = weight_ref[:, pl.ds(pl.multiple_of(start, LANES), columns)]
    return jnp.dot(a_ref[...], weight, preferred_element_type=jnp.float32)


def products(start, columns, refs):
    total = 0.0
    for attended_ref, weight_ref in zip(refs[::2], refs[1::2]):
        total = total + block_dot(attended_ref, weight_ref, start, columns)
    return total


def sent_term_kernel(start, *refs):
    out_ref = refs[-1]
    total = products(start(), out_ref.shape[1], refs[:-1])
    out_ref[...] = total.astype(jnp.bfloat16)


def base_kernel(start, hidden_ref, gate_ref, *refs):
    out_ref = refs[-1]
    total = products(start(), out_ref.shape[1], refs[:-1])
    out_ref[...] = hidden_ref[...].astype(jnp.float32) + gate_ref[...] * total


def final_kernel(early, blocks, base_ref, gate_ref, *refs):
    arrived_refs, (out_ref, result, sems) = refs[:-3], refs[-3:]
    rows = base_ref.shape[0] // blocks
    copies = []
    for n in range(blocks):
        at = slice(n * rows, (n + 1) * rows)
        total = 0.0
        for ref in arrived_refs:
            total = total + ref[at, :].astype(jnp.float32)
        if early:
            result[at, :early] = base_ref[at, :early].astype(jnp.bfloat16)
        total = base_ref[at, early:] + gate_ref[:, early:] * total
        result[at, early:] = total.astype(jnp.bfloat16)
        copies.append(pltpu.make_async_copy(result.at[at, :], out_ref.at[at, :], sems.at[n]))
        copies[n].start()
    for copy in copies:
        copy.wait()


def pack_kernel(early, attended_ref, weight_ref, out_ref):
    rows, width = attended_ref.shape
    for i in range(width // early):
        out_ref[i * rows : (i + 1) * rows, :] = attended_ref[:, i * early : (i + 1) * early]
    other = pl.multiple_of((1 - lax.axis_index("sub")) * early, LANES)
    out_ref[rows * (width // early) :, :] = weight_ref[:, pl.ds(other, early)]


def early_kernel(early, base_ref, gate_ref, attended_ref, weight_ref, packed_ref, out_ref):
    rows, width = attended_ref.shape
    pieces = width // early
    mine = pl.multiple_of(lax.axis_index("sub") * early, LANES)
    total = jnp.dot(
        attended_ref[...],
        weight_ref[:, pl.ds(mine, early)],
        preferred_element_type=jnp.float32,
    ) + jnp.dot(
        jnp.concatenate(
            [packed_ref[i * rows : (i + 1) * rows, :] for i in range(pieces)], axis=1
        ),
        packed_ref[pieces * rows :, :],
        preferred_element_type=jnp.float32,
    )
    out_ref[...] = base_ref[...]
    out_ref[:, :early] = base_ref[:, :early] + gate_ref[:, :early] * total


def solution(mesh):
    patches, heads, subs = mesh.shape["patch"], mesh.shape["head"], mesh.shape["sub"]

    def per_device(
        queries, held_keys, held_values, key_change, value_change, out_weight, hidden_in, gate
    ):
        rows, width = queries.shape
        columns = hidden_in.shape[1]

        early = EARLY if heads == 2 and columns % LANES == 0 and columns > 4 * LANES else 0
        with jax.named_scope("residual_gather"):
            low = jnp.float32(-jnp.inf)
            residual = jnp.maximum(
                lax.pad(key_change, low, ((0, 0, 0), (0, width, 0))),
                lax.pad(value_change, low, ((0, 0, 0), (width, 0, 0))),
            ).astype(jnp.bfloat16)
            blocks = [residual] + [
                shift(residual, "patch", patches, step) for step in gather_steps(patches)
            ]

        with jax.named_scope("weight_swap"):
            swapped, _ = lax.optimization_barrier((out_weight, residual))
            weights = [out_weight] + [shift(swapped, "sub", subs, i) for i in range(1, subs)]

        if early:
            with jax.named_scope("early_weight"):
                early_weight = call(
                    functools.partial(early_weight_kernel, subs, columns, early),
                    jax.ShapeDtypeStruct((width, subs * early), jnp.bfloat16),
                    [ANYWHERE],
                    IN_VMEM,
                    "early_weight",
                    moved=4 * width * subs * early,
                    scratch_shapes=[pltpu.SemaphoreType.DMA((subs,))],
                )(in_hbm(out_weight))
                early_weight = shift(early_weight, "head", heads, 1)

        def weight_and_start(i, step, skip=0):
            def start():
                to = lax.rem(lax.axis_index("head") + step, heads) * subs + lax.axis_index("sub")
                return to * columns + skip

            if columns % LANES == 0:
                return weights[i], start
            return lax.dynamic_slice(weights[i], (0, start()), (width, columns)), lambda: None

        def pairs_and_start(step, skip=0):
            pairs = [
                x
                for i in range(subs)
                for x in (attended_parts[i], weight_and_start(i, step, skip)[0])
            ]
            return pairs, weight_and_start(0, step, skip)[1]

        tokens = rows * patches
        with jax.named_scope("attention"):
            staged_queries, products, values = call(
                functools.partial(stage_kernel, patches),
                [
                    jax.ShapeDtypeStruct((rows, width), jnp.bfloat16),
                    jax.ShapeDtypeStruct((width // HD, rows, tokens), jnp.float32),
                    jax.ShapeDtypeStruct((tokens, width), jnp.bfloat16),
                ],
                [ANYWHERE] * 3,
                [IN_VMEM] * 3,
                "stage",
                flops=2_000_000_000,
                scratch_shapes=[
                    pltpu.VMEM((tokens, width), jnp.bfloat16),
                    pltpu.SemaphoreType.DMA((1 + 2 * patches,)),
                ],
            )(in_hbm(queries), in_hbm(held_keys), in_hbm(held_values))
            attended = call(
                functools.partial(attention_kernel, 1.0 / math.sqrt(HD)),
                jax.ShapeDtypeStruct((rows, width), jnp.bfloat16),
                [IN_VMEM] * (3 + len(blocks)),
                IN_VMEM,
                "attention",
                flops=2_000_000_000,
            )(staged_queries, products, values, *blocks)

        with jax.named_scope("attended_swap"):
            attended_parts = [attended] + [
                shift(attended, "sub", subs, i) for i in range(1, subs)
            ]
            if early:
                other_attended = shift(attended, "head", heads, 1)

        term = jax.ShapeDtypeStruct((rows, columns), jnp.float32)
        sent = jax.ShapeDtypeStruct((rows, columns - early), jnp.bfloat16)
        product_flops = 2 * rows * width * columns
        with jax.named_scope("projection"):
            arrived = []
            for step in range(1, heads):
                pairs, start = pairs_and_start(step, early)
                total = call(
                    functools.partial(sent_term_kernel, start),
                    sent,
                    [IN_VMEM] * len(pairs),
                    IN_VMEM,
                    "sent_term",
                    2 * product_flops,
                )(*pairs)
                arrived.append(shift(total, "head", heads, step))
            gate_row = gate.reshape(1, columns)
            pairs, start = pairs_and_start(0)
            base = call(
                functools.partial(base_kernel, start),
                term,
                [IN_VMEM] * (2 + len(pairs)),
                IN_VMEM,
                "base",
                2 * product_flops,
            )(hidden_in, gate_row, *pairs)
            if early:
                packed = call(
                    functools.partial(pack_kernel, early),
                    jax.ShapeDtypeStruct((rows * (width // early) + width, early), jnp.bfloat16),
                    [IN_VMEM] * 2,
                    IN_VMEM,
                    "pack",
                )(other_attended, early_weight)
                packed = shift(packed, "sub", subs, 1)
                base = call(
                    functools.partial(early_kernel, early),
                    term,
                    [IN_VMEM] * 5,
                    IN_VMEM,
                    "early",
                    product_flops // 2,
                )(base, gate_row, other_attended, early_weight, packed)
            row_blocks = 3 if rows % (3 * ROW_TILE) == 0 else 1
            return call(
                functools.partial(final_kernel, early, row_blocks),
                jax.ShapeDtypeStruct((rows, columns), jnp.bfloat16),
                [IN_VMEM] * (2 + len(arrived)),
                ANYWHERE,
                "final",
                moved=rows * columns * 8,
                scratch_shapes=[
                    pltpu.VMEM((rows, columns), jnp.bfloat16),
                    pltpu.SemaphoreType.DMA((row_blocks,)),
                ],
            )(base, gate_row, *arrived)

    in_specs = (
        P(("groups", "patch"), ("head", "sub")),
        P("groups", ("head", "sub")),
        P("groups", ("head", "sub")),
        P(("groups", "patch"), ("head", "sub")),
        P(("groups", "patch"), ("head", "sub")),
        P(("head", "sub"), None),
        P(("groups", "patch"), ("head", "sub")),
        P(("groups", "head", "sub")),
    )
    out_specs = P(("groups", "patch"), ("head", "sub"))
    return jax.shard_map(
        per_device, mesh=mesh, in_specs=in_specs, out_specs=out_specs, check_vma=False
    )
```

```python
import functools
import math

import jax
import jax.numpy as jnp
from jax import lax
from jax.experimental import pallas as pl
from jax.experimental.pallas import tpu as pltpu
from jax.sharding import PartitionSpec as P

HD = 128
LANES = 128
ROW_TILE = 16
VMEM_LIMIT = 12 * 1024 * 1024

IN_VMEM = pl.BlockSpec(memory_space=pltpu.VMEM)
ANYWHERE = pl.BlockSpec(memory_space=pl.ANY)


def call(kernel, out_shape, in_specs, out_specs, name, flops=0, moved=0, scratch_shapes=()):
    return pl.pallas_call(
        kernel,
        out_shape=out_shape,
        in_specs=in_specs,
        out_specs=out_specs,
        scratch_shapes=scratch_shapes,
        name=name,
        cost_estimate=pl.CostEstimate(flops=flops, bytes_accessed=moved, transcendentals=0),
        compiler_params=pltpu.CompilerParams(vmem_limit_bytes=VMEM_LIMIT),
    )


def in_hbm(array):
    return pltpu.with_memory_space_constraint(array, pltpu.HBM)


def shift(array, axis, size, step):
    return lax.ppermute(array, axis, [(i, (i + step) % size) for i in range(size)])


def to_neighbour(array, patches):
    return lax.ppermute(array, "patch", [(i, i ^ 1) for i in range(patches)])


def to_neighbours_other_core(array, patches, subs):
    pairs = [
        (place * subs + sub, (place ^ 1) * subs + (subs - 1 - sub))
        for place in range(patches)
        for sub in range(subs)
    ]
    return lax.ppermute(array, ("patch", "sub"), pairs)


def start_all(copies):
    for copy in copies:
        copy.start()
    return copies


def prepare_kernel(
    keys_hbm, values_hbm, queries_hbm, same_ref, flip_ref, q_same_ref, q_flip_ref, buffers, sems
):
    parity = lax.rem(lax.axis_index("patch"), 2)
    head_cols = [
        pl.ds(pl.multiple_of(head * HD, LANES), HD) for head in (1 - parity, parity)
    ]
    copies = start_all(
        [
            pltpu.make_async_copy(source.at[:, cols], buffers.at[2 * i + n], sems.at[2 * i + n])
            for i, cols in enumerate(head_cols)
            for n, source in enumerate((keys_hbm, values_hbm))
        ]
        + [
            pltpu.make_async_copy(queries_hbm.at[:, cols], ref, sems.at[4 + i])
            for i, (cols, ref) in enumerate(zip(head_cols, (q_flip_ref, q_same_ref)))
        ]
    )
    for i, ref in enumerate((flip_ref, same_ref)):
        for n in range(2):
            copies[2 * i + n].wait()
            ref[:, n * HD : (n + 1) * HD] = buffers[2 * i + n].astype(jnp.bfloat16)
    for copy in copies[4:]:
        copy.wait()


def stage_kernel(steps, patches, held_k_hbm, held_v_hbm, keys_ref, values_ref, sems):
    rows = keys_ref.shape[0] // patches
    place = lax.axis_index("patch")
    cols = pl.ds(pl.multiple_of(lax.rem(place, 2) * HD, LANES), HD)
    copies = []
    for i, step in enumerate(steps):
        at = pl.ds(pl.multiple_of(lax.rem(place + patches - step, patches) * rows, rows), rows)
        for n, (held, ref) in enumerate(((held_k_hbm, keys_ref), (held_v_hbm, values_ref))):
            copies.append(
                pltpu.make_async_copy(
                    held.at[at, cols], ref.at[i * rows : (i + 1) * rows, :], sems.at[2 * i + n]
                )
            )
    for copy in start_all(copies):
        copy.wait()


def attention_kernel(scale, q_own_ref, q_other_ref, keys_ref, values_ref, *refs):
    block_refs, out_refs = refs[:-2], refs[-2:]
    rows = q_own_ref.shape[0]
    blocks = jnp.concatenate([ref[...] for ref in block_refs], axis=0)
    q = jnp.concatenate([q_own_ref[...], q_other_ref[...]], axis=0)
    products = lax.dot_general(
        jnp.concatenate([q, q], axis=1),
        jnp.concatenate([keys_ref[...], blocks[:, :HD]], axis=1),
        (((1,), (1,)), ((), ())),
        preferred_element_type=jnp.float32,
    )
    scores = products * scale
    weights = jnp.exp(scores - jnp.max(scores, axis=1, keepdims=True))
    totals = jnp.sum(weights, axis=1, keepdims=True)
    high = weights.astype(jnp.bfloat16)
    low = (weights - high.astype(jnp.float32)).astype(jnp.bfloat16)
    sums = jnp.dot(
        jnp.concatenate([high, low], axis=0),
        jnp.concatenate([values_ref[...], blocks[:, HD:]], axis=1),
        preferred_element_type=jnp.float32,
    )
    sums = sums[: 2 * rows] + sums[2 * rows :]
    sums = sums[:, :HD] + sums[:, HD:]
    attended = (sums / totals).astype(jnp.bfloat16)
    for n, ref in enumerate(out_refs):
        ref[...] = attended[n * rows : (n + 1) * rows, :]


def block_products(start, columns, refs):
    even = lax.rem(lax.axis_index("patch"), 2) == 0
    total = 0.0
    for same_ref, flip_ref, weight_ref in zip(refs[::3], refs[1::3], refs[2::3]):
        same, flip = same_ref[...], flip_ref[...]
        attended = jnp.concatenate(
            [jnp.where(even, same, flip), jnp.where(even, flip, same)], axis=1
        )
        if start is None:
            weight = weight_ref[...]
        else:
            weight = weight_ref[:, pl.ds(pl.multiple_of(start, LANES), columns)]
        total = total + jnp.dot(attended, weight, preferred_element_type=jnp.float32)
    return total


def sent_kernel(start, *refs):
    out_ref = refs[-1]
    out_ref[...] = block_products(start(), out_ref.shape[1], refs[:-1]).astype(jnp.bfloat16)


def base_kernel(start, hidden_ref, gate_ref, *refs):
    out_ref = refs[-1]
    total = block_products(start(), out_ref.shape[1], refs[:-1])
    out_ref[...] = hidden_ref[...].astype(jnp.float32) + gate_ref[...] * total


def final_kernel(base_ref, gate_ref, *refs):
    arrived_refs, out_ref = refs[:-1], refs[-1]
    total = 0.0
    for ref in arrived_refs:
        total = total + ref[...].astype(jnp.float32)
    out_ref[...] = (base_ref[...] + gate_ref[...] * total).astype(jnp.bfloat16)


def solution(mesh):
    patches, heads, subs = mesh.shape["patch"], mesh.shape["head"], mesh.shape["sub"]

    def per_device(
        queries, held_keys, held_values, key_change, value_change, out_weight, hidden_in, gate
    ):
        rows, width = queries.shape
        columns = hidden_in.shape[1]
        tokens = rows * patches
        assert width == 2 * HD and patches % 2 == 0 and subs == 2

        def rows_of(count, kind=jnp.bfloat16):
            return jax.ShapeDtypeStruct((rows, count), kind)

        with jax.named_scope("residual_exchange"):
            same, flip, q_same, q_flip = call(
                prepare_kernel,
                [rows_of(2 * HD), rows_of(2 * HD), rows_of(HD), rows_of(HD)],
                [ANYWHERE] * 3,
                [IN_VMEM] * 4,
                "prepare",
                scratch_shapes=[
                    pltpu.VMEM((4, rows, HD), jnp.float32),
                    pltpu.SemaphoreType.DMA((6,)),
                ],
            )(in_hbm(key_change), in_hbm(value_change), in_hbm(queries))
            steps = [0] + list(range(patches - 1, 0, -1))
            blocks = [same] + [
                shift(same if step % 2 == 0 else flip, "patch", patches, step)
                for step in steps[1:]
            ]
            q_other = to_neighbour(q_flip, patches)

        with jax.named_scope("weight_swap"):
            swapped, _ = lax.optimization_barrier((out_weight, same))
            weights = [out_weight, shift(swapped, "sub", subs, 1)]

        with jax.named_scope("attention"):
            keys, values = call(
                functools.partial(stage_kernel, steps, patches),
                [jax.ShapeDtypeStruct((tokens, HD), jnp.bfloat16)] * 2,
                [ANYWHERE] * 2,
                [IN_VMEM] * 2,
                "stage",
                flops=2_000_000_000,
                scratch_shapes=[pltpu.SemaphoreType.DMA((2 * patches,))],
            )(in_hbm(held_keys), in_hbm(held_values))
            own_same, other_same = call(
                functools.partial(attention_kernel, 1.0 / math.sqrt(HD)),
                [rows_of(HD)] * 2,
                [IN_VMEM] * (4 + patches),
                [IN_VMEM] * 2,
                "attention",
                flops=2_000_000_000,
            )(q_same, q_other, keys, values, *blocks)

        with jax.named_scope("attended_exchange"):
            attended = [
                (own_same, to_neighbour(other_same, patches)),
                (
                    shift(own_same, "sub", subs, 1),
                    to_neighbours_other_core(other_same, patches, subs),
                ),
            ]

        def operands_and_start(step):
            def start():
                to = lax.rem(lax.axis_index("head") + step, heads) * subs + lax.axis_index("sub")
                return to * columns

            def block(weight):
                if columns % LANES == 0:
                    return weight
                return lax.dynamic_slice(weight, (0, start()), (width, columns))

            operands = [
                x for pair, weight in zip(attended, weights) for x in (*pair, block(weight))
            ]
            return operands, start if columns % LANES == 0 else lambda: None

        product_flops = 4 * rows * width * columns
        with jax.named_scope("projection"):
            arrived = []
            for step in range(1, heads):
                operands, start = operands_and_start(step)
                term = call(
                    functools.partial(sent_kernel, start),
                    rows_of(columns),
                    [IN_VMEM] * len(operands),
                    IN_VMEM,
                    "sent_term",
                    product_flops,
                )(*operands)
                arrived.append(shift(term, "head", heads, step))
            gate_row = gate.reshape(1, columns)
            operands, start = operands_and_start(0)
            base = call(
                functools.partial(base_kernel, start),
                rows_of(columns, jnp.float32),
                [IN_VMEM] * (2 + len(operands)),
                IN_VMEM,
                "base",
                product_flops,
            )(hidden_in, gate_row, *operands)
            return call(
                final_kernel,
                rows_of(columns),
                [IN_VMEM] * (2 + len(arrived)),
                IN_VMEM,
                "final",
                moved=rows * columns * 8,
            )(base, gate_row, *arrived)

    in_specs = (
        P(("groups", "patch"), ("head", "sub")),
        P("groups", ("head", "sub")),
        P("groups", ("head", "sub")),
        P(("groups", "patch"), ("head", "sub")),
        P(("groups", "patch"), ("head", "sub")),
        P(("head", "sub"), None),
        P(("groups", "patch"), ("head", "sub")),
        P(("groups", "head", "sub")),
    )
    out_specs = P(("groups", "patch"), ("head", "sub"))
    return jax.shard_map(
        per_device, mesh=mesh, in_specs=in_specs, out_specs=out_specs, check_vma=False
    )
```

```python
import functools
import math

import jax
import jax.numpy as jnp
from jax import lax
from jax.experimental import pallas as pl
from jax.experimental.pallas import tpu as pltpu
from jax.sharding import PartitionSpec as P

HD = 128
LANES = 128
ROW_TILE = 16
VMEM_LIMIT = 12 * 1024 * 1024
EARLY = 256

IN_VMEM = pl.BlockSpec(memory_space=pltpu.VMEM)
ANYWHERE = pl.BlockSpec(memory_space=pl.ANY)


def call(
    kernel,
    out_shape,
    in_specs,
    out_specs,
    name,
    flops=0,
    moved=0,
    scratch_shapes=(),
    vmem=VMEM_LIMIT,
):
    return pl.pallas_call(
        kernel,
        out_shape=out_shape,
        in_specs=in_specs,
        out_specs=out_specs,
        scratch_shapes=scratch_shapes,
        name=name,
        cost_estimate=pl.CostEstimate(flops=flops, bytes_accessed=moved, transcendentals=0),
        compiler_params=pltpu.CompilerParams(vmem_limit_bytes=vmem),
    )


def in_hbm(array):
    return pltpu.with_memory_space_constraint(array, pltpu.HBM)


def shift(array, axis, size, step):
    return lax.ppermute(array, axis, [(i, (i + step) % size) for i in range(size)])


FIRST = ((0, 2), (2, 3), (3, 1), (1, 0))
SECOND = ((0, 1), (1, 3), (3, 2), (2, 0))
MIDDLE = ((1, 2), (2, 1), (0, 0), (3, 3))
PASSED = ((0, 1), (1, 0), (2, 3), (3, 2))


def gather(own, patches):
    if patches != 4:
        return [own] + [shift(own, "patch", patches, step) for step in range(patches - 1, 0, -1)]
    first = lax.ppermute(own, "patch", FIRST)
    second = lax.ppermute(own, "patch", SECOND)
    middle = lax.ppermute(own, "patch", MIDDLE)
    passed = lax.ppermute(first, "patch", PASSED)
    return [own, middle, second, first, passed]


def gathered(refs):
    blocks = [ref[...] for ref in refs]
    if len(blocks) != 5:
        return blocks
    place = lax.axis_index("patch")
    inner = jnp.logical_and(place > 0, place < 3)
    own, middle, second, first, passed = blocks
    return [own, first, second, jnp.where(inner, middle, passed)]


def by_place(place, entries):
    value = jnp.int32(entries[0])
    for i, entry in enumerate(entries[1:], 1):
        value = jnp.where(place == i, jnp.int32(entry), value)
    return value


def gather_sources(patches, place):
    if patches != 4:
        return [place] + [
            lax.rem(place + patches - step, patches) for step in range(patches - 1, 0, -1)
        ]
    return [place] + [
        by_place(place, entries) for entries in ((1, 3, 0, 2), (2, 0, 3, 1), (3, 2, 1, 0))
    ]


def early_weight_kernel(subs, columns, early, weight_ref, out_ref, sems):
    chip = (1 - lax.axis_index("head")) * subs
    copies = []
    for sub in range(subs):
        at = pl.multiple_of((chip + sub) * columns, LANES)
        copies.append(
            pltpu.make_async_copy(
                weight_ref.at[:, pl.ds(at, early)],
                out_ref.at[:, pl.ds(sub * early, early)],
                sems.at[sub],
            )
        )
    for copy in copies:
        copy.start()
    for copy in copies:
        copy.wait()


def stage_kernel(
    patches, q_hbm, held_k_hbm, held_v_hbm, q_ref, products_ref, values_ref, keys_ref, sems
):
    rows, width = q_ref.shape
    sources = gather_sources(patches, lax.axis_index("patch"))
    copies = [pltpu.make_async_copy(q_hbm, q_ref, sems.at[0])]
    for i, source in enumerate(sources):
        at = pl.multiple_of(source * rows, rows)
        for n, (held, ref) in enumerate(((held_k_hbm, keys_ref), (held_v_hbm, values_ref))):
            copies.append(
                pltpu.make_async_copy(
                    held.at[pl.ds(at, rows), :],
                    ref.at[i * rows : (i + 1) * rows, :],
                    sems.at[1 + 2 * i + n],
                )
            )
    for copy in copies:
        copy.start()
    for copy in copies:
        copy.wait()
    for head in range(width // HD):
        cols = slice(head * HD, (head + 1) * HD)
        products_ref[head] = dot_transposed(q_ref[:, cols], keys_ref[:, cols])


def dot_transposed(a, b):
    return lax.dot_general(
        a, b, (((1,), (1,)), ((), ())), preferred_element_type=jnp.float32
    )


def attention_kernel(scale, q_ref, products_ref, values_ref, *refs):
    block_refs, out_ref = refs[:-1], refs[-1]
    rows, width = q_ref.shape
    blocks = jnp.concatenate(gathered(block_refs), axis=0)
    for head in range(width // HD):
        cols = slice(head * HD, (head + 1) * HD)
        value_cols = slice(width + head * HD, width + (head + 1) * HD)
        products = products_ref[head] + dot_transposed(q_ref[:, cols], blocks[:, cols])
        scores = products * scale
        weights = jnp.exp(scores - jnp.max(scores, axis=1, keepdims=True))
        totals = jnp.sum(weights, axis=1, keepdims=True)
        high = weights.astype(jnp.bfloat16)
        low = (weights - high.astype(jnp.float32)).astype(jnp.bfloat16)
        sums = jnp.dot(
            jnp.concatenate([high, low], axis=0),
            jnp.concatenate([values_ref[:, cols], blocks[:, value_cols]], axis=1),
            preferred_element_type=jnp.float32,
        )
        sums = sums[:rows] + sums[rows:]
        sums = sums[:, :HD] + sums[:, HD:]
        out_ref[:, cols] = (sums / totals).astype(jnp.bfloat16)


def block_dot(a_ref, weight_ref, start, columns):
    if start is None:
        weight = weight_ref[...]
    else:
        weight = weight_ref[:, pl.ds(pl.multiple_of(start, LANES), columns)]
    return jnp.dot(a_ref[...], weight, preferred_element_type=jnp.float32)


def products(start, columns, refs):
    total = 0.0
    for attended_ref, weight_ref in zip(refs[::2], refs[1::2]):
        total = total + block_dot(attended_ref, weight_ref, start, columns)
    return total


def sent_term_kernel(start, *refs):
    out_ref = refs[-1]
    total = products(start(), out_ref.shape[1], refs[:-1])
    out_ref[...] = total.astype(jnp.bfloat16)


def base_kernel(start, hidden_ref, gate_ref, *refs):
    out_ref = refs[-1]
    total = products(start(), out_ref.shape[1], refs[:-1])
    out_ref[...] = hidden_ref[...].astype(jnp.float32) + gate_ref[...] * total


def final_kernel(early, blocks, base_ref, gate_ref, *refs):
    arrived_refs, (out_ref, result, sems) = refs[:-3], refs[-3:]
    rows = base_ref.shape[0] // blocks
    copies = []
    for n in range(blocks):
        at = slice(n * rows, (n + 1) * rows)
        total = 0.0
        for ref in arrived_refs:
            total = total + ref[at, :].astype(jnp.float32)
        if early:
            result[at, :early] = base_ref[at, :early].astype(jnp.bfloat16)
        total = base_ref[at, early:] + gate_ref[:, early:] * total
        result[at, early:] = total.astype(jnp.bfloat16)
        copies.append(pltpu.make_async_copy(result.at[at, :], out_ref.at[at, :], sems.at[n]))
        copies[n].start()
    for copy in copies:
        copy.wait()


def pack_kernel(early, attended_ref, weight_ref, out_ref):
    rows, width = attended_ref.shape
    for i in range(width // early):
        out_ref[i * rows : (i + 1) * rows, :] = attended_ref[:, i * early : (i + 1) * early]
    other = pl.multiple_of((1 - lax.axis_index("sub")) * early, LANES)
    out_ref[rows * (width // early) :, :] = weight_ref[:, pl.ds(other, early)]


def early_kernel(early, base_ref, gate_ref, attended_ref, weight_ref, packed_ref, out_ref):
    rows, width = attended_ref.shape
    pieces = width // early
    mine = pl.multiple_of(lax.axis_index("sub") * early, LANES)
    total = jnp.dot(
        attended_ref[...],
        weight_ref[:, pl.ds(mine, early)],
        preferred_element_type=jnp.float32,
    ) + jnp.dot(
        jnp.concatenate(
            [packed_ref[i * rows : (i + 1) * rows, :] for i in range(pieces)], axis=1
        ),
        packed_ref[pieces * rows :, :],
        preferred_element_type=jnp.float32,
    )
    out_ref[...] = base_ref[...]
    out_ref[:, :early] = base_ref[:, :early] + gate_ref[:, :early] * total


def solution(mesh):
    patches, heads, subs = mesh.shape["patch"], mesh.shape["head"], mesh.shape["sub"]

    def per_device(
        queries, held_keys, held_values, key_change, value_change, out_weight, hidden_in, gate
    ):
        rows, width = queries.shape
        columns = hidden_in.shape[1]

        early = EARLY if heads == 2 and columns % LANES == 0 and columns > 4 * LANES else 0
        with jax.named_scope("residual_gather"):
            low = jnp.float32(-jnp.inf)
            residual = jnp.maximum(
                lax.pad(key_change, low, ((0, 0, 0), (0, width, 0))),
                lax.pad(value_change, low, ((0, 0, 0), (width, 0, 0))),
            ).astype(jnp.bfloat16)
            blocks = gather(residual, patches)

        with jax.named_scope("weight_swap"):
            swapped, _ = lax.optimization_barrier((out_weight, residual))
            weights = [out_weight] + [shift(swapped, "sub", subs, i) for i in range(1, subs)]

        if early:
            with jax.named_scope("early_weight"):
                early_weight = call(
                    functools.partial(early_weight_kernel, subs, columns, early),
                    jax.ShapeDtypeStruct((width, subs * early), jnp.bfloat16),
                    [ANYWHERE],
                    IN_VMEM,
                    "early_weight",
                    moved=4 * width * subs * early,
                    scratch_shapes=[pltpu.SemaphoreType.DMA((subs,))],
                )(in_hbm(out_weight))
                early_weight = shift(early_weight, "head", heads, 1)

        def weight_and_start(i, step, skip=0):
            def start():
                to = lax.rem(lax.axis_index("head") + step, heads) * subs + lax.axis_index("sub")
                return to * columns + skip

            if columns % LANES == 0:
                return weights[i], start
            return lax.dynamic_slice(weights[i], (0, start()), (width, columns)), lambda: None

        def pairs_and_start(step, skip=0):
            pairs = [
                x
                for i in range(subs)
                for x in (attended_parts[i], weight_and_start(i, step, skip)[0])
            ]
            return pairs, weight_and_start(0, step, skip)[1]

        tokens = rows * patches
        with jax.named_scope("attention"):
            staged_queries, products, values = call(
                functools.partial(stage_kernel, patches),
                [
                    jax.ShapeDtypeStruct((rows, width), jnp.bfloat16),
                    jax.ShapeDtypeStruct((width // HD, rows, tokens), jnp.float32),
                    jax.ShapeDtypeStruct((tokens, width), jnp.bfloat16),
                ],
                [ANYWHERE] * 3,
                [IN_VMEM] * 3,
                "stage",
                flops=2_000_000_000,
                scratch_shapes=[
                    pltpu.VMEM((tokens, width), jnp.bfloat16),
                    pltpu.SemaphoreType.DMA((1 + 2 * patches,)),
                ],
            )(in_hbm(queries), in_hbm(held_keys), in_hbm(held_values))
            attended = call(
                functools.partial(attention_kernel, 1.0 / math.sqrt(HD)),
                jax.ShapeDtypeStruct((rows, width), jnp.bfloat16),
                [IN_VMEM] * (3 + len(blocks)),
                IN_VMEM,
                "attention",
                flops=2_000_000_000,
            )(staged_queries, products, values, *blocks)

        with jax.named_scope("attended_swap"):
            attended_parts = [attended] + [
                shift(attended, "sub", subs, i) for i in range(1, subs)
            ]
            if early:
                other_attended = shift(attended, "head", heads, 1)

        term = jax.ShapeDtypeStruct((rows, columns), jnp.float32)
        sent = jax.ShapeDtypeStruct((rows, columns - early), jnp.bfloat16)
        product_flops = 2 * rows * width * columns
        with jax.named_scope("projection"):
            arrived = []
            for step in range(1, heads):
                pairs, start = pairs_and_start(step, early)
                total = call(
                    functools.partial(sent_term_kernel, start),
                    sent,
                    [IN_VMEM] * len(pairs),
                    IN_VMEM,
                    "sent_term",
                    2 * product_flops,
                )(*pairs)
                arrived.append(shift(total, "head", heads, step))
            gate_row = gate.reshape(1, columns)
            pairs, start = pairs_and_start(0)
            base = call(
                functools.partial(base_kernel, start),
                term,
                [IN_VMEM] * (2 + len(pairs)),
                IN_VMEM,
                "base",
                2 * product_flops,
            )(hidden_in, gate_row, *pairs)
            if early:
                packed = call(
                    functools.partial(pack_kernel, early),
                    jax.ShapeDtypeStruct((rows * (width // early) + width, early), jnp.bfloat16),
                    [IN_VMEM] * 2,
                    IN_VMEM,
                    "pack",
                )(other_attended, early_weight)
                packed = shift(packed, "sub", subs, 1)
                base = call(
                    functools.partial(early_kernel, early),
                    term,
                    [IN_VMEM] * 5,
                    IN_VMEM,
                    "early",
                    product_flops // 2,
                )(base, gate_row, other_attended, early_weight, packed)
            row_blocks = 3 if rows % (3 * ROW_TILE) == 0 else 1
            return call(
                functools.partial(final_kernel, early, row_blocks),
                jax.ShapeDtypeStruct((rows, columns), jnp.bfloat16),
                [IN_VMEM] * (2 + len(arrived)),
                ANYWHERE,
                "final",
                moved=rows * columns * 8,
                scratch_shapes=[
                    pltpu.VMEM((rows, columns), jnp.bfloat16),
                    pltpu.SemaphoreType.DMA((row_blocks,)),
                ],
            )(base, gate_row, *arrived)

    in_specs = (
        P(("groups", "patch"), ("head", "sub")),
        P("groups", ("head", "sub")),
        P("groups", ("head", "sub")),
        P(("groups", "patch"), ("head", "sub")),
        P(("groups", "patch"), ("head", "sub")),
        P(("head", "sub"), None),
        P(("groups", "patch"), ("head", "sub")),
        P(("groups", "head", "sub")),
    )
    out_specs = P(("groups", "patch"), ("head", "sub"))
    return jax.shard_map(
        per_device, mesh=mesh, in_specs=in_specs, out_specs=out_specs, check_vma=False
    )
```

```python
import functools
import math

import jax
import jax.numpy as jnp
from jax import lax
from jax.experimental import pallas as pl
from jax.experimental.pallas import tpu as pltpu
from jax.sharding import PartitionSpec as P

HD = 128
LANES = 128
ROW_TILE = 16
VMEM_LIMIT = 12 * 1024 * 1024
EARLY = 256

IN_VMEM = pl.BlockSpec(memory_space=pltpu.VMEM)
ANYWHERE = pl.BlockSpec(memory_space=pl.ANY)


def call(
    kernel,
    out_shape,
    in_specs,
    out_specs,
    name,
    flops=0,
    moved=0,
    scratch_shapes=(),
    vmem=VMEM_LIMIT,
):
    return pl.pallas_call(
        kernel,
        out_shape=out_shape,
        in_specs=in_specs,
        out_specs=out_specs,
        scratch_shapes=scratch_shapes,
        name=name,
        cost_estimate=pl.CostEstimate(flops=flops, bytes_accessed=moved, transcendentals=0),
        compiler_params=pltpu.CompilerParams(vmem_limit_bytes=vmem),
    )


def in_hbm(array):
    return pltpu.with_memory_space_constraint(array, pltpu.HBM)


def shift(array, axis, size, step):
    return lax.ppermute(array, axis, [(i, (i + step) % size) for i in range(size)])


def gather_steps(patches):
    return list(range(patches - 1, 0, -1))


def gather_sources(patches, place):
    return [place] + [lax.rem(place + patches - step, patches) for step in gather_steps(patches)]


def early_weight_kernel(subs, columns, early, weight_ref, out_ref, sems):
    chip = (1 - lax.axis_index("head")) * subs
    copies = []
    for sub in range(subs):
        at = pl.multiple_of((chip + sub) * columns, LANES)
        copies.append(
            pltpu.make_async_copy(
                weight_ref.at[:, pl.ds(at, early)],
                out_ref.at[:, pl.ds(sub * early, early)],
                sems.at[sub],
            )
        )
    for copy in copies:
        copy.start()
    for copy in copies:
        copy.wait()


def stage_kernel(
    patches, q_hbm, held_k_hbm, held_v_hbm, q_ref, products_ref, values_ref, keys_ref, sems
):
    rows, width = q_ref.shape
    sources = gather_sources(patches, lax.axis_index("patch"))
    copies = [pltpu.make_async_copy(q_hbm, q_ref, sems.at[0])]
    for i, source in enumerate(sources):
        at = pl.multiple_of(source * rows, rows)
        for n, (held, ref) in enumerate(((held_k_hbm, keys_ref), (held_v_hbm, values_ref))):
            copies.append(
                pltpu.make_async_copy(
                    held.at[pl.ds(at, rows), :],
                    ref.at[i * rows : (i + 1) * rows, :],
                    sems.at[1 + 2 * i + n],
                )
            )
    for copy in copies:
        copy.start()
    for copy in copies:
        copy.wait()
    for head in range(width // HD):
        cols = slice(head * HD, (head + 1) * HD)
        products_ref[head] = dot_transposed(q_ref[:, cols], keys_ref[:, cols])


def dot_transposed(a, b):
    return lax.dot_general(
        a, b, (((1,), (1,)), ((), ())), preferred_element_type=jnp.float32
    )


def attention_kernel(scale, q_ref, products_ref, values_ref, *refs):
    block_refs, out_ref = refs[:-1], refs[-1]
    rows, width = q_ref.shape
    blocks = jnp.concatenate([ref[...] for ref in block_refs], axis=0)
    for head in range(width // HD):
        cols = slice(head * HD, (head + 1) * HD)
        value_cols = slice(width + head * HD, width + (head + 1) * HD)
        products = products_ref[head] + dot_transposed(q_ref[:, cols], blocks[:, cols])
        scores = products * scale
        weights = jnp.exp(scores - jnp.max(scores, axis=1, keepdims=True))
        totals = jnp.sum(weights, axis=1, keepdims=True)
        high = weights.astype(jnp.bfloat16)
        low = (weights - high.astype(jnp.float32)).astype(jnp.bfloat16)
        sums = jnp.dot(
            jnp.concatenate([high, low], axis=0),
            jnp.concatenate([values_ref[:, cols], blocks[:, value_cols]], axis=1),
            preferred_element_type=jnp.float32,
        )
        sums = sums[:rows] + sums[rows:]
        sums = sums[:, :HD] + sums[:, HD:]
        out_ref[:, cols] = (sums / totals).astype(jnp.bfloat16)


def block_dot(a_ref, weight_ref, start, columns):
    if start is None:
        weight = weight_ref[...]
    else:
        weight = weight_ref[:, pl.ds(pl.multiple_of(start, LANES), columns)]
    return jnp.dot(a_ref[...], weight, preferred_element_type=jnp.float32)


def products(start, columns, refs):
    total = 0.0
    for attended_ref, weight_ref in zip(refs[::2], refs[1::2]):
        total = total + block_dot(attended_ref, weight_ref, start, columns)
    return total


def sent_term_kernel(start, *refs):
    out_ref = refs[-1]
    total = products(start(), out_ref.shape[1], refs[:-1])
    out_ref[...] = total.astype(jnp.bfloat16)


def base_kernel(start, hidden_ref, gate_ref, *refs):
    out_ref = refs[-1]
    total = products(start(), out_ref.shape[1], refs[:-1])
    out_ref[...] = hidden_ref[...].astype(jnp.float32) + gate_ref[...] * total


def final_kernel(early, blocks, base_ref, gate_ref, *refs):
    arrived_refs, (out_ref, result, sems) = refs[:-3], refs[-3:]
    rows = base_ref.shape[0] // blocks
    copies = []
    for n in range(blocks):
        at = slice(n * rows, (n + 1) * rows)
        total = 0.0
        for ref in arrived_refs:
            total = total + ref[at, :].astype(jnp.float32)
        if early:
            result[at, :early] = base_ref[at, :early].astype(jnp.bfloat16)
        total = base_ref[at, early:] + gate_ref[:, early:] * total
        result[at, early:] = total.astype(jnp.bfloat16)
        copies.append(pltpu.make_async_copy(result.at[at, :], out_ref.at[at, :], sems.at[n]))
        copies[n].start()
    for copy in copies:
        copy.wait()


def pack_kernel(early, attended_ref, weight_ref, out_ref):
    rows, width = attended_ref.shape
    other = pl.multiple_of((1 - lax.axis_index("sub")) * early, LANES)
    out_ref[:rows, :width] = attended_ref[...]
    out_ref[rows:, :early] = weight_ref[:, pl.ds(other, early)]


def early_kernel(early, base_ref, gate_ref, attended_ref, weight_ref, packed_ref, out_ref):
    rows, width = attended_ref.shape
    mine = pl.multiple_of(lax.axis_index("sub") * early, LANES)
    total = jnp.dot(
        attended_ref[...],
        weight_ref[:, pl.ds(mine, early)],
        preferred_element_type=jnp.float32,
    ) + jnp.dot(
        packed_ref[:rows, :width], packed_ref[rows:, :early], preferred_element_type=jnp.float32
    )
    out_ref[...] = base_ref[...]
    out_ref[:, :early] = base_ref[:, :early] + gate_ref[:, :early] * total


def solution(mesh):
    patches, heads, subs = mesh.shape["patch"], mesh.shape["head"], mesh.shape["sub"]

    def per_device(
        queries, held_keys, held_values, key_change, value_change, out_weight, hidden_in, gate
    ):
        rows, width = queries.shape
        columns = hidden_in.shape[1]

        early = EARLY if heads == 2 and columns % LANES == 0 and columns > 4 * LANES else 0
        if early:
            with jax.named_scope("early_weight"):
                early_weight = call(
                    functools.partial(early_weight_kernel, subs, columns, early),
                    jax.ShapeDtypeStruct((width, subs * early), jnp.bfloat16),
                    [ANYWHERE],
                    IN_VMEM,
                    "early_weight",
                    moved=4 * width * subs * early,
                    scratch_shapes=[pltpu.SemaphoreType.DMA((subs,))],
                )(in_hbm(out_weight))
                key_change, value_change, early_weight = lax.optimization_barrier(
                    (key_change, value_change, early_weight)
                )

        with jax.named_scope("residual_gather"):
            low = jnp.float32(-jnp.inf)
            residual = jnp.maximum(
                lax.pad(key_change, low, ((0, 0, 0), (0, width, 0))),
                lax.pad(value_change, low, ((0, 0, 0), (width, 0, 0))),
            ).astype(jnp.bfloat16)
            blocks = [residual] + [
                shift(residual, "patch", patches, step) for step in gather_steps(patches)
            ]

        with jax.named_scope("weight_swap"):
            weights = [out_weight] + [shift(out_weight, "sub", subs, i) for i in range(1, subs)]

        if early:
            with jax.named_scope("early_weight"):
                early_weight = shift(early_weight, "head", heads, 1)

        def weight_and_start(i, step, skip=0):
            def start():
                to = lax.rem(lax.axis_index("head") + step, heads) * subs + lax.axis_index("sub")
                return to * columns + skip

            if columns % LANES == 0:
                return weights[i], start
            return lax.dynamic_slice(weights[i], (0, start()), (width, columns)), lambda: None

        def pairs_and_start(step, skip=0):
            pairs = [
                x
                for i in range(subs)
                for x in (attended_parts[i], weight_and_start(i, step, skip)[0])
            ]
            return pairs, weight_and_start(0, step, skip)[1]

        tokens = rows * patches
        with jax.named_scope("attention"):
            staged_queries, products, values = call(
                functools.partial(stage_kernel, patches),
                [
                    jax.ShapeDtypeStruct((rows, width), jnp.bfloat16),
                    jax.ShapeDtypeStruct((width // HD, rows, tokens), jnp.float32),
                    jax.ShapeDtypeStruct((tokens, width), jnp.bfloat16),
                ],
                [ANYWHERE] * 3,
                [IN_VMEM] * 3,
                "stage",
                flops=2_000_000_000,
                scratch_shapes=[
                    pltpu.VMEM((tokens, width), jnp.bfloat16),
                    pltpu.SemaphoreType.DMA((1 + 2 * patches,)),
                ],
            )(in_hbm(queries), in_hbm(held_keys), in_hbm(held_values))
            attended = call(
                functools.partial(attention_kernel, 1.0 / math.sqrt(HD)),
                jax.ShapeDtypeStruct((rows, width), jnp.bfloat16),
                [IN_VMEM] * (3 + len(blocks)),
                IN_VMEM,
                "attention",
                flops=2_000_000_000,
            )(staged_queries, products, values, *blocks)

        with jax.named_scope("attended_swap"):
            attended_parts = [attended] + [
                shift(attended, "sub", subs, i) for i in range(1, subs)
            ]
            if early:
                other_attended = shift(attended, "head", heads, 1)

        term = jax.ShapeDtypeStruct((rows, columns), jnp.float32)
        sent = jax.ShapeDtypeStruct((rows, columns - early), jnp.bfloat16)
        product_flops = 2 * rows * width * columns
        with jax.named_scope("projection"):
            arrived = []
            for step in range(1, heads):
                pairs, start = pairs_and_start(step, early)
                total = call(
                    functools.partial(sent_term_kernel, start),
                    sent,
                    [IN_VMEM] * len(pairs),
                    IN_VMEM,
                    "sent_term",
                    2 * product_flops,
                )(*pairs)
                arrived.append(shift(total, "head", heads, step))
            gate_row = gate.reshape(1, columns)
            pairs, start = pairs_and_start(0)
            base = call(
                functools.partial(base_kernel, start),
                term,
                [IN_VMEM] * (2 + len(pairs)),
                IN_VMEM,
                "base",
                2 * product_flops,
            )(hidden_in, gate_row, *pairs)
            if early:
                packed = call(
                    functools.partial(pack_kernel, early),
                    jax.ShapeDtypeStruct((rows + width, max(early, width)), jnp.bfloat16),
                    [IN_VMEM] * 2,
                    IN_VMEM,
                    "pack",
                )(other_attended, early_weight)
                packed = shift(packed, "sub", subs, 1)
                base = call(
                    functools.partial(early_kernel, early),
                    term,
                    [IN_VMEM] * 5,
                    IN_VMEM,
                    "early",
                    product_flops // 2,
                )(base, gate_row, other_attended, early_weight, packed)
            row_blocks = 3 if rows % (3 * ROW_TILE) == 0 else 1
            return call(
                functools.partial(final_kernel, early, row_blocks),
                jax.ShapeDtypeStruct((rows, columns), jnp.bfloat16),
                [IN_VMEM] * (2 + len(arrived)),
                ANYWHERE,
                "final",
                moved=rows * columns * 8,
                scratch_shapes=[
                    pltpu.VMEM((rows, columns), jnp.bfloat16),
                    pltpu.SemaphoreType.DMA((row_blocks,)),
                ],
            )(base, gate_row, *arrived)

    in_specs = (
        P(("groups", "patch"), ("head", "sub")),
        P("groups", ("head", "sub")),
        P("groups", ("head", "sub")),
        P(("groups", "patch"), ("head", "sub")),
        P(("groups", "patch"), ("head", "sub")),
        P(("head", "sub"), None),
        P(("groups", "patch"), ("head", "sub")),
        P(("groups", "head", "sub")),
    )
    out_specs = P(("groups", "patch"), ("head", "sub"))
    return jax.shard_map(
        per_device, mesh=mesh, in_specs=in_specs, out_specs=out_specs, check_vma=False
    )
```

```python
import functools
import math

import jax
import jax.numpy as jnp
from jax import lax
from jax.experimental import pallas as pl
from jax.experimental.pallas import tpu as pltpu
from jax.sharding import PartitionSpec as P

HD = 128
LANES = 128
ROW_TILE = 16
VMEM_LIMIT = 12 * 1024 * 1024
EARLY = 256

IN_VMEM = pl.BlockSpec(memory_space=pltpu.VMEM)
ANYWHERE = pl.BlockSpec(memory_space=pl.ANY)


def call(
    kernel,
    out_shape,
    in_specs,
    out_specs,
    name,
    flops=0,
    moved=0,
    scratch_shapes=(),
    vmem=VMEM_LIMIT,
):
    return pl.pallas_call(
        kernel,
        out_shape=out_shape,
        in_specs=in_specs,
        out_specs=out_specs,
        scratch_shapes=scratch_shapes,
        name=name,
        cost_estimate=pl.CostEstimate(flops=flops, bytes_accessed=moved, transcendentals=0),
        compiler_params=pltpu.CompilerParams(vmem_limit_bytes=vmem),
    )


def in_hbm(array):
    return pltpu.with_memory_space_constraint(array, pltpu.HBM)


def shift(array, axis, size, step):
    return lax.ppermute(array, axis, [(i, (i + step) % size) for i in range(size)])


LINE_OF_FOUR = (
    ((0, 2), (1, 0), (2, 3), (3, 1)),
    ((0, 3), (1, 2), (2, 1), (3, 0)),
    ((0, 1), (1, 3), (2, 0), (3, 2)),
)


def gather_permutes(patches):
    if patches == 4:
        return LINE_OF_FOUR
    return [
        [(i, (i + step) % patches) for i in range(patches)] for step in range(patches - 1, 0, -1)
    ]


def gather_sources(patches, place):
    sources = [place]
    for pairs in gather_permutes(patches):
        before = {target: source for source, target in pairs}
        value = jnp.int32(before[0])
        for i in range(1, patches):
            value = jnp.where(place == i, jnp.int32(before[i]), value)
        sources.append(value)
    return sources


def early_weight_kernel(subs, columns, early, weight_ref, out_ref, sems):
    chip = (1 - lax.axis_index("head")) * subs
    copies = []
    for sub in range(subs):
        at = pl.multiple_of((chip + sub) * columns, LANES)
        copies.append(
            pltpu.make_async_copy(
                weight_ref.at[:, pl.ds(at, early)],
                out_ref.at[:, pl.ds(sub * early, early)],
                sems.at[sub],
            )
        )
    for copy in copies:
        copy.start()
    for copy in copies:
        copy.wait()


def stage_kernel(
    patches, q_hbm, held_k_hbm, held_v_hbm, q_ref, products_ref, values_ref, keys_ref, sems
):
    rows, width = q_ref.shape
    sources = gather_sources(patches, lax.axis_index("patch"))
    copies = [pltpu.make_async_copy(q_hbm, q_ref, sems.at[0])]
    for i, source in enumerate(sources):
        at = pl.multiple_of(source * rows, rows)
        for n, (held, ref) in enumerate(((held_k_hbm, keys_ref), (held_v_hbm, values_ref))):
            copies.append(
                pltpu.make_async_copy(
                    held.at[pl.ds(at, rows), :],
                    ref.at[i * rows : (i + 1) * rows, :],
                    sems.at[1 + 2 * i + n],
                )
            )
    for copy in copies:
        copy.start()
    for copy in copies:
        copy.wait()
    for head in range(width // HD):
        cols = slice(head * HD, (head + 1) * HD)
        products_ref[head] = dot_transposed(q_ref[:, cols], keys_ref[:, cols])


def dot_transposed(a, b):
    return lax.dot_general(
        a, b, (((1,), (1,)), ((), ())), preferred_element_type=jnp.float32
    )


def attention_kernel(scale, q_ref, products_ref, values_ref, *refs):
    block_refs, out_ref = refs[:-1], refs[-1]
    rows, width = q_ref.shape
    blocks = jnp.concatenate([ref[...] for ref in block_refs], axis=0)
    for head in range(width // HD):
        cols = slice(head * HD, (head + 1) * HD)
        value_cols = slice(width + head * HD, width + (head + 1) * HD)
        products = products_ref[head] + dot_transposed(q_ref[:, cols], blocks[:, cols])
        scores = products * scale
        weights = jnp.exp(scores - jnp.max(scores, axis=1, keepdims=True))
        totals = jnp.sum(weights, axis=1, keepdims=True)
        high = weights.astype(jnp.bfloat16)
        low = (weights - high.astype(jnp.float32)).astype(jnp.bfloat16)
        sums = jnp.dot(
            jnp.concatenate([high, low], axis=0),
            jnp.concatenate([values_ref[:, cols], blocks[:, value_cols]], axis=1),
            preferred_element_type=jnp.float32,
        )
        sums = sums[:rows] + sums[rows:]
        sums = sums[:, :HD] + sums[:, HD:]
        out_ref[:, cols] = (sums / totals).astype(jnp.bfloat16)


def block_dot(a_ref, weight_ref, start, columns):
    if start is None:
        weight = weight_ref[...]
    else:
        weight = weight_ref[:, pl.ds(pl.multiple_of(start, LANES), columns)]
    return jnp.dot(a_ref[...], weight, preferred_element_type=jnp.float32)


def products(start, columns, refs):
    total = 0.0
    for attended_ref, weight_ref in zip(refs[::2], refs[1::2]):
        total = total + block_dot(attended_ref, weight_ref, start, columns)
    return total


def sent_term_kernel(start, *refs):
    out_ref = refs[-1]
    total = products(start(), out_ref.shape[1], refs[:-1])
    out_ref[...] = total.astype(jnp.bfloat16)


def base_kernel(start, hidden_ref, gate_ref, *refs):
    out_ref = refs[-1]
    total = products(start(), out_ref.shape[1], refs[:-1])
    out_ref[...] = hidden_ref[...].astype(jnp.float32) + gate_ref[...] * total


def final_kernel(early, blocks, base_ref, gate_ref, *refs):
    arrived_refs, (out_ref, result, sems) = refs[:-3], refs[-3:]
    rows = base_ref.shape[0] // blocks
    copies = []
    for n in range(blocks):
        at = slice(n * rows, (n + 1) * rows)
        total = 0.0
        for ref in arrived_refs:
            total = total + ref[at, :].astype(jnp.float32)
        if early:
            result[at, :early] = base_ref[at, :early].astype(jnp.bfloat16)
        total = base_ref[at, early:] + gate_ref[:, early:] * total
        result[at, early:] = total.astype(jnp.bfloat16)
        copies.append(pltpu.make_async_copy(result.at[at, :], out_ref.at[at, :], sems.at[n]))
        copies[n].start()
    for copy in copies:
        copy.wait()


def pack_kernel(early, attended_ref, weight_ref, out_ref):
    rows, width = attended_ref.shape
    other = pl.multiple_of((1 - lax.axis_index("sub")) * early, LANES)
    out_ref[:rows, :width] = attended_ref[...]
    out_ref[rows:, :early] = weight_ref[:, pl.ds(other, early)]


def early_kernel(early, base_ref, gate_ref, attended_ref, weight_ref, packed_ref, out_ref):
    rows, width = attended_ref.shape
    mine = pl.multiple_of(lax.axis_index("sub") * early, LANES)
    total = jnp.dot(
        attended_ref[...],
        weight_ref[:, pl.ds(mine, early)],
        preferred_element_type=jnp.float32,
    ) + jnp.dot(
        packed_ref[:rows, :width], packed_ref[rows:, :early], preferred_element_type=jnp.float32
    )
    out_ref[...] = base_ref[...]
    out_ref[:, :early] = base_ref[:, :early] + gate_ref[:, :early] * total


def solution(mesh):
    patches, heads, subs = mesh.shape["patch"], mesh.shape["head"], mesh.shape["sub"]

    def per_device(
        queries, held_keys, held_values, key_change, value_change, out_weight, hidden_in, gate
    ):
        rows, width = queries.shape
        columns = hidden_in.shape[1]

        early = EARLY if heads == 2 and columns % LANES == 0 and columns > 4 * LANES else 0
        if early:
            with jax.named_scope("early_weight"):
                early_weight = call(
                    functools.partial(early_weight_kernel, subs, columns, early),
                    jax.ShapeDtypeStruct((width, subs * early), jnp.bfloat16),
                    [ANYWHERE],
                    IN_VMEM,
                    "early_weight",
                    moved=4 * width * subs * early,
                    scratch_shapes=[pltpu.SemaphoreType.DMA((subs,))],
                )(in_hbm(out_weight))
                key_change, value_change, early_weight = lax.optimization_barrier(
                    (key_change, value_change, early_weight)
                )

        with jax.named_scope("residual_gather"):
            low = jnp.float32(-jnp.inf)
            residual = jnp.maximum(
                lax.pad(key_change, low, ((0, 0, 0), (0, width, 0))),
                lax.pad(value_change, low, ((0, 0, 0), (width, 0, 0))),
            ).astype(jnp.bfloat16)
            blocks = [residual] + [
                lax.ppermute(residual, "patch", pairs) for pairs in gather_permutes(patches)
            ]

        with jax.named_scope("weight_swap"):
            weights = [out_weight] + [shift(out_weight, "sub", subs, i) for i in range(1, subs)]

        if early:
            with jax.named_scope("early_weight"):
                early_weight = shift(early_weight, "head", heads, 1)

        def weight_and_start(i, step, skip=0):
            def start():
                to = lax.rem(lax.axis_index("head") + step, heads) * subs + lax.axis_index("sub")
                return to * columns + skip

            if columns % LANES == 0:
                return weights[i], start
            return lax.dynamic_slice(weights[i], (0, start()), (width, columns)), lambda: None

        def pairs_and_start(step, skip=0):
            pairs = [
                x
                for i in range(subs)
                for x in (attended_parts[i], weight_and_start(i, step, skip)[0])
            ]
            return pairs, weight_and_start(0, step, skip)[1]

        tokens = rows * patches
        with jax.named_scope("attention"):
            staged_queries, products, values = call(
                functools.partial(stage_kernel, patches),
                [
                    jax.ShapeDtypeStruct((rows, width), jnp.bfloat16),
                    jax.ShapeDtypeStruct((width // HD, rows, tokens), jnp.float32),
                    jax.ShapeDtypeStruct((tokens, width), jnp.bfloat16),
                ],
                [ANYWHERE] * 3,
                [IN_VMEM] * 3,
                "stage",
                flops=2_000_000_000,
                scratch_shapes=[
                    pltpu.VMEM((tokens, width), jnp.bfloat16),
                    pltpu.SemaphoreType.DMA((1 + 2 * patches,)),
                ],
            )(in_hbm(queries), in_hbm(held_keys), in_hbm(held_values))
            attended = call(
                functools.partial(attention_kernel, 1.0 / math.sqrt(HD)),
                jax.ShapeDtypeStruct((rows, width), jnp.bfloat16),
                [IN_VMEM] * (3 + len(blocks)),
                IN_VMEM,
                "attention",
                flops=2_000_000_000,
            )(staged_queries, products, values, *blocks)

        with jax.named_scope("attended_swap"):
            attended_parts = [attended] + [
                shift(attended, "sub", subs, i) for i in range(1, subs)
            ]
            if early:
                other_attended = shift(attended, "head", heads, 1)

        term = jax.ShapeDtypeStruct((rows, columns), jnp.float32)
        sent = jax.ShapeDtypeStruct((rows, columns - early), jnp.bfloat16)
        product_flops = 2 * rows * width * columns
        with jax.named_scope("projection"):
            arrived = []
            for step in range(1, heads):
                pairs, start = pairs_and_start(step, early)
                total = call(
                    functools.partial(sent_term_kernel, start),
                    sent,
                    [IN_VMEM] * len(pairs),
                    IN_VMEM,
                    "sent_term",
                    2 * product_flops,
                )(*pairs)
                arrived.append(shift(total, "head", heads, step))
            gate_row = gate.reshape(1, columns)
            pairs, start = pairs_and_start(0)
            base = call(
                functools.partial(base_kernel, start),
                term,
                [IN_VMEM] * (2 + len(pairs)),
                IN_VMEM,
                "base",
                2 * product_flops,
            )(hidden_in, gate_row, *pairs)
            if early:
                packed = call(
                    functools.partial(pack_kernel, early),
                    jax.ShapeDtypeStruct((rows + width, max(early, width)), jnp.bfloat16),
                    [IN_VMEM] * 2,
                    IN_VMEM,
                    "pack",
                )(other_attended, early_weight)
                packed = shift(packed, "sub", subs, 1)
                base = call(
                    functools.partial(early_kernel, early),
                    term,
                    [IN_VMEM] * 5,
                    IN_VMEM,
                    "early",
                    product_flops // 2,
                )(base, gate_row, other_attended, early_weight, packed)
            row_blocks = 3 if rows % (3 * ROW_TILE) == 0 else 1
            return call(
                functools.partial(final_kernel, early, row_blocks),
                jax.ShapeDtypeStruct((rows, columns), jnp.bfloat16),
                [IN_VMEM] * (2 + len(arrived)),
                ANYWHERE,
                "final",
                moved=rows * columns * 8,
                scratch_shapes=[
                    pltpu.VMEM((rows, columns), jnp.bfloat16),
                    pltpu.SemaphoreType.DMA((row_blocks,)),
                ],
            )(base, gate_row, *arrived)

    in_specs = (
        P(("groups", "patch"), ("head", "sub")),
        P("groups", ("head", "sub")),
        P("groups", ("head", "sub")),
        P(("groups", "patch"), ("head", "sub")),
        P(("groups", "patch"), ("head", "sub")),
        P(("head", "sub"), None),
        P(("groups", "patch"), ("head", "sub")),
        P(("groups", "head", "sub")),
    )
    out_specs = P(("groups", "patch"), ("head", "sub"))
    return jax.shard_map(
        per_device, mesh=mesh, in_specs=in_specs, out_specs=out_specs, check_vma=False
    )
```

```python
import functools
import math

import jax
import jax.numpy as jnp
from jax import lax
from jax.experimental import pallas as pl
from jax.experimental.pallas import tpu as pltpu
from jax.sharding import PartitionSpec as P

HD = 128
LANES = 128
ROW_TILE = 16
VMEM_LIMIT = 12 * 1024 * 1024
EARLY = 256

IN_VMEM = pl.BlockSpec(memory_space=pltpu.VMEM)
ANYWHERE = pl.BlockSpec(memory_space=pl.ANY)


def call(
    kernel,
    out_shape,
    in_specs,
    out_specs,
    name,
    flops=0,
    moved=0,
    scratch_shapes=(),
    vmem=VMEM_LIMIT,
):
    return pl.pallas_call(
        kernel,
        out_shape=out_shape,
        in_specs=in_specs,
        out_specs=out_specs,
        scratch_shapes=scratch_shapes,
        name=name,
        cost_estimate=pl.CostEstimate(flops=flops, bytes_accessed=moved, transcendentals=0),
        compiler_params=pltpu.CompilerParams(vmem_limit_bytes=vmem),
    )


def in_hbm(array):
    return pltpu.with_memory_space_constraint(array, pltpu.HBM)


def shift(array, axis, size, step):
    return lax.ppermute(array, axis, [(i, (i + step) % size) for i in range(size)])


LINE_OF_FOUR = (
    ((0, 3), (1, 2), (2, 1), (3, 0)),
    ((0, 2), (1, 0), (2, 3), (3, 1)),
    ((0, 1), (1, 3), (2, 0), (3, 2)),
)


def gather_permutes(patches):
    if patches == 4:
        return LINE_OF_FOUR
    return [
        [(i, (i + step) % patches) for i in range(patches)] for step in range(patches - 1, 0, -1)
    ]


def gather_sources(patches, place):
    sources = [place]
    for pairs in gather_permutes(patches):
        before = {target: source for source, target in pairs}
        value = jnp.int32(before[0])
        for i in range(1, patches):
            value = jnp.where(place == i, jnp.int32(before[i]), value)
        sources.append(value)
    return sources


def early_weight_kernel(subs, columns, early, weight_ref, out_ref, sems):
    chip = (1 - lax.axis_index("head")) * subs
    copies = []
    for sub in range(subs):
        at = pl.multiple_of((chip + sub) * columns, LANES)
        copies.append(
            pltpu.make_async_copy(
                weight_ref.at[:, pl.ds(at, early)],
                out_ref.at[:, pl.ds(sub * early, early)],
                sems.at[sub],
            )
        )
    for copy in copies:
        copy.start()
    for copy in copies:
        copy.wait()


def stage_kernel(
    patches, q_hbm, held_k_hbm, held_v_hbm, q_ref, products_ref, values_ref, keys_ref, sems
):
    rows, width = q_ref.shape
    sources = gather_sources(patches, lax.axis_index("patch"))
    copies = [pltpu.make_async_copy(q_hbm, q_ref, sems.at[0])]
    for i, source in enumerate(sources):
        at = pl.multiple_of(source * rows, rows)
        for n, (held, ref) in enumerate(((held_k_hbm, keys_ref), (held_v_hbm, values_ref))):
            copies.append(
                pltpu.make_async_copy(
                    held.at[pl.ds(at, rows), :],
                    ref.at[i * rows : (i + 1) * rows, :],
                    sems.at[1 + 2 * i + n],
                )
            )
    for copy in copies:
        copy.start()
    for copy in copies:
        copy.wait()
    for head in range(width // HD):
        cols = slice(head * HD, (head + 1) * HD)
        products_ref[head] = dot_transposed(q_ref[:, cols], keys_ref[:, cols])


def dot_transposed(a, b):
    return lax.dot_general(
        a, b, (((1,), (1,)), ((), ())), preferred_element_type=jnp.float32
    )


def attention_kernel(scale, q_ref, products_ref, values_ref, *refs):
    block_refs, out_ref = refs[:-1], refs[-1]
    rows, width = q_ref.shape
    blocks = jnp.concatenate([ref[...] for ref in block_refs], axis=0)
    for head in range(width // HD):
        cols = slice(head * HD, (head + 1) * HD)
        value_cols = slice(width + head * HD, width + (head + 1) * HD)
        products = products_ref[head] + dot_transposed(q_ref[:, cols], blocks[:, cols])
        scores = products * scale
        weights = jnp.exp(scores - jnp.max(scores, axis=1, keepdims=True))
        totals = jnp.sum(weights, axis=1, keepdims=True)
        high = weights.astype(jnp.bfloat16)
        low = (weights - high.astype(jnp.float32)).astype(jnp.bfloat16)
        sums = jnp.dot(
            jnp.concatenate([high, low], axis=0),
            jnp.concatenate([values_ref[:, cols], blocks[:, value_cols]], axis=1),
            preferred_element_type=jnp.float32,
        )
        sums = sums[:rows] + sums[rows:]
        sums = sums[:, :HD] + sums[:, HD:]
        out_ref[:, cols] = (sums / totals).astype(jnp.bfloat16)


def block_dot(a_ref, weight_ref, start, columns):
    if start is None:
        weight = weight_ref[...]
    else:
        weight = weight_ref[:, pl.ds(pl.multiple_of(start, LANES), columns)]
    return jnp.dot(a_ref[...], weight, preferred_element_type=jnp.float32)


def products(start, columns, refs):
    total = 0.0
    for attended_ref, weight_ref in zip(refs[::2], refs[1::2]):
        total = total + block_dot(attended_ref, weight_ref, start, columns)
    return total


def sent_term_kernel(start, *refs):
    out_ref = refs[-1]
    total = products(start(), out_ref.shape[1], refs[:-1])
    out_ref[...] = total.astype(jnp.bfloat16)


def base_kernel(start, hidden_ref, gate_ref, *refs):
    out_ref = refs[-1]
    total = products(start(), out_ref.shape[1], refs[:-1])
    out_ref[...] = hidden_ref[...].astype(jnp.float32) + gate_ref[...] * total


def final_kernel(early, blocks, base_ref, gate_ref, *refs):
    arrived_refs, (out_ref, result, sems) = refs[:-3], refs[-3:]
    rows = base_ref.shape[0] // blocks
    copies = []
    for n in range(blocks):
        at = slice(n * rows, (n + 1) * rows)
        total = 0.0
        for ref in arrived_refs:
            total = total + ref[at, :].astype(jnp.float32)
        if early:
            result[at, :early] = base_ref[at, :early].astype(jnp.bfloat16)
        total = base_ref[at, early:] + gate_ref[:, early:] * total
        result[at, early:] = total.astype(jnp.bfloat16)
        copies.append(pltpu.make_async_copy(result.at[at, :], out_ref.at[at, :], sems.at[n]))
        copies[n].start()
    for copy in copies:
        copy.wait()


def pack_kernel(early, attended_ref, weight_ref, out_ref):
    rows, width = attended_ref.shape
    other = pl.multiple_of((1 - lax.axis_index("sub")) * early, LANES)
    out_ref[:rows, :width] = attended_ref[...]
    out_ref[rows:, :early] = weight_ref[:, pl.ds(other, early)]


def early_kernel(early, base_ref, gate_ref, attended_ref, weight_ref, packed_ref, out_ref):
    rows, width = attended_ref.shape
    mine = pl.multiple_of(lax.axis_index("sub") * early, LANES)
    total = jnp.dot(
        attended_ref[...],
        weight_ref[:, pl.ds(mine, early)],
        preferred_element_type=jnp.float32,
    ) + jnp.dot(
        packed_ref[:rows, :width], packed_ref[rows:, :early], preferred_element_type=jnp.float32
    )
    out_ref[...] = base_ref[...]
    out_ref[:, :early] = base_ref[:, :early] + gate_ref[:, :early] * total


def solution(mesh):
    patches, heads, subs = mesh.shape["patch"], mesh.shape["head"], mesh.shape["sub"]

    def per_device(
        queries, held_keys, held_values, key_change, value_change, out_weight, hidden_in, gate
    ):
        rows, width = queries.shape
        columns = hidden_in.shape[1]

        early = EARLY if heads == 2 and columns % LANES == 0 and columns > 4 * LANES else 0
        if early:
            with jax.named_scope("early_weight"):
                early_weight = call(
                    functools.partial(early_weight_kernel, subs, columns, early),
                    jax.ShapeDtypeStruct((width, subs * early), jnp.bfloat16),
                    [ANYWHERE],
                    IN_VMEM,
                    "early_weight",
                    moved=4 * width * subs * early,
                    scratch_shapes=[pltpu.SemaphoreType.DMA((subs,))],
                )(in_hbm(out_weight))
                key_change, value_change, early_weight = lax.optimization_barrier(
                    (key_change, value_change, early_weight)
                )

        with jax.named_scope("residual_gather"):
            low = jnp.float32(-jnp.inf)
            residual = jnp.maximum(
                lax.pad(key_change, low, ((0, 0, 0), (0, width, 0))),
                lax.pad(value_change, low, ((0, 0, 0), (width, 0, 0))),
            ).astype(jnp.bfloat16)
            blocks = [residual] + [
                lax.ppermute(residual, "patch", pairs) for pairs in gather_permutes(patches)
            ]

        with jax.named_scope("weight_swap"):
            weights = [out_weight] + [shift(out_weight, "sub", subs, i) for i in range(1, subs)]

        if early:
            with jax.named_scope("early_weight"):
                early_weight = shift(early_weight, "head", heads, 1)

        def weight_and_start(i, step, skip=0):
            def start():
                to = lax.rem(lax.axis_index("head") + step, heads) * subs + lax.axis_index("sub")
                return to * columns + skip

            if columns % LANES == 0:
                return weights[i], start
            return lax.dynamic_slice(weights[i], (0, start()), (width, columns)), lambda: None

        def pairs_and_start(step, skip=0):
            pairs = [
                x
                for i in range(subs)
                for x in (attended_parts[i], weight_and_start(i, step, skip)[0])
            ]
            return pairs, weight_and_start(0, step, skip)[1]

        tokens = rows * patches
        with jax.named_scope("attention"):
            staged_queries, products, values = call(
                functools.partial(stage_kernel, patches),
                [
                    jax.ShapeDtypeStruct((rows, width), jnp.bfloat16),
                    jax.ShapeDtypeStruct((width // HD, rows, tokens), jnp.float32),
                    jax.ShapeDtypeStruct((tokens, width), jnp.bfloat16),
                ],
                [ANYWHERE] * 3,
                [IN_VMEM] * 3,
                "stage",
                flops=2_000_000_000,
                scratch_shapes=[
                    pltpu.VMEM((tokens, width), jnp.bfloat16),
                    pltpu.SemaphoreType.DMA((1 + 2 * patches,)),
                ],
            )(in_hbm(queries), in_hbm(held_keys), in_hbm(held_values))
            attended = call(
                functools.partial(attention_kernel, 1.0 / math.sqrt(HD)),
                jax.ShapeDtypeStruct((rows, width), jnp.bfloat16),
                [IN_VMEM] * (3 + len(blocks)),
                IN_VMEM,
                "attention",
                flops=2_000_000_000,
            )(staged_queries, products, values, *blocks)

        with jax.named_scope("attended_swap"):
            attended_parts = [attended] + [
                shift(attended, "sub", subs, i) for i in range(1, subs)
            ]
            if early:
                other_attended = shift(attended, "head", heads, 1)

        term = jax.ShapeDtypeStruct((rows, columns), jnp.float32)
        sent = jax.ShapeDtypeStruct((rows, columns - early), jnp.bfloat16)
        product_flops = 2 * rows * width * columns
        with jax.named_scope("projection"):
            arrived = []
            for step in range(1, heads):
                pairs, start = pairs_and_start(step, early)
                total = call(
                    functools.partial(sent_term_kernel, start),
                    sent,
                    [IN_VMEM] * len(pairs),
                    IN_VMEM,
                    "sent_term",
                    2 * product_flops,
                )(*pairs)
                arrived.append(shift(total, "head", heads, step))
            gate_row = gate.reshape(1, columns)
            pairs, start = pairs_and_start(0)
            base = call(
                functools.partial(base_kernel, start),
                term,
                [IN_VMEM] * (2 + len(pairs)),
                IN_VMEM,
                "base",
                2 * product_flops,
            )(hidden_in, gate_row, *pairs)
            if early:
                packed = call(
                    functools.partial(pack_kernel, early),
                    jax.ShapeDtypeStruct((rows + width, max(early, width)), jnp.bfloat16),
                    [IN_VMEM] * 2,
                    IN_VMEM,
                    "pack",
                )(other_attended, early_weight)
                packed = shift(packed, "sub", subs, 1)
                base = call(
                    functools.partial(early_kernel, early),
                    term,
                    [IN_VMEM] * 5,
                    IN_VMEM,
                    "early",
                    product_flops // 2,
                )(base, gate_row, other_attended, early_weight, packed)
            row_blocks = 3 if rows % (3 * ROW_TILE) == 0 else 1
            return call(
                functools.partial(final_kernel, early, row_blocks),
                jax.ShapeDtypeStruct((rows, columns), jnp.bfloat16),
                [IN_VMEM] * (2 + len(arrived)),
                ANYWHERE,
                "final",
                moved=rows * columns * 8,
                scratch_shapes=[
                    pltpu.VMEM((rows, columns), jnp.bfloat16),
                    pltpu.SemaphoreType.DMA((row_blocks,)),
                ],
            )(base, gate_row, *arrived)

    in_specs = (
        P(("groups", "patch"), ("head", "sub")),
        P("groups", ("head", "sub")),
        P("groups", ("head", "sub")),
        P(("groups", "patch"), ("head", "sub")),
        P(("groups", "patch"), ("head", "sub")),
        P(("head", "sub"), None),
        P(("groups", "patch"), ("head", "sub")),
        P(("groups", "head", "sub")),
    )
    out_specs = P(("groups", "patch"), ("head", "sub"))
    return jax.shard_map(
        per_device, mesh=mesh, in_specs=in_specs, out_specs=out_specs, check_vma=False
    )
```

```python
import functools
import math

import jax
import jax.numpy as jnp
from jax import lax
from jax.experimental import pallas as pl
from jax.experimental.pallas import tpu as pltpu
from jax.sharding import PartitionSpec as P

HD = 128
LANES = 128
ROW_TILE = 16
VMEM_LIMIT = 12 * 1024 * 1024
EARLY = 256

IN_VMEM = pl.BlockSpec(memory_space=pltpu.VMEM)
ANYWHERE = pl.BlockSpec(memory_space=pl.ANY)


def call(
    kernel,
    out_shape,
    in_specs,
    out_specs,
    name,
    flops=0,
    moved=0,
    scratch_shapes=(),
    vmem=VMEM_LIMIT,
):
    return pl.pallas_call(
        kernel,
        out_shape=out_shape,
        in_specs=in_specs,
        out_specs=out_specs,
        scratch_shapes=scratch_shapes,
        name=name,
        cost_estimate=pl.CostEstimate(flops=flops, bytes_accessed=moved, transcendentals=0),
        compiler_params=pltpu.CompilerParams(vmem_limit_bytes=vmem),
    )


def in_hbm(array):
    return pltpu.with_memory_space_constraint(array, pltpu.HBM)


def shift(array, axis, size, step):
    return lax.ppermute(array, axis, [(i, (i + step) % size) for i in range(size)])


LINE_OF_FOUR = (
    ((2, 0, 3, 1), (3, 0, 1, 2)),
    ((3, 2, 1, 0), (2, 3, 0, 1)),
    ((1, 3, 0, 2), (1, 2, 3, 0)),
)


def gather_targets(patches, subs):
    if patches == 4 and subs == 2:
        return LINE_OF_FOUR
    return [
        [[(i + step) % patches for i in range(patches)]] * subs
        for step in range(patches - 1, 0, -1)
    ]


def gather(own, patches, subs):
    blocks = [own]
    for targets in gather_targets(patches, subs):
        pairs = [
            (place * subs + sub, targets[sub][place] * subs + sub)
            for place in range(patches)
            for sub in range(subs)
        ]
        blocks.append(lax.ppermute(own, ("patch", "sub"), pairs))
    return blocks


def gather_sources(patches, subs):
    place, core = lax.axis_index("patch"), lax.axis_index("sub")
    sources = [place]
    for targets in gather_targets(patches, subs):
        value = jnp.int32(0)
        for sub in range(subs):
            for source, target in enumerate(targets[sub]):
                here = jnp.logical_and(place == target, core == sub)
                value = jnp.where(here, jnp.int32(source), value)
        sources.append(value)
    return sources


def early_weight_kernel(subs, columns, early, weight_ref, out_ref, sems):
    chip = (1 - lax.axis_index("head")) * subs
    copies = []
    for sub in range(subs):
        at = pl.multiple_of((chip + sub) * columns, LANES)
        copies.append(
            pltpu.make_async_copy(
                weight_ref.at[:, pl.ds(at, early)],
                out_ref.at[:, pl.ds(sub * early, early)],
                sems.at[sub],
            )
        )
    for copy in copies:
        copy.start()
    for copy in copies:
        copy.wait()


def stage_kernel(
    patches, subs, q_hbm, held_k_hbm, held_v_hbm, q_ref, products_ref, values_ref, keys_ref, sems
):
    rows, width = q_ref.shape
    sources = gather_sources(patches, subs)
    copies = [pltpu.make_async_copy(q_hbm, q_ref, sems.at[0])]
    for i, source in enumerate(sources):
        at = pl.multiple_of(source * rows, rows)
        for n, (held, ref) in enumerate(((held_k_hbm, keys_ref), (held_v_hbm, values_ref))):
            copies.append(
                pltpu.make_async_copy(
                    held.at[pl.ds(at, rows), :],
                    ref.at[i * rows : (i + 1) * rows, :],
                    sems.at[1 + 2 * i + n],
                )
            )
    for copy in copies:
        copy.start()
    for copy in copies:
        copy.wait()
    for head in range(width // HD):
        cols = slice(head * HD, (head + 1) * HD)
        products_ref[head] = dot_transposed(q_ref[:, cols], keys_ref[:, cols])


def dot_transposed(a, b):
    return lax.dot_general(
        a, b, (((1,), (1,)), ((), ())), preferred_element_type=jnp.float32
    )


def attention_kernel(scale, q_ref, products_ref, values_ref, *refs):
    block_refs, out_ref = refs[:-1], refs[-1]
    rows, width = q_ref.shape
    blocks = jnp.concatenate([ref[...] for ref in block_refs], axis=0)
    for head in range(width // HD):
        cols = slice(head * HD, (head + 1) * HD)
        value_cols = slice(width + head * HD, width + (head + 1) * HD)
        products = products_ref[head] + dot_transposed(q_ref[:, cols], blocks[:, cols])
        scores = products * scale
        weights = jnp.exp(scores - jnp.max(scores, axis=1, keepdims=True))
        totals = jnp.sum(weights, axis=1, keepdims=True)
        high = weights.astype(jnp.bfloat16)
        low = (weights - high.astype(jnp.float32)).astype(jnp.bfloat16)
        sums = jnp.dot(
            jnp.concatenate([high, low], axis=0),
            jnp.concatenate([values_ref[:, cols], blocks[:, value_cols]], axis=1),
            preferred_element_type=jnp.float32,
        )
        sums = sums[:rows] + sums[rows:]
        sums = sums[:, :HD] + sums[:, HD:]
        out_ref[:, cols] = (sums / totals).astype(jnp.bfloat16)


def block_dot(a_ref, weight_ref, start, columns):
    if start is None:
        weight = weight_ref[...]
    else:
        weight = weight_ref[:, pl.ds(pl.multiple_of(start, LANES), columns)]
    return jnp.dot(a_ref[...], weight, preferred_element_type=jnp.float32)


def products(start, columns, refs):
    total = 0.0
    for attended_ref, weight_ref in zip(refs[::2], refs[1::2]):
        total = total + block_dot(attended_ref, weight_ref, start, columns)
    return total


def sent_term_kernel(start, *refs):
    out_ref = refs[-1]
    total = products(start(), out_ref.shape[1], refs[:-1])
    out_ref[...] = total.astype(jnp.bfloat16)


def base_kernel(start, hidden_ref, gate_ref, *refs):
    out_ref = refs[-1]
    total = products(start(), out_ref.shape[1], refs[:-1])
    out_ref[...] = hidden_ref[...].astype(jnp.float32) + gate_ref[...] * total


def final_kernel(early, blocks, base_ref, gate_ref, *refs):
    arrived_refs, (out_ref, result, sems) = refs[:-3], refs[-3:]
    rows = base_ref.shape[0] // blocks
    copies = []
    for n in range(blocks):
        at = slice(n * rows, (n + 1) * rows)
        total = 0.0
        for ref in arrived_refs:
            total = total + ref[at, :].astype(jnp.float32)
        if early:
            result[at, :early] = base_ref[at, :early].astype(jnp.bfloat16)
        total = base_ref[at, early:] + gate_ref[:, early:] * total
        result[at, early:] = total.astype(jnp.bfloat16)
        copies.append(pltpu.make_async_copy(result.at[at, :], out_ref.at[at, :], sems.at[n]))
        copies[n].start()
    for copy in copies:
        copy.wait()


def pack_kernel(early, attended_ref, weight_ref, out_ref):
    rows, width = attended_ref.shape
    other = pl.multiple_of((1 - lax.axis_index("sub")) * early, LANES)
    out_ref[:rows, :width] = attended_ref[...]
    out_ref[rows:, :early] = weight_ref[:, pl.ds(other, early)]


def early_kernel(early, base_ref, gate_ref, attended_ref, weight_ref, packed_ref, out_ref):
    rows, width = attended_ref.shape
    mine = pl.multiple_of(lax.axis_index("sub") * early, LANES)
    total = jnp.dot(
        attended_ref[...],
        weight_ref[:, pl.ds(mine, early)],
        preferred_element_type=jnp.float32,
    ) + jnp.dot(
        packed_ref[:rows, :width], packed_ref[rows:, :early], preferred_element_type=jnp.float32
    )
    out_ref[...] = base_ref[...]
    out_ref[:, :early] = base_ref[:, :early] + gate_ref[:, :early] * total


def solution(mesh):
    patches, heads, subs = mesh.shape["patch"], mesh.shape["head"], mesh.shape["sub"]

    def per_device(
        queries, held_keys, held_values, key_change, value_change, out_weight, hidden_in, gate
    ):
        rows, width = queries.shape
        columns = hidden_in.shape[1]

        early = EARLY if heads == 2 and columns % LANES == 0 and columns > 4 * LANES else 0
        if early:
            with jax.named_scope("early_weight"):
                early_weight = call(
                    functools.partial(early_weight_kernel, subs, columns, early),
                    jax.ShapeDtypeStruct((width, subs * early), jnp.bfloat16),
                    [ANYWHERE],
                    IN_VMEM,
                    "early_weight",
                    moved=4 * width * subs * early,
                    scratch_shapes=[pltpu.SemaphoreType.DMA((subs,))],
                )(in_hbm(out_weight))
                key_change, value_change, early_weight = lax.optimization_barrier(
                    (key_change, value_change, early_weight)
                )

        with jax.named_scope("residual_gather"):
            low = jnp.float32(-jnp.inf)
            residual = jnp.maximum(
                lax.pad(key_change, low, ((0, 0, 0), (0, width, 0))),
                lax.pad(value_change, low, ((0, 0, 0), (width, 0, 0))),
            ).astype(jnp.bfloat16)
            blocks = gather(residual, patches, subs)

        with jax.named_scope("weight_swap"):
            weights = [out_weight] + [shift(out_weight, "sub", subs, i) for i in range(1, subs)]

        if early:
            with jax.named_scope("early_weight"):
                early_weight = shift(early_weight, "head", heads, 1)

        def weight_and_start(i, step, skip=0):
            def start():
                to = lax.rem(lax.axis_index("head") + step, heads) * subs + lax.axis_index("sub")
                return to * columns + skip

            if columns % LANES == 0:
                return weights[i], start
            return lax.dynamic_slice(weights[i], (0, start()), (width, columns)), lambda: None

        def pairs_and_start(step, skip=0):
            pairs = [
                x
                for i in range(subs)
                for x in (attended_parts[i], weight_and_start(i, step, skip)[0])
            ]
            return pairs, weight_and_start(0, step, skip)[1]

        tokens = rows * patches
        with jax.named_scope("attention"):
            staged_queries, products, values = call(
                functools.partial(stage_kernel, patches, subs),
                [
                    jax.ShapeDtypeStruct((rows, width), jnp.bfloat16),
                    jax.ShapeDtypeStruct((width // HD, rows, tokens), jnp.float32),
                    jax.ShapeDtypeStruct((tokens, width), jnp.bfloat16),
                ],
                [ANYWHERE] * 3,
                [IN_VMEM] * 3,
                "stage",
                flops=2_000_000_000,
                scratch_shapes=[
                    pltpu.VMEM((tokens, width), jnp.bfloat16),
                    pltpu.SemaphoreType.DMA((1 + 2 * patches,)),
                ],
            )(in_hbm(queries), in_hbm(held_keys), in_hbm(held_values))
            attended = call(
                functools.partial(attention_kernel, 1.0 / math.sqrt(HD)),
                jax.ShapeDtypeStruct((rows, width), jnp.bfloat16),
                [IN_VMEM] * (3 + len(blocks)),
                IN_VMEM,
                "attention",
                flops=2_000_000_000,
            )(staged_queries, products, values, *blocks)

        with jax.named_scope("attended_swap"):
            attended_parts = [attended] + [
                shift(attended, "sub", subs, i) for i in range(1, subs)
            ]
            if early:
                other_attended = shift(attended, "head", heads, 1)

        term = jax.ShapeDtypeStruct((rows, columns), jnp.float32)
        sent = jax.ShapeDtypeStruct((rows, columns - early), jnp.bfloat16)
        product_flops = 2 * rows * width * columns
        with jax.named_scope("projection"):
            arrived = []
            for step in range(1, heads):
                pairs, start = pairs_and_start(step, early)
                total = call(
                    functools.partial(sent_term_kernel, start),
                    sent,
                    [IN_VMEM] * len(pairs),
                    IN_VMEM,
                    "sent_term",
                    2 * product_flops,
                )(*pairs)
                arrived.append(shift(total, "head", heads, step))
            gate_row = gate.reshape(1, columns)
            pairs, start = pairs_and_start(0)
            base = call(
                functools.partial(base_kernel, start),
                term,
                [IN_VMEM] * (2 + len(pairs)),
                IN_VMEM,
                "base",
                2 * product_flops,
            )(hidden_in, gate_row, *pairs)
            if early:
                packed = call(
                    functools.partial(pack_kernel, early),
                    jax.ShapeDtypeStruct((rows + width, max(early, width)), jnp.bfloat16),
                    [IN_VMEM] * 2,
                    IN_VMEM,
                    "pack",
                )(other_attended, early_weight)
                packed = shift(packed, "sub", subs, 1)
                base = call(
                    functools.partial(early_kernel, early),
                    term,
                    [IN_VMEM] * 5,
                    IN_VMEM,
                    "early",
                    product_flops // 2,
                )(base, gate_row, other_attended, early_weight, packed)
            row_blocks = 3 if rows % (3 * ROW_TILE) == 0 else 1
            return call(
                functools.partial(final_kernel, early, row_blocks),
                jax.ShapeDtypeStruct((rows, columns), jnp.bfloat16),
                [IN_VMEM] * (2 + len(arrived)),
                ANYWHERE,
                "final",
                moved=rows * columns * 8,
                scratch_shapes=[
                    pltpu.VMEM((rows, columns), jnp.bfloat16),
                    pltpu.SemaphoreType.DMA((row_blocks,)),
                ],
            )(base, gate_row, *arrived)

    in_specs = (
        P(("groups", "patch"), ("head", "sub")),
        P("groups", ("head", "sub")),
        P("groups", ("head", "sub")),
        P(("groups", "patch"), ("head", "sub")),
        P(("groups", "patch"), ("head", "sub")),
        P(("head", "sub"), None),
        P(("groups", "patch"), ("head", "sub")),
        P(("groups", "head", "sub")),
    )
    out_specs = P(("groups", "patch"), ("head", "sub"))
    return jax.shard_map(
        per_device, mesh=mesh, in_specs=in_specs, out_specs=out_specs, check_vma=False
    )
```

```python
import functools
import math

import jax
import jax.numpy as jnp
from jax import lax
from jax.experimental import pallas as pl
from jax.experimental.pallas import tpu as pltpu
from jax.sharding import PartitionSpec as P

HD = 128
LANES = 128
ROW_TILE = 16
VMEM_LIMIT = 12 * 1024 * 1024
EARLY = 256

IN_VMEM = pl.BlockSpec(memory_space=pltpu.VMEM)
ANYWHERE = pl.BlockSpec(memory_space=pl.ANY)


def call(
    kernel,
    out_shape,
    in_specs,
    out_specs,
    name,
    flops=0,
    moved=0,
    scratch_shapes=(),
    vmem=VMEM_LIMIT,
):
    return pl.pallas_call(
        kernel,
        out_shape=out_shape,
        in_specs=in_specs,
        out_specs=out_specs,
        scratch_shapes=scratch_shapes,
        name=name,
        cost_estimate=pl.CostEstimate(flops=flops, bytes_accessed=moved, transcendentals=0),
        compiler_params=pltpu.CompilerParams(vmem_limit_bytes=vmem),
    )


def in_hbm(array):
    return pltpu.with_memory_space_constraint(array, pltpu.HBM)


def shift(array, axis, size, step):
    return lax.ppermute(array, axis, [(i, (i + step) % size) for i in range(size)])


LINE_OF_FOUR = (
    ((3, 0, 1, 2), (2, 0, 3, 1)),
    ((2, 3, 0, 1), (3, 2, 1, 0)),
    ((1, 2, 3, 0), (1, 3, 0, 2)),
)


def gather_targets(patches, subs):
    if patches == 4 and subs == 2:
        return LINE_OF_FOUR
    return [
        [[(i + step) % patches for i in range(patches)]] * subs
        for step in range(patches - 1, 0, -1)
    ]


def gather(own, patches, subs):
    blocks = [own]
    for targets in gather_targets(patches, subs):
        pairs = [
            (place * subs + sub, targets[sub][place] * subs + sub)
            for place in range(patches)
            for sub in range(subs)
        ]
        blocks.append(lax.ppermute(own, ("patch", "sub"), pairs))
    return blocks


def gather_sources(patches, subs):
    place, core = lax.axis_index("patch"), lax.axis_index("sub")
    sources = [place]
    for targets in gather_targets(patches, subs):
        value = jnp.int32(0)
        for sub in range(subs):
            for source, target in enumerate(targets[sub]):
                here = jnp.logical_and(place == target, core == sub)
                value = jnp.where(here, jnp.int32(source), value)
        sources.append(value)
    return sources


def early_weight_kernel(subs, columns, early, weight_ref, out_ref, sems):
    chip = (1 - lax.axis_index("head")) * subs
    copies = []
    for sub in range(subs):
        at = pl.multiple_of((chip + sub) * columns, LANES)
        copies.append(
            pltpu.make_async_copy(
                weight_ref.at[:, pl.ds(at, early)],
                out_ref.at[:, pl.ds(sub * early, early)],
                sems.at[sub],
            )
        )
    for copy in copies:
        copy.start()
    for copy in copies:
        copy.wait()


def stage_kernel(
    patches, subs, q_hbm, held_k_hbm, held_v_hbm, q_ref, products_ref, values_ref, keys_ref, sems
):
    rows, width = q_ref.shape
    sources = gather_sources(patches, subs)
    copies = [pltpu.make_async_copy(q_hbm, q_ref, sems.at[0])]
    for i, source in enumerate(sources):
        at = pl.multiple_of(source * rows, rows)
        for n, (held, ref) in enumerate(((held_k_hbm, keys_ref), (held_v_hbm, values_ref))):
            copies.append(
                pltpu.make_async_copy(
                    held.at[pl.ds(at, rows), :],
                    ref.at[i * rows : (i + 1) * rows, :],
                    sems.at[1 + 2 * i + n],
                )
            )
    for copy in copies:
        copy.start()
    for copy in copies:
        copy.wait()
    for head in range(width // HD):
        cols = slice(head * HD, (head + 1) * HD)
        products_ref[head] = dot_transposed(q_ref[:, cols], keys_ref[:, cols])


def dot_transposed(a, b):
    return lax.dot_general(
        a, b, (((1,), (1,)), ((), ())), preferred_element_type=jnp.float32
    )


def attention_kernel(scale, q_ref, products_ref, values_ref, *refs):
    block_refs, out_ref = refs[:-1], refs[-1]
    rows, width = q_ref.shape
    blocks = jnp.concatenate([ref[...] for ref in block_refs], axis=0)
    for head in range(width // HD):
        cols = slice(head * HD, (head + 1) * HD)
        value_cols = slice(width + head * HD, width + (head + 1) * HD)
        products = products_ref[head] + dot_transposed(q_ref[:, cols], blocks[:, cols])
        scores = products * scale
        weights = jnp.exp(scores - jnp.max(scores, axis=1, keepdims=True))
        totals = jnp.sum(weights, axis=1, keepdims=True)
        high = weights.astype(jnp.bfloat16)
        low = (weights - high.astype(jnp.float32)).astype(jnp.bfloat16)
        sums = jnp.dot(
            jnp.concatenate([high, low], axis=0),
            jnp.concatenate([values_ref[:, cols], blocks[:, value_cols]], axis=1),
            preferred_element_type=jnp.float32,
        )
        sums = sums[:rows] + sums[rows:]
        sums = sums[:, :HD] + sums[:, HD:]
        out_ref[:, cols] = (sums / totals).astype(jnp.bfloat16)


def block_dot(a_ref, weight_ref, start, columns):
    if start is None:
        weight = weight_ref[...]
    else:
        weight = weight_ref[:, pl.ds(pl.multiple_of(start, LANES), columns)]
    return jnp.dot(a_ref[...], weight, preferred_element_type=jnp.float32)


def products(start, columns, refs):
    total = 0.0
    for attended_ref, weight_ref in zip(refs[::2], refs[1::2]):
        total = total + block_dot(attended_ref, weight_ref, start, columns)
    return total


def sent_term_kernel(start, *refs):
    out_ref = refs[-1]
    total = products(start(), out_ref.shape[1], refs[:-1])
    out_ref[...] = total.astype(jnp.bfloat16)


def base_kernel(start, hidden_ref, gate_ref, *refs):
    out_ref = refs[-1]
    total = products(start(), out_ref.shape[1], refs[:-1])
    out_ref[...] = hidden_ref[...].astype(jnp.float32) + gate_ref[...] * total


def final_kernel(early, blocks, base_ref, gate_ref, *refs):
    arrived_refs, (out_ref, result, sems) = refs[:-3], refs[-3:]
    rows = base_ref.shape[0] // blocks
    copies = []
    for n in range(blocks):
        at = slice(n * rows, (n + 1) * rows)
        total = 0.0
        for ref in arrived_refs:
            total = total + ref[at, :].astype(jnp.float32)
        if early:
            result[at, :early] = base_ref[at, :early].astype(jnp.bfloat16)
        total = base_ref[at, early:] + gate_ref[:, early:] * total
        result[at, early:] = total.astype(jnp.bfloat16)
        copies.append(pltpu.make_async_copy(result.at[at, :], out_ref.at[at, :], sems.at[n]))
        copies[n].start()
    for copy in copies:
        copy.wait()


def pack_kernel(early, attended_ref, weight_ref, out_ref):
    rows, width = attended_ref.shape
    other = pl.multiple_of((1 - lax.axis_index("sub")) * early, LANES)
    out_ref[:rows, :width] = attended_ref[...]
    out_ref[rows:, :early] = weight_ref[:, pl.ds(other, early)]


def early_kernel(early, base_ref, gate_ref, attended_ref, weight_ref, packed_ref, out_ref):
    rows, width = attended_ref.shape
    mine = pl.multiple_of(lax.axis_index("sub") * early, LANES)
    total = jnp.dot(
        attended_ref[...],
        weight_ref[:, pl.ds(mine, early)],
        preferred_element_type=jnp.float32,
    ) + jnp.dot(
        packed_ref[:rows, :width], packed_ref[rows:, :early], preferred_element_type=jnp.float32
    )
    out_ref[...] = base_ref[...]
    out_ref[:, :early] = base_ref[:, :early] + gate_ref[:, :early] * total


def solution(mesh):
    patches, heads, subs = mesh.shape["patch"], mesh.shape["head"], mesh.shape["sub"]

    def per_device(
        queries, held_keys, held_values, key_change, value_change, out_weight, hidden_in, gate
    ):
        rows, width = queries.shape
        columns = hidden_in.shape[1]

        early = EARLY if heads == 2 and columns % LANES == 0 and columns > 4 * LANES else 0
        if early:
            with jax.named_scope("early_weight"):
                early_weight = call(
                    functools.partial(early_weight_kernel, subs, columns, early),
                    jax.ShapeDtypeStruct((width, subs * early), jnp.bfloat16),
                    [ANYWHERE],
                    IN_VMEM,
                    "early_weight",
                    moved=4 * width * subs * early,
                    scratch_shapes=[pltpu.SemaphoreType.DMA((subs,))],
                )(in_hbm(out_weight))
                key_change, value_change, early_weight = lax.optimization_barrier(
                    (key_change, value_change, early_weight)
                )

        with jax.named_scope("residual_gather"):
            low = jnp.float32(-jnp.inf)
            residual = jnp.maximum(
                lax.pad(key_change, low, ((0, 0, 0), (0, width, 0))),
                lax.pad(value_change, low, ((0, 0, 0), (width, 0, 0))),
            ).astype(jnp.bfloat16)
            blocks = gather(residual, patches, subs)

        with jax.named_scope("weight_swap"):
            weights = [out_weight] + [shift(out_weight, "sub", subs, i) for i in range(1, subs)]

        if early:
            with jax.named_scope("early_weight"):
                early_weight = shift(early_weight, "head", heads, 1)

        def weight_and_start(i, step, skip=0):
            def start():
                to = lax.rem(lax.axis_index("head") + step, heads) * subs + lax.axis_index("sub")
                return to * columns + skip

            if columns % LANES == 0:
                return weights[i], start
            return lax.dynamic_slice(weights[i], (0, start()), (width, columns)), lambda: None

        def pairs_and_start(step, skip=0):
            pairs = [
                x
                for i in range(subs)
                for x in (attended_parts[i], weight_and_start(i, step, skip)[0])
            ]
            return pairs, weight_and_start(0, step, skip)[1]

        tokens = rows * patches
        with jax.named_scope("attention"):
            staged_queries, products, values = call(
                functools.partial(stage_kernel, patches, subs),
                [
                    jax.ShapeDtypeStruct((rows, width), jnp.bfloat16),
                    jax.ShapeDtypeStruct((width // HD, rows, tokens), jnp.float32),
                    jax.ShapeDtypeStruct((tokens, width), jnp.bfloat16),
                ],
                [ANYWHERE] * 3,
                [IN_VMEM] * 3,
                "stage",
                flops=2_000_000_000,
                scratch_shapes=[
                    pltpu.VMEM((tokens, width), jnp.bfloat16),
                    pltpu.SemaphoreType.DMA((1 + 2 * patches,)),
                ],
            )(in_hbm(queries), in_hbm(held_keys), in_hbm(held_values))
            attended = call(
                functools.partial(attention_kernel, 1.0 / math.sqrt(HD)),
                jax.ShapeDtypeStruct((rows, width), jnp.bfloat16),
                [IN_VMEM] * (3 + len(blocks)),
                IN_VMEM,
                "attention",
                flops=2_000_000_000,
            )(staged_queries, products, values, *blocks)

        with jax.named_scope("attended_swap"):
            attended_parts = [attended] + [
                shift(attended, "sub", subs, i) for i in range(1, subs)
            ]
            if early:
                other_attended = shift(attended, "head", heads, 1)

        term = jax.ShapeDtypeStruct((rows, columns), jnp.float32)
        sent = jax.ShapeDtypeStruct((rows, columns - early), jnp.bfloat16)
        product_flops = 2 * rows * width * columns
        with jax.named_scope("projection"):
            arrived = []
            for step in range(1, heads):
                pairs, start = pairs_and_start(step, early)
                total = call(
                    functools.partial(sent_term_kernel, start),
                    sent,
                    [IN_VMEM] * len(pairs),
                    IN_VMEM,
                    "sent_term",
                    2 * product_flops,
                )(*pairs)
                arrived.append(shift(total, "head", heads, step))
            gate_row = gate.reshape(1, columns)
            pairs, start = pairs_and_start(0)
            base = call(
                functools.partial(base_kernel, start),
                term,
                [IN_VMEM] * (2 + len(pairs)),
                IN_VMEM,
                "base",
                2 * product_flops,
            )(hidden_in, gate_row, *pairs)
            if early:
                packed = call(
                    functools.partial(pack_kernel, early),
                    jax.ShapeDtypeStruct((rows + width, max(early, width)), jnp.bfloat16),
                    [IN_VMEM] * 2,
                    IN_VMEM,
                    "pack",
                )(other_attended, early_weight)
                packed = shift(packed, "sub", subs, 1)
                base = call(
                    functools.partial(early_kernel, early),
                    term,
                    [IN_VMEM] * 5,
                    IN_VMEM,
                    "early",
                    product_flops // 2,
                )(base, gate_row, other_attended, early_weight, packed)
            row_blocks = 3 if rows % (3 * ROW_TILE) == 0 else 1
            return call(
                functools.partial(final_kernel, early, row_blocks),
                jax.ShapeDtypeStruct((rows, columns), jnp.bfloat16),
                [IN_VMEM] * (2 + len(arrived)),
                ANYWHERE,
                "final",
                moved=rows * columns * 8,
                scratch_shapes=[
                    pltpu.VMEM((rows, columns), jnp.bfloat16),
                    pltpu.SemaphoreType.DMA((row_blocks,)),
                ],
            )(base, gate_row, *arrived)

    in_specs = (
        P(("groups", "patch"), ("head", "sub")),
        P("groups", ("head", "sub")),
        P("groups", ("head", "sub")),
        P(("groups", "patch"), ("head", "sub")),
        P(("groups", "patch"), ("head", "sub")),
        P(("head", "sub"), None),
        P(("groups", "patch"), ("head", "sub")),
        P(("groups", "head", "sub")),
    )
    out_specs = P(("groups", "patch"), ("head", "sub"))
    return jax.shard_map(
        per_device, mesh=mesh, in_specs=in_specs, out_specs=out_specs, check_vma=False
    )
```

```python
import functools
import math

import jax
import jax.numpy as jnp
from jax import lax
from jax.experimental import pallas as pl
from jax.experimental.pallas import tpu as pltpu
from jax.sharding import PartitionSpec as P

HD = 128
LANES = 128
ROW_TILE = 16
VMEM_LIMIT = 12 * 1024 * 1024
EARLY = 256

IN_VMEM = pl.BlockSpec(memory_space=pltpu.VMEM)
ANYWHERE = pl.BlockSpec(memory_space=pl.ANY)


def call(
    kernel,
    out_shape,
    in_specs,
    out_specs,
    name,
    flops=0,
    moved=0,
    scratch_shapes=(),
    vmem=VMEM_LIMIT,
):
    return pl.pallas_call(
        kernel,
        out_shape=out_shape,
        in_specs=in_specs,
        out_specs=out_specs,
        scratch_shapes=scratch_shapes,
        name=name,
        cost_estimate=pl.CostEstimate(flops=flops, bytes_accessed=moved, transcendentals=0),
        compiler_params=pltpu.CompilerParams(vmem_limit_bytes=vmem),
    )


def in_hbm(array):
    return pltpu.with_memory_space_constraint(array, pltpu.HBM)


def shift(array, axis, size, step):
    return lax.ppermute(array, axis, [(i, (i + step) % size) for i in range(size)])


LINE_OF_FOUR = (
    ((2, 0, 3, 1), (3, 0, 1, 2)),
    ((3, 2, 1, 0), (2, 3, 0, 1)),
    ((1, 3, 0, 2), (1, 2, 3, 0)),
)


def gather_targets(patches, subs):
    if patches == 4 and subs == 2:
        return LINE_OF_FOUR
    return [
        [[(i + step) % patches for i in range(patches)]] * subs
        for step in range(patches - 1, 0, -1)
    ]


def gather(own, patches, subs):
    blocks = [own]
    for targets in gather_targets(patches, subs):
        pairs = [
            (place * subs + sub, targets[sub][place] * subs + sub)
            for place in range(patches)
            for sub in range(subs)
        ]
        blocks.append(lax.ppermute(own, ("patch", "sub"), pairs))
    return blocks


def gather_sources(patches, subs):
    place, core = lax.axis_index("patch"), lax.axis_index("sub")
    sources = [place]
    for targets in gather_targets(patches, subs):
        value = jnp.int32(0)
        for sub in range(subs):
            for source, target in enumerate(targets[sub]):
                here = jnp.logical_and(place == target, core == sub)
                value = jnp.where(here, jnp.int32(source), value)
        sources.append(value)
    return sources


def early_weight_kernel(subs, columns, early, weight_ref, out_ref, sems):
    chip = (1 - lax.axis_index("head")) * subs
    copies = []
    for sub in range(subs):
        at = pl.multiple_of((chip + sub) * columns, LANES)
        copies.append(
            pltpu.make_async_copy(
                weight_ref.at[:, pl.ds(at, early)],
                out_ref.at[:, pl.ds(sub * early, early)],
                sems.at[sub],
            )
        )
    for copy in copies:
        copy.start()
    for copy in copies:
        copy.wait()


def stage_kernel(
    patches, subs, q_hbm, held_k_hbm, held_v_hbm, q_ref, products_ref, values_ref, keys_ref, sems
):
    rows, width = q_ref.shape
    sources = gather_sources(patches, subs)
    copies = [pltpu.make_async_copy(q_hbm, q_ref, sems.at[0])]
    for i, source in enumerate(sources):
        at = pl.multiple_of(source * rows, rows)
        for n, (held, ref) in enumerate(((held_k_hbm, keys_ref), (held_v_hbm, values_ref))):
            copies.append(
                pltpu.make_async_copy(
                    held.at[pl.ds(at, rows), :],
                    ref.at[i * rows : (i + 1) * rows, :],
                    sems.at[1 + 2 * i + n],
                )
            )
    for copy in copies:
        copy.start()
    for copy in copies:
        copy.wait()
    for head in range(width // HD):
        cols = slice(head * HD, (head + 1) * HD)
        products_ref[head] = dot_transposed(q_ref[:, cols], keys_ref[:, cols])


def dot_transposed(a, b):
    return lax.dot_general(
        a, b, (((1,), (1,)), ((), ())), preferred_element_type=jnp.float32
    )


def attention_kernel(scale, q_ref, products_ref, values_ref, *refs):
    block_refs, out_ref = refs[:-1], refs[-1]
    rows, width = q_ref.shape
    blocks = jnp.concatenate([ref[...] for ref in block_refs], axis=0)
    heads = [slice(at, at + HD) for at in range(0, width, HD)]
    products = [
        products_ref[n] + dot_transposed(q_ref[:, cols], blocks[:, cols])
        for n, cols in enumerate(heads)
    ]
    highest = [jnp.max(p, axis=1, keepdims=True) for p in products]
    weights = [jnp.exp((p - h) * scale) for p, h in zip(products, highest)]
    totals = [jnp.sum(w, axis=1, keepdims=True) for w in weights]
    high = [w.astype(jnp.bfloat16) for w in weights]
    low = [(w - h.astype(jnp.float32)).astype(jnp.bfloat16) for w, h in zip(weights, high)]
    sums = [
        jnp.dot(
            jnp.concatenate([high[n], low[n]], axis=0),
            jnp.concatenate(
                [values_ref[:, cols], blocks[:, width + cols.start : width + cols.stop]], axis=1
            ),
            preferred_element_type=jnp.float32,
        )
        for n, cols in enumerate(heads)
    ]
    for cols, total, both in zip(heads, totals, sums):
        both = both[:rows] + both[rows:]
        out_ref[:, cols] = ((both[:, :HD] + both[:, HD:]) / total).astype(jnp.bfloat16)


def block_dot(a_ref, weight_ref, start, columns):
    if start is None:
        weight = weight_ref[...]
    else:
        weight = weight_ref[:, pl.ds(pl.multiple_of(start, LANES), columns)]
    return jnp.dot(a_ref[...], weight, preferred_element_type=jnp.float32)


def products(start, columns, refs):
    total = 0.0
    for attended_ref, weight_ref in zip(refs[::2], refs[1::2]):
        total = total + block_dot(attended_ref, weight_ref, start, columns)
    return total


def sent_term_kernel(start, *refs):
    out_ref = refs[-1]
    total = products(start(), out_ref.shape[1], refs[:-1])
    out_ref[...] = total.astype(jnp.bfloat16)


def base_kernel(start, hidden_ref, gate_ref, *refs):
    out_ref = refs[-1]
    total = products(start(), out_ref.shape[1], refs[:-1])
    out_ref[...] = hidden_ref[...].astype(jnp.float32) + gate_ref[...] * total


def final_kernel(early, blocks, base_ref, gate_ref, *refs):
    arrived_refs, (out_ref, result, sems) = refs[:-3], refs[-3:]
    rows = base_ref.shape[0] // blocks
    copies = []
    for n in range(blocks):
        at = slice(n * rows, (n + 1) * rows)
        total = 0.0
        for ref in arrived_refs:
            total = total + ref[at, :].astype(jnp.float32)
        if early:
            result[at, :early] = base_ref[at, :early].astype(jnp.bfloat16)
        total = base_ref[at, early:] + gate_ref[:, early:] * total
        result[at, early:] = total.astype(jnp.bfloat16)
        copies.append(pltpu.make_async_copy(result.at[at, :], out_ref.at[at, :], sems.at[n]))
        copies[n].start()
    for copy in copies:
        copy.wait()


def pack_kernel(early, attended_ref, weight_ref, out_ref):
    rows, width = attended_ref.shape
    other = pl.multiple_of((1 - lax.axis_index("sub")) * early, LANES)
    out_ref[:rows, :width] = attended_ref[...]
    out_ref[rows:, :early] = weight_ref[:, pl.ds(other, early)]


def early_kernel(early, base_ref, gate_ref, attended_ref, weight_ref, packed_ref, out_ref):
    rows, width = attended_ref.shape
    mine = pl.multiple_of(lax.axis_index("sub") * early, LANES)
    total = jnp.dot(
        attended_ref[...],
        weight_ref[:, pl.ds(mine, early)],
        preferred_element_type=jnp.float32,
    ) + jnp.dot(
        packed_ref[:rows, :width], packed_ref[rows:, :early], preferred_element_type=jnp.float32
    )
    out_ref[...] = base_ref[...]
    out_ref[:, :early] = base_ref[:, :early] + gate_ref[:, :early] * total


def solution(mesh):
    patches, heads, subs = mesh.shape["patch"], mesh.shape["head"], mesh.shape["sub"]

    def per_device(
        queries, held_keys, held_values, key_change, value_change, out_weight, hidden_in, gate
    ):
        rows, width = queries.shape
        columns = hidden_in.shape[1]

        early = EARLY if heads == 2 and columns % LANES == 0 and columns > 4 * LANES else 0
        if early:
            with jax.named_scope("early_weight"):
                early_weight = call(
                    functools.partial(early_weight_kernel, subs, columns, early),
                    jax.ShapeDtypeStruct((width, subs * early), jnp.bfloat16),
                    [ANYWHERE],
                    IN_VMEM,
                    "early_weight",
                    moved=4 * width * subs * early,
                    scratch_shapes=[pltpu.SemaphoreType.DMA((subs,))],
                )(in_hbm(out_weight))
                key_change, value_change, early_weight = lax.optimization_barrier(
                    (key_change, value_change, early_weight)
                )

        with jax.named_scope("residual_gather"):
            low = jnp.float32(-jnp.inf)
            residual = jnp.maximum(
                lax.pad(key_change, low, ((0, 0, 0), (0, width, 0))),
                lax.pad(value_change, low, ((0, 0, 0), (width, 0, 0))),
            ).astype(jnp.bfloat16)
            blocks = gather(residual, patches, subs)

        with jax.named_scope("weight_swap"):
            weights = [out_weight] + [shift(out_weight, "sub", subs, i) for i in range(1, subs)]

        if early:
            with jax.named_scope("early_weight"):
                early_weight = shift(early_weight, "head", heads, 1)

        def weight_and_start(i, step, skip=0):
            def start():
                to = lax.rem(lax.axis_index("head") + step, heads) * subs + lax.axis_index("sub")
                return to * columns + skip

            if columns % LANES == 0:
                return weights[i], start
            return lax.dynamic_slice(weights[i], (0, start()), (width, columns)), lambda: None

        def pairs_and_start(step, skip=0):
            pairs = [
                x
                for i in range(subs)
                for x in (attended_parts[i], weight_and_start(i, step, skip)[0])
            ]
            return pairs, weight_and_start(0, step, skip)[1]

        tokens = rows * patches
        with jax.named_scope("attention"):
            staged_queries, products, values = call(
                functools.partial(stage_kernel, patches, subs),
                [
                    jax.ShapeDtypeStruct((rows, width), jnp.bfloat16),
                    jax.ShapeDtypeStruct((width // HD, rows, tokens), jnp.float32),
                    jax.ShapeDtypeStruct((tokens, width), jnp.bfloat16),
                ],
                [ANYWHERE] * 3,
                [IN_VMEM] * 3,
                "stage",
                flops=2_000_000_000,
                scratch_shapes=[
                    pltpu.VMEM((tokens, width), jnp.bfloat16),
                    pltpu.SemaphoreType.DMA((1 + 2 * patches,)),
                ],
            )(in_hbm(queries), in_hbm(held_keys), in_hbm(held_values))
            attended = call(
                functools.partial(attention_kernel, 1.0 / math.sqrt(HD)),
                jax.ShapeDtypeStruct((rows, width), jnp.bfloat16),
                [IN_VMEM] * (3 + len(blocks)),
                IN_VMEM,
                "attention",
                flops=2_000_000_000,
            )(staged_queries, products, values, *blocks)

        with jax.named_scope("attended_swap"):
            attended_parts = [attended] + [
                shift(attended, "sub", subs, i) for i in range(1, subs)
            ]
            if early:
                other_attended = shift(attended, "head", heads, 1)

        term = jax.ShapeDtypeStruct((rows, columns), jnp.float32)
        sent = jax.ShapeDtypeStruct((rows, columns - early), jnp.bfloat16)
        product_flops = 2 * rows * width * columns
        with jax.named_scope("projection"):
            arrived = []
            for step in range(1, heads):
                pairs, start = pairs_and_start(step, early)
                total = call(
                    functools.partial(sent_term_kernel, start),
                    sent,
                    [IN_VMEM] * len(pairs),
                    IN_VMEM,
                    "sent_term",
                    2 * product_flops,
                )(*pairs)
                arrived.append(shift(total, "head", heads, step))
            gate_row = gate.reshape(1, columns)
            pairs, start = pairs_and_start(0)
            base = call(
                functools.partial(base_kernel, start),
                term,
                [IN_VMEM] * (2 + len(pairs)),
                IN_VMEM,
                "base",
                2 * product_flops,
            )(hidden_in, gate_row, *pairs)
            if early:
                packed = call(
                    functools.partial(pack_kernel, early),
                    jax.ShapeDtypeStruct((rows + width, max(early, width)), jnp.bfloat16),
                    [IN_VMEM] * 2,
                    IN_VMEM,
                    "pack",
                )(other_attended, early_weight)
                packed = shift(packed, "sub", subs, 1)
                base = call(
                    functools.partial(early_kernel, early),
                    term,
                    [IN_VMEM] * 5,
                    IN_VMEM,
                    "early",
                    product_flops // 2,
                )(base, gate_row, other_attended, early_weight, packed)
            row_blocks = 3 if rows % (3 * ROW_TILE) == 0 else 1
            return call(
                functools.partial(final_kernel, early, row_blocks),
                jax.ShapeDtypeStruct((rows, columns), jnp.bfloat16),
                [IN_VMEM] * (2 + len(arrived)),
                ANYWHERE,
                "final",
                moved=rows * columns * 8,
                scratch_shapes=[
                    pltpu.VMEM((rows, columns), jnp.bfloat16),
                    pltpu.SemaphoreType.DMA((row_blocks,)),
                ],
            )(base, gate_row, *arrived)

    in_specs = (
        P(("groups", "patch"), ("head", "sub")),
        P("groups", ("head", "sub")),
        P("groups", ("head", "sub")),
        P(("groups", "patch"), ("head", "sub")),
        P(("groups", "patch"), ("head", "sub")),
        P(("head", "sub"), None),
        P(("groups", "patch"), ("head", "sub")),
        P(("groups", "head", "sub")),
    )
    out_specs = P(("groups", "patch"), ("head", "sub"))
    return jax.shard_map(
        per_device, mesh=mesh, in_specs=in_specs, out_specs=out_specs, check_vma=False
    )
```

```python
import functools
import math

import jax
import jax.numpy as jnp
from jax import lax
from jax.experimental import pallas as pl
from jax.experimental.pallas import tpu as pltpu
from jax.sharding import PartitionSpec as P

HD = 128
LANES = 128
ROW_TILE = 16
VMEM_LIMIT = 12 * 1024 * 1024
EARLY = 256

IN_VMEM = pl.BlockSpec(memory_space=pltpu.VMEM)
ANYWHERE = pl.BlockSpec(memory_space=pl.ANY)


def call(
    kernel,
    out_shape,
    in_specs,
    out_specs,
    name,
    flops=0,
    moved=0,
    scratch_shapes=(),
    vmem=VMEM_LIMIT,
):
    return pl.pallas_call(
        kernel,
        out_shape=out_shape,
        in_specs=in_specs,
        out_specs=out_specs,
        scratch_shapes=scratch_shapes,
        name=name,
        cost_estimate=pl.CostEstimate(flops=flops, bytes_accessed=moved, transcendentals=0),
        compiler_params=pltpu.CompilerParams(vmem_limit_bytes=vmem),
    )


def in_hbm(array):
    return pltpu.with_memory_space_constraint(array, pltpu.HBM)


def shift(array, axis, size, step):
    return lax.ppermute(array, axis, [(i, (i + step) % size) for i in range(size)])


LINE_OF_FOUR = (
    ((2, 0, 3, 1), (1, 2, 3, 0)),
    ((3, 2, 1, 0), (3, 0, 1, 2)),
    ((1, 3, 0, 2), (2, 3, 0, 1)),
)


def gather_targets(patches, subs):
    if patches == 4 and subs == 2:
        return LINE_OF_FOUR
    return [
        [[(i + step) % patches for i in range(patches)]] * subs
        for step in range(patches - 1, 0, -1)
    ]


def gather(own, patches, subs):
    blocks = [own]
    for targets in gather_targets(patches, subs):
        pairs = [
            (place * subs + sub, targets[sub][place] * subs + sub)
            for place in range(patches)
            for sub in range(subs)
        ]
        blocks.append(lax.ppermute(own, ("patch", "sub"), pairs))
    return blocks


def gather_sources(patches, subs):
    place, core = lax.axis_index("patch"), lax.axis_index("sub")
    sources = [place]
    for targets in gather_targets(patches, subs):
        value = jnp.int32(0)
        for sub in range(subs):
            for source, target in enumerate(targets[sub]):
                here = jnp.logical_and(place == target, core == sub)
                value = jnp.where(here, jnp.int32(source), value)
        sources.append(value)
    return sources


def early_weight_kernel(subs, columns, early, weight_ref, out_ref, sems):
    chip = (1 - lax.axis_index("head")) * subs
    copies = []
    for sub in range(subs):
        at = pl.multiple_of((chip + sub) * columns, LANES)
        copies.append(
            pltpu.make_async_copy(
                weight_ref.at[:, pl.ds(at, early)],
                out_ref.at[:, pl.ds(sub * early, early)],
                sems.at[sub],
            )
        )
    for copy in copies:
        copy.start()
    for copy in copies:
        copy.wait()


def stage_kernel(
    patches, subs, q_hbm, held_k_hbm, held_v_hbm, q_ref, products_ref, values_ref, keys_ref, sems
):
    rows, width = q_ref.shape
    sources = gather_sources(patches, subs)
    copies = [pltpu.make_async_copy(q_hbm, q_ref, sems.at[0])]
    for i, source in enumerate(sources):
        at = pl.multiple_of(source * rows, rows)
        for n, (held, ref) in enumerate(((held_k_hbm, keys_ref), (held_v_hbm, values_ref))):
            copies.append(
                pltpu.make_async_copy(
                    held.at[pl.ds(at, rows), :],
                    ref.at[i * rows : (i + 1) * rows, :],
                    sems.at[1 + 2 * i + n],
                )
            )
    for copy in copies:
        copy.start()
    for copy in copies:
        copy.wait()
    for head in range(width // HD):
        cols = slice(head * HD, (head + 1) * HD)
        products_ref[head] = dot_transposed(q_ref[:, cols], keys_ref[:, cols])


def dot_transposed(a, b):
    return lax.dot_general(
        a, b, (((1,), (1,)), ((), ())), preferred_element_type=jnp.float32
    )


def attention_kernel(scale, q_ref, products_ref, values_ref, *refs):
    block_refs, out_ref = refs[:-1], refs[-1]
    rows, width = q_ref.shape
    blocks = jnp.concatenate([ref[...] for ref in block_refs], axis=0)
    heads = [slice(at, at + HD) for at in range(0, width, HD)]
    products = [
        products_ref[n] + dot_transposed(q_ref[:, cols], blocks[:, cols])
        for n, cols in enumerate(heads)
    ]
    highest = [jnp.max(p, axis=1, keepdims=True) for p in products]
    weights = [jnp.exp((p - h) * scale) for p, h in zip(products, highest)]
    totals = [jnp.sum(w, axis=1, keepdims=True) for w in weights]
    high = [w.astype(jnp.bfloat16) for w in weights]
    low = [(w - h.astype(jnp.float32)).astype(jnp.bfloat16) for w, h in zip(weights, high)]
    sums = [
        jnp.dot(
            jnp.concatenate([high[n], low[n]], axis=0),
            jnp.concatenate(
                [values_ref[:, cols], blocks[:, width + cols.start : width + cols.stop]], axis=1
            ),
            preferred_element_type=jnp.float32,
        )
        for n, cols in enumerate(heads)
    ]
    for cols, total, both in zip(heads, totals, sums):
        both = both[:rows] + both[rows:]
        out_ref[:, cols] = ((both[:, :HD] + both[:, HD:]) / total).astype(jnp.bfloat16)


def block_dot(a_ref, weight_ref, start, columns):
    if start is None:
        weight = weight_ref[...]
    else:
        weight = weight_ref[:, pl.ds(pl.multiple_of(start, LANES), columns)]
    return jnp.dot(a_ref[...], weight, preferred_element_type=jnp.float32)


def products(start, columns, refs):
    total = 0.0
    for attended_ref, weight_ref in zip(refs[::2], refs[1::2]):
        total = total + block_dot(attended_ref, weight_ref, start, columns)
    return total


def sent_term_kernel(start, *refs):
    out_ref = refs[-1]
    total = products(start(), out_ref.shape[1], refs[:-1])
    out_ref[...] = total.astype(jnp.bfloat16)


def base_kernel(start, hidden_ref, gate_ref, *refs):
    out_ref = refs[-1]
    total = products(start(), out_ref.shape[1], refs[:-1])
    out_ref[...] = hidden_ref[...].astype(jnp.float32) + gate_ref[...] * total


def final_kernel(early, blocks, base_ref, gate_ref, *refs):
    arrived_refs, (out_ref, result, sems) = refs[:-3], refs[-3:]
    rows = base_ref.shape[0] // blocks
    copies = []
    for n in range(blocks):
        at = slice(n * rows, (n + 1) * rows)
        total = 0.0
        for ref in arrived_refs:
            total = total + ref[at, :].astype(jnp.float32)
        if early:
            result[at, :early] = base_ref[at, :early].astype(jnp.bfloat16)
        total = base_ref[at, early:] + gate_ref[:, early:] * total
        result[at, early:] = total.astype(jnp.bfloat16)
        copies.append(pltpu.make_async_copy(result.at[at, :], out_ref.at[at, :], sems.at[n]))
        copies[n].start()
    for copy in copies:
        copy.wait()


def pack_kernel(early, attended_ref, weight_ref, out_ref):
    rows, width = attended_ref.shape
    other = pl.multiple_of((1 - lax.axis_index("sub")) * early, LANES)
    out_ref[:rows, :width] = attended_ref[...]
    out_ref[rows:, :early] = weight_ref[:, pl.ds(other, early)]


def early_kernel(early, base_ref, gate_ref, attended_ref, weight_ref, packed_ref, out_ref):
    rows, width = attended_ref.shape
    mine = pl.multiple_of(lax.axis_index("sub") * early, LANES)
    total = jnp.dot(
        attended_ref[...],
        weight_ref[:, pl.ds(mine, early)],
        preferred_element_type=jnp.float32,
    ) + jnp.dot(
        packed_ref[:rows, :width], packed_ref[rows:, :early], preferred_element_type=jnp.float32
    )
    out_ref[...] = base_ref[...]
    out_ref[:, :early] = base_ref[:, :early] + gate_ref[:, :early] * total


def solution(mesh):
    patches, heads, subs = mesh.shape["patch"], mesh.shape["head"], mesh.shape["sub"]

    def per_device(
        queries, held_keys, held_values, key_change, value_change, out_weight, hidden_in, gate
    ):
        rows, width = queries.shape
        columns = hidden_in.shape[1]

        early = EARLY if heads == 2 and columns % LANES == 0 and columns > 4 * LANES else 0
        if early:
            with jax.named_scope("early_weight"):
                early_weight = call(
                    functools.partial(early_weight_kernel, subs, columns, early),
                    jax.ShapeDtypeStruct((width, subs * early), jnp.bfloat16),
                    [ANYWHERE],
                    IN_VMEM,
                    "early_weight",
                    moved=4 * width * subs * early,
                    scratch_shapes=[pltpu.SemaphoreType.DMA((subs,))],
                )(in_hbm(out_weight))
                key_change, value_change, early_weight = lax.optimization_barrier(
                    (key_change, value_change, early_weight)
                )

        with jax.named_scope("residual_gather"):
            low = jnp.float32(-jnp.inf)
            residual = jnp.maximum(
                lax.pad(key_change, low, ((0, 0, 0), (0, width, 0))),
                lax.pad(value_change, low, ((0, 0, 0), (width, 0, 0))),
            ).astype(jnp.bfloat16)
            blocks = gather(residual, patches, subs)

        with jax.named_scope("weight_swap"):
            weights = [out_weight] + [shift(out_weight, "sub", subs, i) for i in range(1, subs)]

        if early:
            with jax.named_scope("early_weight"):
                early_weight = shift(early_weight, "head", heads, 1)

        def weight_and_start(i, step, skip=0):
            def start():
                to = lax.rem(lax.axis_index("head") + step, heads) * subs + lax.axis_index("sub")
                return to * columns + skip

            if columns % LANES == 0:
                return weights[i], start
            return lax.dynamic_slice(weights[i], (0, start()), (width, columns)), lambda: None

        def pairs_and_start(step, skip=0):
            pairs = [
                x
                for i in range(subs)
                for x in (attended_parts[i], weight_and_start(i, step, skip)[0])
            ]
            return pairs, weight_and_start(0, step, skip)[1]

        tokens = rows * patches
        with jax.named_scope("attention"):
            staged_queries, products, values = call(
                functools.partial(stage_kernel, patches, subs),
                [
                    jax.ShapeDtypeStruct((rows, width), jnp.bfloat16),
                    jax.ShapeDtypeStruct((width // HD, rows, tokens), jnp.float32),
                    jax.ShapeDtypeStruct((tokens, width), jnp.bfloat16),
                ],
                [ANYWHERE] * 3,
                [IN_VMEM] * 3,
                "stage",
                flops=2_000_000_000,
                scratch_shapes=[
                    pltpu.VMEM((tokens, width), jnp.bfloat16),
                    pltpu.SemaphoreType.DMA((1 + 2 * patches,)),
                ],
            )(in_hbm(queries), in_hbm(held_keys), in_hbm(held_values))
            attended = call(
                functools.partial(attention_kernel, 1.0 / math.sqrt(HD)),
                jax.ShapeDtypeStruct((rows, width), jnp.bfloat16),
                [IN_VMEM] * (3 + len(blocks)),
                IN_VMEM,
                "attention",
                flops=2_000_000_000,
            )(staged_queries, products, values, *blocks)

        with jax.named_scope("attended_swap"):
            attended_parts = [attended] + [
                shift(attended, "sub", subs, i) for i in range(1, subs)
            ]
            if early:
                other_attended = shift(attended, "head", heads, 1)

        term = jax.ShapeDtypeStruct((rows, columns), jnp.float32)
        sent = jax.ShapeDtypeStruct((rows, columns - early), jnp.bfloat16)
        product_flops = 2 * rows * width * columns
        with jax.named_scope("projection"):
            arrived = []
            for step in range(1, heads):
                pairs, start = pairs_and_start(step, early)
                total = call(
                    functools.partial(sent_term_kernel, start),
                    sent,
                    [IN_VMEM] * len(pairs),
                    IN_VMEM,
                    "sent_term",
                    2 * product_flops,
                )(*pairs)
                arrived.append(shift(total, "head", heads, step))
            gate_row = gate.reshape(1, columns)
            pairs, start = pairs_and_start(0)
            base = call(
                functools.partial(base_kernel, start),
                term,
                [IN_VMEM] * (2 + len(pairs)),
                IN_VMEM,
                "base",
                2 * product_flops,
            )(hidden_in, gate_row, *pairs)
            if early:
                packed = call(
                    functools.partial(pack_kernel, early),
                    jax.ShapeDtypeStruct((rows + width, max(early, width)), jnp.bfloat16),
                    [IN_VMEM] * 2,
                    IN_VMEM,
                    "pack",
                )(other_attended, early_weight)
                packed = shift(packed, "sub", subs, 1)
                base = call(
                    functools.partial(early_kernel, early),
                    term,
                    [IN_VMEM] * 5,
                    IN_VMEM,
                    "early",
                    product_flops // 2,
                )(base, gate_row, other_attended, early_weight, packed)
            row_blocks = 3 if rows % (3 * ROW_TILE) == 0 else 1
            return call(
                functools.partial(final_kernel, early, row_blocks),
                jax.ShapeDtypeStruct((rows, columns), jnp.bfloat16),
                [IN_VMEM] * (2 + len(arrived)),
                ANYWHERE,
                "final",
                moved=rows * columns * 8,
                scratch_shapes=[
                    pltpu.VMEM((rows, columns), jnp.bfloat16),
                    pltpu.SemaphoreType.DMA((row_blocks,)),
                ],
            )(base, gate_row, *arrived)

    in_specs = (
        P(("groups", "patch"), ("head", "sub")),
        P("groups", ("head", "sub")),
        P("groups", ("head", "sub")),
        P(("groups", "patch"), ("head", "sub")),
        P(("groups", "patch"), ("head", "sub")),
        P(("head", "sub"), None),
        P(("groups", "patch"), ("head", "sub")),
        P(("groups", "head", "sub")),
    )
    out_specs = P(("groups", "patch"), ("head", "sub"))
    return jax.shard_map(
        per_device, mesh=mesh, in_specs=in_specs, out_specs=out_specs, check_vma=False
    )
```

```python
import functools
import math

import jax
import jax.numpy as jnp
from jax import lax
from jax.experimental import pallas as pl
from jax.experimental.pallas import tpu as pltpu
from jax.sharding import PartitionSpec as P

HD = 128
LANES = 128
ROW_TILE = 16
VMEM_LIMIT = 12 * 1024 * 1024
EARLY = 256

IN_VMEM = pl.BlockSpec(memory_space=pltpu.VMEM)
ANYWHERE = pl.BlockSpec(memory_space=pl.ANY)


def call(
    kernel,
    out_shape,
    in_specs,
    out_specs,
    name,
    flops=0,
    moved=0,
    scratch_shapes=(),
    vmem=VMEM_LIMIT,
):
    return pl.pallas_call(
        kernel,
        out_shape=out_shape,
        in_specs=in_specs,
        out_specs=out_specs,
        scratch_shapes=scratch_shapes,
        name=name,
        cost_estimate=pl.CostEstimate(flops=flops, bytes_accessed=moved, transcendentals=0),
        compiler_params=pltpu.CompilerParams(vmem_limit_bytes=vmem),
    )


def in_hbm(array):
    return pltpu.with_memory_space_constraint(array, pltpu.HBM)


def shift(array, axis, size, step):
    return lax.ppermute(array, axis, [(i, (i + step) % size) for i in range(size)])


LINE_OF_FOUR = (
    ((2, 0, 3, 1), (2, 3, 0, 1)),
    ((3, 2, 1, 0), (3, 0, 1, 2)),
    ((1, 3, 0, 2), (1, 2, 3, 0)),
)


def gather_targets(patches, subs):
    if patches == 4 and subs == 2:
        return LINE_OF_FOUR
    return [
        [[(i + step) % patches for i in range(patches)]] * subs
        for step in range(patches - 1, 0, -1)
    ]


def gather(own, patches, subs):
    blocks = [own]
    for targets in gather_targets(patches, subs):
        pairs = [
            (place * subs + sub, targets[sub][place] * subs + sub)
            for place in range(patches)
            for sub in range(subs)
        ]
        blocks.append(lax.ppermute(own, ("patch", "sub"), pairs))
    return blocks


def gather_sources(patches, subs):
    place, core = lax.axis_index("patch"), lax.axis_index("sub")
    sources = [place]
    for targets in gather_targets(patches, subs):
        value = jnp.int32(0)
        for sub in range(subs):
            for source, target in enumerate(targets[sub]):
                here = jnp.logical_and(place == target, core == sub)
                value = jnp.where(here, jnp.int32(source), value)
        sources.append(value)
    return sources


def early_weight_kernel(subs, columns, early, weight_ref, out_ref, sems):
    chip = (1 - lax.axis_index("head")) * subs
    copies = []
    for sub in range(subs):
        at = pl.multiple_of((chip + sub) * columns, LANES)
        copies.append(
            pltpu.make_async_copy(
                weight_ref.at[:, pl.ds(at, early)],
                out_ref.at[:, pl.ds(sub * early, early)],
                sems.at[sub],
            )
        )
    for copy in copies:
        copy.start()
    for copy in copies:
        copy.wait()


def stage_kernel(
    patches, subs, q_hbm, held_k_hbm, held_v_hbm, q_ref, products_ref, values_ref, keys_ref, sems
):
    rows, width = q_ref.shape
    sources = gather_sources(patches, subs)
    copies = [pltpu.make_async_copy(q_hbm, q_ref, sems.at[0])]
    for i, source in enumerate(sources):
        at = pl.multiple_of(source * rows, rows)
        for n, (held, ref) in enumerate(((held_k_hbm, keys_ref), (held_v_hbm, values_ref))):
            copies.append(
                pltpu.make_async_copy(
                    held.at[pl.ds(at, rows), :],
                    ref.at[i * rows : (i + 1) * rows, :],
                    sems.at[1 + 2 * i + n],
                )
            )
    for copy in copies:
        copy.start()
    for copy in copies:
        copy.wait()
    for head in range(width // HD):
        cols = slice(head * HD, (head + 1) * HD)
        products_ref[head] = dot_transposed(q_ref[:, cols], keys_ref[:, cols])


def dot_transposed(a, b):
    return lax.dot_general(
        a, b, (((1,), (1,)), ((), ())), preferred_element_type=jnp.float32
    )


def attention_kernel(scale, q_ref, products_ref, values_ref, *refs):
    block_refs, out_ref = refs[:-1], refs[-1]
    rows, width = q_ref.shape
    blocks = jnp.concatenate([ref[...] for ref in block_refs], axis=0)
    heads = [slice(at, at + HD) for at in range(0, width, HD)]
    products = [
        products_ref[n] + dot_transposed(q_ref[:, cols], blocks[:, cols])
        for n, cols in enumerate(heads)
    ]
    highest = [jnp.max(p, axis=1, keepdims=True) for p in products]
    weights = [jnp.exp((p - h) * scale) for p, h in zip(products, highest)]
    totals = [jnp.sum(w, axis=1, keepdims=True) for w in weights]
    high = [w.astype(jnp.bfloat16) for w in weights]
    low = [(w - h.astype(jnp.float32)).astype(jnp.bfloat16) for w, h in zip(weights, high)]
    sums = [
        jnp.dot(
            jnp.concatenate([high[n], low[n]], axis=0),
            jnp.concatenate(
                [values_ref[:, cols], blocks[:, width + cols.start : width + cols.stop]], axis=1
            ),
            preferred_element_type=jnp.float32,
        )
        for n, cols in enumerate(heads)
    ]
    for cols, total, both in zip(heads, totals, sums):
        both = both[:rows] + both[rows:]
        out_ref[:, cols] = ((both[:, :HD] + both[:, HD:]) / total).astype(jnp.bfloat16)


def block_dot(a_ref, weight_ref, start, columns):
    if start is None:
        weight = weight_ref[...]
    else:
        weight = weight_ref[:, pl.ds(pl.multiple_of(start, LANES), columns)]
    return jnp.dot(a_ref[...], weight, preferred_element_type=jnp.float32)


def products(start, columns, refs):
    total = 0.0
    for attended_ref, weight_ref in zip(refs[::2], refs[1::2]):
        total = total + block_dot(attended_ref, weight_ref, start, columns)
    return total


def sent_term_kernel(start, *refs):
    out_ref = refs[-1]
    total = products(start(), out_ref.shape[1], refs[:-1])
    out_ref[...] = total.astype(jnp.bfloat16)


def base_kernel(start, hidden_ref, gate_ref, *refs):
    out_ref = refs[-1]
    total = products(start(), out_ref.shape[1], refs[:-1])
    out_ref[...] = hidden_ref[...].astype(jnp.float32) + gate_ref[...] * total


def final_kernel(early, blocks, base_ref, gate_ref, *refs):
    arrived_refs, (out_ref, result, sems) = refs[:-3], refs[-3:]
    rows = base_ref.shape[0] // blocks
    copies = []
    for n in range(blocks):
        at = slice(n * rows, (n + 1) * rows)
        total = 0.0
        for ref in arrived_refs:
            total = total + ref[at, :].astype(jnp.float32)
        if early:
            result[at, :early] = base_ref[at, :early].astype(jnp.bfloat16)
        total = base_ref[at, early:] + gate_ref[:, early:] * total
        result[at, early:] = total.astype(jnp.bfloat16)
        copies.append(pltpu.make_async_copy(result.at[at, :], out_ref.at[at, :], sems.at[n]))
        copies[n].start()
    for copy in copies:
        copy.wait()


def pack_kernel(early, attended_ref, weight_ref, out_ref):
    rows, width = attended_ref.shape
    other = pl.multiple_of((1 - lax.axis_index("sub")) * early, LANES)
    out_ref[:rows, :width] = attended_ref[...]
    out_ref[rows:, :early] = weight_ref[:, pl.ds(other, early)]


def early_kernel(early, base_ref, gate_ref, attended_ref, weight_ref, packed_ref, out_ref):
    rows, width = attended_ref.shape
    mine = pl.multiple_of(lax.axis_index("sub") * early, LANES)
    total = jnp.dot(
        attended_ref[...],
        weight_ref[:, pl.ds(mine, early)],
        preferred_element_type=jnp.float32,
    ) + jnp.dot(
        packed_ref[:rows, :width], packed_ref[rows:, :early], preferred_element_type=jnp.float32
    )
    out_ref[...] = base_ref[...]
    out_ref[:, :early] = base_ref[:, :early] + gate_ref[:, :early] * total


def solution(mesh):
    patches, heads, subs = mesh.shape["patch"], mesh.shape["head"], mesh.shape["sub"]

    def per_device(
        queries, held_keys, held_values, key_change, value_change, out_weight, hidden_in, gate
    ):
        rows, width = queries.shape
        columns = hidden_in.shape[1]

        early = EARLY if heads == 2 and columns % LANES == 0 and columns > 4 * LANES else 0
        if early:
            with jax.named_scope("early_weight"):
                early_weight = call(
                    functools.partial(early_weight_kernel, subs, columns, early),
                    jax.ShapeDtypeStruct((width, subs * early), jnp.bfloat16),
                    [ANYWHERE],
                    IN_VMEM,
                    "early_weight",
                    moved=4 * width * subs * early,
                    scratch_shapes=[pltpu.SemaphoreType.DMA((subs,))],
                )(in_hbm(out_weight))
                key_change, value_change, early_weight = lax.optimization_barrier(
                    (key_change, value_change, early_weight)
                )

        with jax.named_scope("residual_gather"):
            low = jnp.float32(-jnp.inf)
            residual = jnp.maximum(
                lax.pad(key_change, low, ((0, 0, 0), (0, width, 0))),
                lax.pad(value_change, low, ((0, 0, 0), (width, 0, 0))),
            ).astype(jnp.bfloat16)
            blocks = gather(residual, patches, subs)

        with jax.named_scope("weight_swap"):
            weights = [out_weight] + [shift(out_weight, "sub", subs, i) for i in range(1, subs)]

        if early:
            with jax.named_scope("early_weight"):
                early_weight = shift(early_weight, "head", heads, 1)

        def weight_and_start(i, step, skip=0):
            def start():
                to = lax.rem(lax.axis_index("head") + step, heads) * subs + lax.axis_index("sub")
                return to * columns + skip

            if columns % LANES == 0:
                return weights[i], start
            return lax.dynamic_slice(weights[i], (0, start()), (width, columns)), lambda: None

        def pairs_and_start(step, skip=0):
            pairs = [
                x
                for i in range(subs)
                for x in (attended_parts[i], weight_and_start(i, step, skip)[0])
            ]
            return pairs, weight_and_start(0, step, skip)[1]

        tokens = rows * patches
        with jax.named_scope("attention"):
            staged_queries, products, values = call(
                functools.partial(stage_kernel, patches, subs),
                [
                    jax.ShapeDtypeStruct((rows, width), jnp.bfloat16),
                    jax.ShapeDtypeStruct((width // HD, rows, tokens), jnp.float32),
                    jax.ShapeDtypeStruct((tokens, width), jnp.bfloat16),
                ],
                [ANYWHERE] * 3,
                [IN_VMEM] * 3,
                "stage",
                flops=2_000_000_000,
                scratch_shapes=[
                    pltpu.VMEM((tokens, width), jnp.bfloat16),
                    pltpu.SemaphoreType.DMA((1 + 2 * patches,)),
                ],
            )(in_hbm(queries), in_hbm(held_keys), in_hbm(held_values))
            attended = call(
                functools.partial(attention_kernel, 1.0 / math.sqrt(HD)),
                jax.ShapeDtypeStruct((rows, width), jnp.bfloat16),
                [IN_VMEM] * (3 + len(blocks)),
                IN_VMEM,
                "attention",
                flops=2_000_000_000,
            )(staged_queries, products, values, *blocks)

        with jax.named_scope("attended_swap"):
            attended_parts = [attended] + [
                shift(attended, "sub", subs, i) for i in range(1, subs)
            ]
            if early:
                other_attended = shift(attended, "head", heads, 1)

        term = jax.ShapeDtypeStruct((rows, columns), jnp.float32)
        sent = jax.ShapeDtypeStruct((rows, columns - early), jnp.bfloat16)
        product_flops = 2 * rows * width * columns
        with jax.named_scope("projection"):
            arrived = []
            for step in range(1, heads):
                pairs, start = pairs_and_start(step, early)
                total = call(
                    functools.partial(sent_term_kernel, start),
                    sent,
                    [IN_VMEM] * len(pairs),
                    IN_VMEM,
                    "sent_term",
                    2 * product_flops,
                )(*pairs)
                arrived.append(shift(total, "head", heads, step))
            gate_row = gate.reshape(1, columns)
            pairs, start = pairs_and_start(0)
            base = call(
                functools.partial(base_kernel, start),
                term,
                [IN_VMEM] * (2 + len(pairs)),
                IN_VMEM,
                "base",
                2 * product_flops,
            )(hidden_in, gate_row, *pairs)
            if early:
                packed = call(
                    functools.partial(pack_kernel, early),
                    jax.ShapeDtypeStruct((rows + width, max(early, width)), jnp.bfloat16),
                    [IN_VMEM] * 2,
                    IN_VMEM,
                    "pack",
                )(other_attended, early_weight)
                packed = shift(packed, "sub", subs, 1)
                base = call(
                    functools.partial(early_kernel, early),
                    term,
                    [IN_VMEM] * 5,
                    IN_VMEM,
                    "early",
                    product_flops // 2,
                )(base, gate_row, other_attended, early_weight, packed)
            row_blocks = 3 if rows % (3 * ROW_TILE) == 0 else 1
            return call(
                functools.partial(final_kernel, early, row_blocks),
                jax.ShapeDtypeStruct((rows, columns), jnp.bfloat16),
                [IN_VMEM] * (2 + len(arrived)),
                ANYWHERE,
                "final",
                moved=rows * columns * 8,
                scratch_shapes=[
                    pltpu.VMEM((rows, columns), jnp.bfloat16),
                    pltpu.SemaphoreType.DMA((row_blocks,)),
                ],
            )(base, gate_row, *arrived)

    in_specs = (
        P(("groups", "patch"), ("head", "sub")),
        P("groups", ("head", "sub")),
        P("groups", ("head", "sub")),
        P(("groups", "patch"), ("head", "sub")),
        P(("groups", "patch"), ("head", "sub")),
        P(("head", "sub"), None),
        P(("groups", "patch"), ("head", "sub")),
        P(("groups", "head", "sub")),
    )
    out_specs = P(("groups", "patch"), ("head", "sub"))
    return jax.shard_map(
        per_device, mesh=mesh, in_specs=in_specs, out_specs=out_specs, check_vma=False
    )
```

```python
import functools
import math

import jax
import jax.numpy as jnp
from jax import lax
from jax.experimental import pallas as pl
from jax.experimental.pallas import tpu as pltpu
from jax.sharding import PartitionSpec as P

HD = 128
LANES = 128
ROW_TILE = 16
VMEM_LIMIT = 12 * 1024 * 1024
EARLY = 256

IN_VMEM = pl.BlockSpec(memory_space=pltpu.VMEM)
ANYWHERE = pl.BlockSpec(memory_space=pl.ANY)


def call(
    kernel,
    out_shape,
    in_specs,
    out_specs,
    name,
    flops=0,
    moved=0,
    scratch_shapes=(),
    vmem=VMEM_LIMIT,
):
    return pl.pallas_call(
        kernel,
        out_shape=out_shape,
        in_specs=in_specs,
        out_specs=out_specs,
        scratch_shapes=scratch_shapes,
        name=name,
        cost_estimate=pl.CostEstimate(flops=flops, bytes_accessed=moved, transcendentals=0),
        compiler_params=pltpu.CompilerParams(vmem_limit_bytes=vmem),
    )


def in_hbm(array):
    return pltpu.with_memory_space_constraint(array, pltpu.HBM)


def shift(array, axis, size, step):
    return lax.ppermute(array, axis, [(i, (i + step) % size) for i in range(size)])


LINE_OF_FOUR = (
    ((2, 0, 3, 1), (2, 3, 1, 0)),
    ((3, 2, 1, 0), (1, 0, 3, 2)),
    ((1, 3, 0, 2), (3, 2, 0, 1)),
)


def gather_targets(patches, subs):
    if patches == 4 and subs == 2:
        return LINE_OF_FOUR
    return [
        [[(i + step) % patches for i in range(patches)]] * subs
        for step in range(patches - 1, 0, -1)
    ]


def gather(own, patches, subs):
    blocks = [own]
    for targets in gather_targets(patches, subs):
        pairs = [
            (place * subs + sub, targets[sub][place] * subs + sub)
            for place in range(patches)
            for sub in range(subs)
        ]
        blocks.append(lax.ppermute(own, ("patch", "sub"), pairs))
    return blocks


def gather_sources(patches, subs):
    place, core = lax.axis_index("patch"), lax.axis_index("sub")
    sources = [place]
    for targets in gather_targets(patches, subs):
        value = jnp.int32(0)
        for sub in range(subs):
            for source, target in enumerate(targets[sub]):
                here = jnp.logical_and(place == target, core == sub)
                value = jnp.where(here, jnp.int32(source), value)
        sources.append(value)
    return sources


def early_weight_kernel(subs, columns, early, weight_ref, out_ref, sems):
    chip = (1 - lax.axis_index("head")) * subs
    copies = []
    for sub in range(subs):
        at = pl.multiple_of((chip + sub) * columns, LANES)
        copies.append(
            pltpu.make_async_copy(
                weight_ref.at[:, pl.ds(at, early)],
                out_ref.at[:, pl.ds(sub * early, early)],
                sems.at[sub],
            )
        )
    for copy in copies:
        copy.start()
    for copy in copies:
        copy.wait()


def stage_kernel(
    patches, subs, q_hbm, held_k_hbm, held_v_hbm, q_ref, products_ref, values_ref, keys_ref, sems
):
    rows, width = q_ref.shape
    sources = gather_sources(patches, subs)
    copies = [pltpu.make_async_copy(q_hbm, q_ref, sems.at[0])]
    for i, source in enumerate(sources):
        at = pl.multiple_of(source * rows, rows)
        for n, (held, ref) in enumerate(((held_k_hbm, keys_ref), (held_v_hbm, values_ref))):
            copies.append(
                pltpu.make_async_copy(
                    held.at[pl.ds(at, rows), :],
                    ref.at[i * rows : (i + 1) * rows, :],
                    sems.at[1 + 2 * i + n],
                )
            )
    for copy in copies:
        copy.start()
    for copy in copies:
        copy.wait()
    for head in range(width // HD):
        cols = slice(head * HD, (head + 1) * HD)
        products_ref[head] = dot_transposed(q_ref[:, cols], keys_ref[:, cols])


def dot_transposed(a, b):
    return lax.dot_general(
        a, b, (((1,), (1,)), ((), ())), preferred_element_type=jnp.float32
    )


def attention_kernel(scale, q_ref, products_ref, values_ref, *refs):
    block_refs, out_ref = refs[:-1], refs[-1]
    rows, width = q_ref.shape
    blocks = jnp.concatenate([ref[...] for ref in block_refs], axis=0)
    heads = [slice(at, at + HD) for at in range(0, width, HD)]
    products = [
        products_ref[n] + dot_transposed(q_ref[:, cols], blocks[:, cols])
        for n, cols in enumerate(heads)
    ]
    highest = [jnp.max(p, axis=1, keepdims=True) for p in products]
    weights = [jnp.exp((p - h) * scale) for p, h in zip(products, highest)]
    totals = [jnp.sum(w, axis=1, keepdims=True) for w in weights]
    high = [w.astype(jnp.bfloat16) for w in weights]
    low = [(w - h.astype(jnp.float32)).astype(jnp.bfloat16) for w, h in zip(weights, high)]
    sums = [
        jnp.dot(
            jnp.concatenate([high[n], low[n]], axis=0),
            jnp.concatenate(
                [values_ref[:, cols], blocks[:, width + cols.start : width + cols.stop]], axis=1
            ),
            preferred_element_type=jnp.float32,
        )
        for n, cols in enumerate(heads)
    ]
    for cols, total, both in zip(heads, totals, sums):
        both = both[:rows] + both[rows:]
        out_ref[:, cols] = ((both[:, :HD] + both[:, HD:]) / total).astype(jnp.bfloat16)


def block_dot(a_ref, weight_ref, start, columns):
    if start is None:
        weight = weight_ref[...]
    else:
        weight = weight_ref[:, pl.ds(pl.multiple_of(start, LANES), columns)]
    return jnp.dot(a_ref[...], weight, preferred_element_type=jnp.float32)


def products(start, columns, refs):
    total = 0.0
    for attended_ref, weight_ref in zip(refs[::2], refs[1::2]):
        total = total + block_dot(attended_ref, weight_ref, start, columns)
    return total


def sent_term_kernel(start, *refs):
    out_ref = refs[-1]
    total = products(start(), out_ref.shape[1], refs[:-1])
    out_ref[...] = total.astype(jnp.bfloat16)


def base_kernel(start, hidden_ref, gate_ref, *refs):
    out_ref = refs[-1]
    total = products(start(), out_ref.shape[1], refs[:-1])
    out_ref[...] = hidden_ref[...].astype(jnp.float32) + gate_ref[...] * total


def final_kernel(early, blocks, base_ref, gate_ref, *refs):
    arrived_refs, (out_ref, result, sems) = refs[:-3], refs[-3:]
    rows = base_ref.shape[0] // blocks
    copies = []
    for n in range(blocks):
        at = slice(n * rows, (n + 1) * rows)
        total = 0.0
        for ref in arrived_refs:
            total = total + ref[at, :].astype(jnp.float32)
        if early:
            result[at, :early] = base_ref[at, :early].astype(jnp.bfloat16)
        total = base_ref[at, early:] + gate_ref[:, early:] * total
        result[at, early:] = total.astype(jnp.bfloat16)
        copies.append(pltpu.make_async_copy(result.at[at, :], out_ref.at[at, :], sems.at[n]))
        copies[n].start()
    for copy in copies:
        copy.wait()


def pack_kernel(early, attended_ref, weight_ref, out_ref):
    rows, width = attended_ref.shape
    other = pl.multiple_of((1 - lax.axis_index("sub")) * early, LANES)
    out_ref[:rows, :width] = attended_ref[...]
    out_ref[rows:, :early] = weight_ref[:, pl.ds(other, early)]


def early_kernel(early, base_ref, gate_ref, attended_ref, weight_ref, packed_ref, out_ref):
    rows, width = attended_ref.shape
    mine = pl.multiple_of(lax.axis_index("sub") * early, LANES)
    total = jnp.dot(
        attended_ref[...],
        weight_ref[:, pl.ds(mine, early)],
        preferred_element_type=jnp.float32,
    ) + jnp.dot(
        packed_ref[:rows, :width], packed_ref[rows:, :early], preferred_element_type=jnp.float32
    )
    out_ref[...] = base_ref[...]
    out_ref[:, :early] = base_ref[:, :early] + gate_ref[:, :early] * total


def solution(mesh):
    patches, heads, subs = mesh.shape["patch"], mesh.shape["head"], mesh.shape["sub"]

    def per_device(
        queries, held_keys, held_values, key_change, value_change, out_weight, hidden_in, gate
    ):
        rows, width = queries.shape
        columns = hidden_in.shape[1]

        early = EARLY if heads == 2 and columns % LANES == 0 and columns > 4 * LANES else 0
        if early:
            with jax.named_scope("early_weight"):
                early_weight = call(
                    functools.partial(early_weight_kernel, subs, columns, early),
                    jax.ShapeDtypeStruct((width, subs * early), jnp.bfloat16),
                    [ANYWHERE],
                    IN_VMEM,
                    "early_weight",
                    moved=4 * width * subs * early,
                    scratch_shapes=[pltpu.SemaphoreType.DMA((subs,))],
                )(in_hbm(out_weight))
                key_change, value_change, early_weight = lax.optimization_barrier(
                    (key_change, value_change, early_weight)
                )

        with jax.named_scope("residual_gather"):
            low = jnp.float32(-jnp.inf)
            residual = jnp.maximum(
                lax.pad(key_change, low, ((0, 0, 0), (0, width, 0))),
                lax.pad(value_change, low, ((0, 0, 0), (width, 0, 0))),
            ).astype(jnp.bfloat16)
            blocks = gather(residual, patches, subs)

        with jax.named_scope("weight_swap"):
            weights = [out_weight] + [shift(out_weight, "sub", subs, i) for i in range(1, subs)]

        if early:
            with jax.named_scope("early_weight"):
                early_weight = shift(early_weight, "head", heads, 1)

        def weight_and_start(i, step, skip=0):
            def start():
                to = lax.rem(lax.axis_index("head") + step, heads) * subs + lax.axis_index("sub")
                return to * columns + skip

            if columns % LANES == 0:
                return weights[i], start
            return lax.dynamic_slice(weights[i], (0, start()), (width, columns)), lambda: None

        def pairs_and_start(step, skip=0):
            pairs = [
                x
                for i in range(subs)
                for x in (attended_parts[i], weight_and_start(i, step, skip)[0])
            ]
            return pairs, weight_and_start(0, step, skip)[1]

        tokens = rows * patches
        with jax.named_scope("attention"):
            staged_queries, products, values = call(
                functools.partial(stage_kernel, patches, subs),
                [
                    jax.ShapeDtypeStruct((rows, width), jnp.bfloat16),
                    jax.ShapeDtypeStruct((width // HD, rows, tokens), jnp.float32),
                    jax.ShapeDtypeStruct((tokens, width), jnp.bfloat16),
                ],
                [ANYWHERE] * 3,
                [IN_VMEM] * 3,
                "stage",
                flops=2_000_000_000,
                scratch_shapes=[
                    pltpu.VMEM((tokens, width), jnp.bfloat16),
                    pltpu.SemaphoreType.DMA((1 + 2 * patches,)),
                ],
            )(in_hbm(queries), in_hbm(held_keys), in_hbm(held_values))
            attended = call(
                functools.partial(attention_kernel, 1.0 / math.sqrt(HD)),
                jax.ShapeDtypeStruct((rows, width), jnp.bfloat16),
                [IN_VMEM] * (3 + len(blocks)),
                IN_VMEM,
                "attention",
                flops=2_000_000_000,
            )(staged_queries, products, values, *blocks)

        with jax.named_scope("attended_swap"):
            attended_parts = [attended] + [
                shift(attended, "sub", subs, i) for i in range(1, subs)
            ]
            if early:
                other_attended = shift(attended, "head", heads, 1)

        term = jax.ShapeDtypeStruct((rows, columns), jnp.float32)
        sent = jax.ShapeDtypeStruct((rows, columns - early), jnp.bfloat16)
        product_flops = 2 * rows * width * columns
        with jax.named_scope("projection"):
            arrived = []
            for step in range(1, heads):
                pairs, start = pairs_and_start(step, early)
                total = call(
                    functools.partial(sent_term_kernel, start),
                    sent,
                    [IN_VMEM] * len(pairs),
                    IN_VMEM,
                    "sent_term",
                    2 * product_flops,
                )(*pairs)
                arrived.append(shift(total, "head", heads, step))
            gate_row = gate.reshape(1, columns)
            pairs, start = pairs_and_start(0)
            base = call(
                functools.partial(base_kernel, start),
                term,
                [IN_VMEM] * (2 + len(pairs)),
                IN_VMEM,
                "base",
                2 * product_flops,
            )(hidden_in, gate_row, *pairs)
            if early:
                packed = call(
                    functools.partial(pack_kernel, early),
                    jax.ShapeDtypeStruct((rows + width, max(early, width)), jnp.bfloat16),
                    [IN_VMEM] * 2,
                    IN_VMEM,
                    "pack",
                )(other_attended, early_weight)
                packed = shift(packed, "sub", subs, 1)
                base = call(
                    functools.partial(early_kernel, early),
                    term,
                    [IN_VMEM] * 5,
                    IN_VMEM,
                    "early",
                    product_flops // 2,
                )(base, gate_row, other_attended, early_weight, packed)
            row_blocks = 3 if rows % (3 * ROW_TILE) == 0 else 1
            return call(
                functools.partial(final_kernel, early, row_blocks),
                jax.ShapeDtypeStruct((rows, columns), jnp.bfloat16),
                [IN_VMEM] * (2 + len(arrived)),
                ANYWHERE,
                "final",
                moved=rows * columns * 8,
                scratch_shapes=[
                    pltpu.VMEM((rows, columns), jnp.bfloat16),
                    pltpu.SemaphoreType.DMA((row_blocks,)),
                ],
            )(base, gate_row, *arrived)

    in_specs = (
        P(("groups", "patch"), ("head", "sub")),
        P("groups", ("head", "sub")),
        P("groups", ("head", "sub")),
        P(("groups", "patch"), ("head", "sub")),
        P(("groups", "patch"), ("head", "sub")),
        P(("head", "sub"), None),
        P(("groups", "patch"), ("head", "sub")),
        P(("groups", "head", "sub")),
    )
    out_specs = P(("groups", "patch"), ("head", "sub"))
    return jax.shard_map(
        per_device, mesh=mesh, in_specs=in_specs, out_specs=out_specs, check_vma=False
    )
```

```python
import functools
import math

import jax
import jax.numpy as jnp
from jax import lax
from jax.experimental import pallas as pl
from jax.experimental.pallas import tpu as pltpu
from jax.sharding import PartitionSpec as P

HD = 128
LANES = 128
ROW_TILE = 16
VMEM_LIMIT = 12 * 1024 * 1024
EARLY = 256

IN_VMEM = pl.BlockSpec(memory_space=pltpu.VMEM)
ANYWHERE = pl.BlockSpec(memory_space=pl.ANY)


def call(
    kernel,
    out_shape,
    in_specs,
    out_specs,
    name,
    flops=0,
    moved=0,
    scratch_shapes=(),
    vmem=VMEM_LIMIT,
):
    return pl.pallas_call(
        kernel,
        out_shape=out_shape,
        in_specs=in_specs,
        out_specs=out_specs,
        scratch_shapes=scratch_shapes,
        name=name,
        cost_estimate=pl.CostEstimate(flops=flops, bytes_accessed=moved, transcendentals=0),
        compiler_params=pltpu.CompilerParams(vmem_limit_bytes=vmem),
    )


def in_hbm(array):
    return pltpu.with_memory_space_constraint(array, pltpu.HBM)


def shift(array, axis, size, step):
    return lax.ppermute(array, axis, [(i, (i + step) % size) for i in range(size)])


LINE_OF_FOUR = (
    ((1, 2, 3, 0), (2, 0, 3, 1)),
    ((3, 0, 1, 2), (3, 2, 1, 0)),
    ((2, 3, 0, 1), (1, 3, 0, 2)),
)


def gather_targets(patches, subs):
    if patches == 4 and subs == 2:
        return LINE_OF_FOUR
    return [
        [[(i + step) % patches for i in range(patches)]] * subs
        for step in range(patches - 1, 0, -1)
    ]


def gather(own, patches, subs):
    blocks = [own]
    for targets in gather_targets(patches, subs):
        pairs = [
            (place * subs + sub, targets[sub][place] * subs + sub)
            for place in range(patches)
            for sub in range(subs)
        ]
        blocks.append(lax.ppermute(own, ("patch", "sub"), pairs))
    return blocks


def gather_sources(patches, subs):
    place, core = lax.axis_index("patch"), lax.axis_index("sub")
    sources = [place]
    for targets in gather_targets(patches, subs):
        value = jnp.int32(0)
        for sub in range(subs):
            for source, target in enumerate(targets[sub]):
                here = jnp.logical_and(place == target, core == sub)
                value = jnp.where(here, jnp.int32(source), value)
        sources.append(value)
    return sources


def early_weight_kernel(subs, columns, early, weight_ref, out_ref, sems):
    chip = (1 - lax.axis_index("head")) * subs
    copies = []
    for sub in range(subs):
        at = pl.multiple_of((chip + sub) * columns, LANES)
        copies.append(
            pltpu.make_async_copy(
                weight_ref.at[:, pl.ds(at, early)],
                out_ref.at[:, pl.ds(sub * early, early)],
                sems.at[sub],
            )
        )
    for copy in copies:
        copy.start()
    for copy in copies:
        copy.wait()


def stage_kernel(
    patches, subs, q_hbm, held_k_hbm, held_v_hbm, q_ref, products_ref, values_ref, keys_ref, sems
):
    rows, width = q_ref.shape
    sources = gather_sources(patches, subs)
    copies = [pltpu.make_async_copy(q_hbm, q_ref, sems.at[0])]
    for i, source in enumerate(sources):
        at = pl.multiple_of(source * rows, rows)
        for n, (held, ref) in enumerate(((held_k_hbm, keys_ref), (held_v_hbm, values_ref))):
            copies.append(
                pltpu.make_async_copy(
                    held.at[pl.ds(at, rows), :],
                    ref.at[i * rows : (i + 1) * rows, :],
                    sems.at[1 + 2 * i + n],
                )
            )
    for copy in copies:
        copy.start()
    for copy in copies:
        copy.wait()
    for head in range(width // HD):
        cols = slice(head * HD, (head + 1) * HD)
        products_ref[head] = dot_transposed(q_ref[:, cols], keys_ref[:, cols])


def dot_transposed(a, b):
    return lax.dot_general(
        a, b, (((1,), (1,)), ((), ())), preferred_element_type=jnp.float32
    )


def attention_kernel(scale, q_ref, products_ref, values_ref, *refs):
    block_refs, out_ref = refs[:-1], refs[-1]
    rows, width = q_ref.shape
    blocks = jnp.concatenate([ref[...] for ref in block_refs], axis=0)
    heads = [slice(at, at + HD) for at in range(0, width, HD)]
    products = [
        products_ref[n] + dot_transposed(q_ref[:, cols], blocks[:, cols])
        for n, cols in enumerate(heads)
    ]
    highest = [jnp.max(p, axis=1, keepdims=True) for p in products]
    weights = [jnp.exp((p - h) * scale) for p, h in zip(products, highest)]
    totals = [jnp.sum(w, axis=1, keepdims=True) for w in weights]
    high = [w.astype(jnp.bfloat16) for w in weights]
    low = [(w - h.astype(jnp.float32)).astype(jnp.bfloat16) for w, h in zip(weights, high)]
    sums = [
        jnp.dot(
            jnp.concatenate([high[n], low[n]], axis=0),
            jnp.concatenate(
                [values_ref[:, cols], blocks[:, width + cols.start : width + cols.stop]], axis=1
            ),
            preferred_element_type=jnp.float32,
        )
        for n, cols in enumerate(heads)
    ]
    for cols, total, both in zip(heads, totals, sums):
        both = both[:rows] + both[rows:]
        out_ref[:, cols] = ((both[:, :HD] + both[:, HD:]) / total).astype(jnp.bfloat16)


def block_dot(a_ref, weight_ref, start, columns):
    if start is None:
        weight = weight_ref[...]
    else:
        weight = weight_ref[:, pl.ds(pl.multiple_of(start, LANES), columns)]
    return jnp.dot(a_ref[...], weight, preferred_element_type=jnp.float32)


def products(start, columns, refs):
    total = 0.0
    for attended_ref, weight_ref in zip(refs[::2], refs[1::2]):
        total = total + block_dot(attended_ref, weight_ref, start, columns)
    return total


def sent_term_kernel(start, *refs):
    out_ref = refs[-1]
    total = products(start(), out_ref.shape[1], refs[:-1])
    out_ref[...] = total.astype(jnp.bfloat16)


def base_kernel(start, hidden_ref, gate_ref, *refs):
    out_ref = refs[-1]
    total = products(start(), out_ref.shape[1], refs[:-1])
    out_ref[...] = hidden_ref[...].astype(jnp.float32) + gate_ref[...] * total


def final_kernel(early, blocks, base_ref, gate_ref, *refs):
    arrived_refs, (out_ref, result, sems) = refs[:-3], refs[-3:]
    rows = base_ref.shape[0] // blocks
    copies = []
    for n in range(blocks):
        at = slice(n * rows, (n + 1) * rows)
        total = 0.0
        for ref in arrived_refs:
            total = total + ref[at, :].astype(jnp.float32)
        if early:
            result[at, :early] = base_ref[at, :early].astype(jnp.bfloat16)
        total = base_ref[at, early:] + gate_ref[:, early:] * total
        result[at, early:] = total.astype(jnp.bfloat16)
        copies.append(pltpu.make_async_copy(result.at[at, :], out_ref.at[at, :], sems.at[n]))
        copies[n].start()
    for copy in copies:
        copy.wait()


def pack_kernel(early, attended_ref, weight_ref, out_ref):
    rows, width = attended_ref.shape
    other = pl.multiple_of((1 - lax.axis_index("sub")) * early, LANES)
    out_ref[:rows, :width] = attended_ref[...]
    out_ref[rows:, :early] = weight_ref[:, pl.ds(other, early)]


def early_kernel(early, base_ref, gate_ref, attended_ref, weight_ref, packed_ref, out_ref):
    rows, width = attended_ref.shape
    mine = pl.multiple_of(lax.axis_index("sub") * early, LANES)
    total = jnp.dot(
        attended_ref[...],
        weight_ref[:, pl.ds(mine, early)],
        preferred_element_type=jnp.float32,
    ) + jnp.dot(
        packed_ref[:rows, :width], packed_ref[rows:, :early], preferred_element_type=jnp.float32
    )
    out_ref[...] = base_ref[...]
    out_ref[:, :early] = base_ref[:, :early] + gate_ref[:, :early] * total


def solution(mesh):
    patches, heads, subs = mesh.shape["patch"], mesh.shape["head"], mesh.shape["sub"]

    def per_device(
        queries, held_keys, held_values, key_change, value_change, out_weight, hidden_in, gate
    ):
        rows, width = queries.shape
        columns = hidden_in.shape[1]

        early = EARLY if heads == 2 and columns % LANES == 0 and columns > 4 * LANES else 0
        if early:
            with jax.named_scope("early_weight"):
                early_weight = call(
                    functools.partial(early_weight_kernel, subs, columns, early),
                    jax.ShapeDtypeStruct((width, subs * early), jnp.bfloat16),
                    [ANYWHERE],
                    IN_VMEM,
                    "early_weight",
                    moved=4 * width * subs * early,
                    scratch_shapes=[pltpu.SemaphoreType.DMA((subs,))],
                )(in_hbm(out_weight))
                key_change, value_change, early_weight = lax.optimization_barrier(
                    (key_change, value_change, early_weight)
                )

        with jax.named_scope("residual_gather"):
            low = jnp.float32(-jnp.inf)
            residual = jnp.maximum(
                lax.pad(key_change, low, ((0, 0, 0), (0, width, 0))),
                lax.pad(value_change, low, ((0, 0, 0), (width, 0, 0))),
            ).astype(jnp.bfloat16)
            blocks = gather(residual, patches, subs)

        with jax.named_scope("weight_swap"):
            weights = [out_weight] + [shift(out_weight, "sub", subs, i) for i in range(1, subs)]

        if early:
            with jax.named_scope("early_weight"):
                early_weight = shift(early_weight, "head", heads, 1)

        def weight_and_start(i, step, skip=0):
            def start():
                to = lax.rem(lax.axis_index("head") + step, heads) * subs + lax.axis_index("sub")
                return to * columns + skip

            if columns % LANES == 0:
                return weights[i], start
            return lax.dynamic_slice(weights[i], (0, start()), (width, columns)), lambda: None

        def pairs_and_start(step, skip=0):
            pairs = [
                x
                for i in range(subs)
                for x in (attended_parts[i], weight_and_start(i, step, skip)[0])
            ]
            return pairs, weight_and_start(0, step, skip)[1]

        tokens = rows * patches
        with jax.named_scope("attention"):
            staged_queries, products, values = call(
                functools.partial(stage_kernel, patches, subs),
                [
                    jax.ShapeDtypeStruct((rows, width), jnp.bfloat16),
                    jax.ShapeDtypeStruct((width // HD, rows, tokens), jnp.float32),
                    jax.ShapeDtypeStruct((tokens, width), jnp.bfloat16),
                ],
                [ANYWHERE] * 3,
                [IN_VMEM] * 3,
                "stage",
                flops=2_000_000_000,
                scratch_shapes=[
                    pltpu.VMEM((tokens, width), jnp.bfloat16),
                    pltpu.SemaphoreType.DMA((1 + 2 * patches,)),
                ],
            )(in_hbm(queries), in_hbm(held_keys), in_hbm(held_values))
            attended = call(
                functools.partial(attention_kernel, 1.0 / math.sqrt(HD)),
                jax.ShapeDtypeStruct((rows, width), jnp.bfloat16),
                [IN_VMEM] * (3 + len(blocks)),
                IN_VMEM,
                "attention",
                flops=2_000_000_000,
            )(staged_queries, products, values, *blocks)

        with jax.named_scope("attended_swap"):
            attended_parts = [attended] + [
                shift(attended, "sub", subs, i) for i in range(1, subs)
            ]
            if early:
                other_attended = shift(attended, "head", heads, 1)

        term = jax.ShapeDtypeStruct((rows, columns), jnp.float32)
        sent = jax.ShapeDtypeStruct((rows, columns - early), jnp.bfloat16)
        product_flops = 2 * rows * width * columns
        with jax.named_scope("projection"):
            arrived = []
            for step in range(1, heads):
                pairs, start = pairs_and_start(step, early)
                total = call(
                    functools.partial(sent_term_kernel, start),
                    sent,
                    [IN_VMEM] * len(pairs),
                    IN_VMEM,
                    "sent_term",
                    2 * product_flops,
                )(*pairs)
                arrived.append(shift(total, "head", heads, step))
            gate_row = gate.reshape(1, columns)
            pairs, start = pairs_and_start(0)
            base = call(
                functools.partial(base_kernel, start),
                term,
                [IN_VMEM] * (2 + len(pairs)),
                IN_VMEM,
                "base",
                2 * product_flops,
            )(hidden_in, gate_row, *pairs)
            if early:
                packed = call(
                    functools.partial(pack_kernel, early),
                    jax.ShapeDtypeStruct((rows + width, max(early, width)), jnp.bfloat16),
                    [IN_VMEM] * 2,
                    IN_VMEM,
                    "pack",
                )(other_attended, early_weight)
                packed = shift(packed, "sub", subs, 1)
                base = call(
                    functools.partial(early_kernel, early),
                    term,
                    [IN_VMEM] * 5,
                    IN_VMEM,
                    "early",
                    product_flops // 2,
                )(base, gate_row, other_attended, early_weight, packed)
            row_blocks = 3 if rows % (3 * ROW_TILE) == 0 else 1
            return call(
                functools.partial(final_kernel, early, row_blocks),
                jax.ShapeDtypeStruct((rows, columns), jnp.bfloat16),
                [IN_VMEM] * (2 + len(arrived)),
                ANYWHERE,
                "final",
                moved=rows * columns * 8,
                scratch_shapes=[
                    pltpu.VMEM((rows, columns), jnp.bfloat16),
                    pltpu.SemaphoreType.DMA((row_blocks,)),
                ],
            )(base, gate_row, *arrived)

    in_specs = (
        P(("groups", "patch"), ("head", "sub")),
        P("groups", ("head", "sub")),
        P("groups", ("head", "sub")),
        P(("groups", "patch"), ("head", "sub")),
        P(("groups", "patch"), ("head", "sub")),
        P(("head", "sub"), None),
        P(("groups", "patch"), ("head", "sub")),
        P(("groups", "head", "sub")),
    )
    out_specs = P(("groups", "patch"), ("head", "sub"))
    return jax.shard_map(
        per_device, mesh=mesh, in_specs=in_specs, out_specs=out_specs, check_vma=False
    )
```

```python
import functools
import math

import jax
import jax.numpy as jnp
from jax import lax
from jax.experimental import pallas as pl
from jax.experimental.pallas import tpu as pltpu
from jax.sharding import PartitionSpec as P

HD = 128
LANES = 128
ROW_TILE = 16
VMEM_LIMIT = 12 * 1024 * 1024
EARLY = 256

IN_VMEM = pl.BlockSpec(memory_space=pltpu.VMEM)
ANYWHERE = pl.BlockSpec(memory_space=pl.ANY)


def call(
    kernel,
    out_shape,
    in_specs,
    out_specs,
    name,
    flops=0,
    moved=0,
    scratch_shapes=(),
    vmem=VMEM_LIMIT,
):
    return pl.pallas_call(
        kernel,
        out_shape=out_shape,
        in_specs=in_specs,
        out_specs=out_specs,
        scratch_shapes=scratch_shapes,
        name=name,
        cost_estimate=pl.CostEstimate(flops=flops, bytes_accessed=moved, transcendentals=0),
        compiler_params=pltpu.CompilerParams(vmem_limit_bytes=vmem),
    )


def in_hbm(array):
    return pltpu.with_memory_space_constraint(array, pltpu.HBM)


def shift(array, axis, size, step):
    return lax.ppermute(array, axis, [(i, (i + step) % size) for i in range(size)])


LINE_OF_FOUR = (
    ((2, 0, 3, 1), (3, 0, 1, 2)),
    ((3, 2, 1, 0), (1, 2, 3, 0)),
    ((1, 3, 0, 2), (2, 3, 0, 1)),
)


def gather_targets(patches, subs):
    if patches == 4 and subs == 2:
        return LINE_OF_FOUR
    return [
        [[(i + step) % patches for i in range(patches)]] * subs
        for step in range(patches - 1, 0, -1)
    ]


def gather(own, patches, subs):
    blocks = [own]
    for targets in gather_targets(patches, subs):
        pairs = [
            (place * subs + sub, targets[sub][place] * subs + sub)
            for place in range(patches)
            for sub in range(subs)
        ]
        blocks.append(lax.ppermute(own, ("patch", "sub"), pairs))
    return blocks


def gather_sources(patches, subs):
    place, core = lax.axis_index("patch"), lax.axis_index("sub")
    sources = [place]
    for targets in gather_targets(patches, subs):
        value = jnp.int32(0)
        for sub in range(subs):
            for source, target in enumerate(targets[sub]):
                here = jnp.logical_and(place == target, core == sub)
                value = jnp.where(here, jnp.int32(source), value)
        sources.append(value)
    return sources


def early_weight_kernel(subs, columns, early, weight_ref, out_ref, sems):
    chip = (1 - lax.axis_index("head")) * subs
    copies = []
    for sub in range(subs):
        at = pl.multiple_of((chip + sub) * columns, LANES)
        copies.append(
            pltpu.make_async_copy(
                weight_ref.at[:, pl.ds(at, early)],
                out_ref.at[:, pl.ds(sub * early, early)],
                sems.at[sub],
            )
        )
    for copy in copies:
        copy.start()
    for copy in copies:
        copy.wait()


def stage_kernel(
    patches, subs, q_hbm, held_k_hbm, held_v_hbm, q_ref, products_ref, values_ref, keys_ref, sems
):
    rows, width = q_ref.shape
    sources = gather_sources(patches, subs)
    copies = [pltpu.make_async_copy(q_hbm, q_ref, sems.at[0])]
    for i, source in enumerate(sources):
        at = pl.multiple_of(source * rows, rows)
        for n, (held, ref) in enumerate(((held_k_hbm, keys_ref), (held_v_hbm, values_ref))):
            copies.append(
                pltpu.make_async_copy(
                    held.at[pl.ds(at, rows), :],
                    ref.at[i * rows : (i + 1) * rows, :],
                    sems.at[1 + 2 * i + n],
                )
            )
    for copy in copies:
        copy.start()
    for copy in copies:
        copy.wait()
    for head in range(width // HD):
        cols = slice(head * HD, (head + 1) * HD)
        products_ref[head] = dot_transposed(q_ref[:, cols], keys_ref[:, cols])


def dot_transposed(a, b):
    return lax.dot_general(
        a, b, (((1,), (1,)), ((), ())), preferred_element_type=jnp.float32
    )


def attention_kernel(scale, q_ref, products_ref, values_ref, *refs):
    block_refs, out_ref = refs[:-1], refs[-1]
    rows, width = q_ref.shape
    blocks = jnp.concatenate([ref[...] for ref in block_refs], axis=0)
    heads = [slice(at, at + HD) for at in range(0, width, HD)]
    products = [
        products_ref[n] + dot_transposed(q_ref[:, cols], blocks[:, cols])
        for n, cols in enumerate(heads)
    ]
    highest = [jnp.max(p, axis=1, keepdims=True) for p in products]
    weights = [jnp.exp((p - h) * scale) for p, h in zip(products, highest)]
    totals = [jnp.sum(w, axis=1, keepdims=True) for w in weights]
    high = [w.astype(jnp.bfloat16) for w in weights]
    low = [(w - h.astype(jnp.float32)).astype(jnp.bfloat16) for w, h in zip(weights, high)]
    sums = [
        jnp.dot(
            jnp.concatenate([high[n], low[n]], axis=0),
            jnp.concatenate(
                [values_ref[:, cols], blocks[:, width + cols.start : width + cols.stop]], axis=1
            ),
            preferred_element_type=jnp.float32,
        )
        for n, cols in enumerate(heads)
    ]
    for cols, total, both in zip(heads, totals, sums):
        both = both[:rows] + both[rows:]
        out_ref[:, cols] = ((both[:, :HD] + both[:, HD:]) / total).astype(jnp.bfloat16)


def block_dot(a_ref, weight_ref, start, columns):
    if start is None:
        weight = weight_ref[...]
    else:
        weight = weight_ref[:, pl.ds(pl.multiple_of(start, LANES), columns)]
    return jnp.dot(a_ref[...], weight, preferred_element_type=jnp.float32)


def products(start, columns, refs):
    total = 0.0
    for attended_ref, weight_ref in zip(refs[::2], refs[1::2]):
        total = total + block_dot(attended_ref, weight_ref, start, columns)
    return total


def sent_term_kernel(start, *refs):
    out_ref = refs[-1]
    total = products(start(), out_ref.shape[1], refs[:-1])
    out_ref[...] = total.astype(jnp.bfloat16)


def base_kernel(start, hidden_ref, gate_ref, *refs):
    out_ref = refs[-1]
    total = products(start(), out_ref.shape[1], refs[:-1])
    out_ref[...] = hidden_ref[...].astype(jnp.float32) + gate_ref[...] * total


def final_kernel(early, blocks, base_ref, gate_ref, *refs):
    arrived_refs, (out_ref, result, sems) = refs[:-3], refs[-3:]
    rows = base_ref.shape[0] // blocks
    copies = []
    for n in range(blocks):
        at = slice(n * rows, (n + 1) * rows)
        total = 0.0
        for ref in arrived_refs:
            total = total + ref[at, :].astype(jnp.float32)
        if early:
            result[at, :early] = base_ref[at, :early].astype(jnp.bfloat16)
        total = base_ref[at, early:] + gate_ref[:, early:] * total
        result[at, early:] = total.astype(jnp.bfloat16)
        copies.append(pltpu.make_async_copy(result.at[at, :], out_ref.at[at, :], sems.at[n]))
        copies[n].start()
    for copy in copies:
        copy.wait()


def pack_kernel(early, attended_ref, weight_ref, out_ref):
    rows, width = attended_ref.shape
    other = pl.multiple_of((1 - lax.axis_index("sub")) * early, LANES)
    out_ref[:rows, :width] = attended_ref[...]
    out_ref[rows:, :early] = weight_ref[:, pl.ds(other, early)]


def early_kernel(early, base_ref, gate_ref, attended_ref, weight_ref, packed_ref, out_ref):
    rows, width = attended_ref.shape
    mine = pl.multiple_of(lax.axis_index("sub") * early, LANES)
    total = jnp.dot(
        attended_ref[...],
        weight_ref[:, pl.ds(mine, early)],
        preferred_element_type=jnp.float32,
    ) + jnp.dot(
        packed_ref[:rows, :width], packed_ref[rows:, :early], preferred_element_type=jnp.float32
    )
    out_ref[...] = base_ref[...]
    out_ref[:, :early] = base_ref[:, :early] + gate_ref[:, :early] * total


def solution(mesh):
    patches, heads, subs = mesh.shape["patch"], mesh.shape["head"], mesh.shape["sub"]

    def per_device(
        queries, held_keys, held_values, key_change, value_change, out_weight, hidden_in, gate
    ):
        rows, width = queries.shape
        columns = hidden_in.shape[1]

        early = EARLY if heads == 2 and columns % LANES == 0 and columns > 4 * LANES else 0
        if early:
            with jax.named_scope("early_weight"):
                early_weight = call(
                    functools.partial(early_weight_kernel, subs, columns, early),
                    jax.ShapeDtypeStruct((width, subs * early), jnp.bfloat16),
                    [ANYWHERE],
                    IN_VMEM,
                    "early_weight",
                    moved=4 * width * subs * early,
                    scratch_shapes=[pltpu.SemaphoreType.DMA((subs,))],
                )(in_hbm(out_weight))
                key_change, value_change, early_weight = lax.optimization_barrier(
                    (key_change, value_change, early_weight)
                )

        with jax.named_scope("residual_gather"):
            low = jnp.float32(-jnp.inf)
            residual = jnp.maximum(
                lax.pad(key_change, low, ((0, 0, 0), (0, width, 0))),
                lax.pad(value_change, low, ((0, 0, 0), (width, 0, 0))),
            ).astype(jnp.bfloat16)
            blocks = gather(residual, patches, subs)

        with jax.named_scope("weight_swap"):
            weights = [out_weight] + [shift(out_weight, "sub", subs, i) for i in range(1, subs)]

        if early:
            with jax.named_scope("early_weight"):
                early_weight = shift(early_weight, "head", heads, 1)

        def weight_and_start(i, step, skip=0):
            def start():
                to = lax.rem(lax.axis_index("head") + step, heads) * subs + lax.axis_index("sub")
                return to * columns + skip

            if columns % LANES == 0:
                return weights[i], start
            return lax.dynamic_slice(weights[i], (0, start()), (width, columns)), lambda: None

        def pairs_and_start(step, skip=0):
            pairs = [
                x
                for i in range(subs)
                for x in (attended_parts[i], weight_and_start(i, step, skip)[0])
            ]
            return pairs, weight_and_start(0, step, skip)[1]

        tokens = rows * patches
        with jax.named_scope("attention"):
            staged_queries, products, values = call(
                functools.partial(stage_kernel, patches, subs),
                [
                    jax.ShapeDtypeStruct((rows, width), jnp.bfloat16),
                    jax.ShapeDtypeStruct((width // HD, rows, tokens), jnp.float32),
                    jax.ShapeDtypeStruct((tokens, width), jnp.bfloat16),
                ],
                [ANYWHERE] * 3,
                [IN_VMEM] * 3,
                "stage",
                flops=2_000_000_000,
                scratch_shapes=[
                    pltpu.VMEM((tokens, width), jnp.bfloat16),
                    pltpu.SemaphoreType.DMA((1 + 2 * patches,)),
                ],
            )(in_hbm(queries), in_hbm(held_keys), in_hbm(held_values))
            attended = call(
                functools.partial(attention_kernel, 1.0 / math.sqrt(HD)),
                jax.ShapeDtypeStruct((rows, width), jnp.bfloat16),
                [IN_VMEM] * (3 + len(blocks)),
                IN_VMEM,
                "attention",
                flops=2_000_000_000,
            )(staged_queries, products, values, *blocks)

        with jax.named_scope("attended_swap"):
            attended_parts = [attended] + [
                shift(attended, "sub", subs, i) for i in range(1, subs)
            ]
            if early:
                other_attended = shift(attended, "head", heads, 1)

        term = jax.ShapeDtypeStruct((rows, columns), jnp.float32)
        sent = jax.ShapeDtypeStruct((rows, columns - early), jnp.bfloat16)
        product_flops = 2 * rows * width * columns
        with jax.named_scope("projection"):
            arrived = []
            for step in range(1, heads):
                pairs, start = pairs_and_start(step, early)
                total = call(
                    functools.partial(sent_term_kernel, start),
                    sent,
                    [IN_VMEM] * len(pairs),
                    IN_VMEM,
                    "sent_term",
                    2 * product_flops,
                )(*pairs)
                arrived.append(shift(total, "head", heads, step))
            gate_row = gate.reshape(1, columns)
            pairs, start = pairs_and_start(0)
            base = call(
                functools.partial(base_kernel, start),
                term,
                [IN_VMEM] * (2 + len(pairs)),
                IN_VMEM,
                "base",
                2 * product_flops,
            )(hidden_in, gate_row, *pairs)
            if early:
                packed = call(
                    functools.partial(pack_kernel, early),
                    jax.ShapeDtypeStruct((rows + width, max(early, width)), jnp.bfloat16),
                    [IN_VMEM] * 2,
                    IN_VMEM,
                    "pack",
                )(other_attended, early_weight)
                packed = shift(packed, "sub", subs, 1)
                base = call(
                    functools.partial(early_kernel, early),
                    term,
                    [IN_VMEM] * 5,
                    IN_VMEM,
                    "early",
                    product_flops // 2,
                )(base, gate_row, other_attended, early_weight, packed)
            row_blocks = 3 if rows % (3 * ROW_TILE) == 0 else 1
            return call(
                functools.partial(final_kernel, early, row_blocks),
                jax.ShapeDtypeStruct((rows, columns), jnp.bfloat16),
                [IN_VMEM] * (2 + len(arrived)),
                ANYWHERE,
                "final",
                moved=rows * columns * 8,
                scratch_shapes=[
                    pltpu.VMEM((rows, columns), jnp.bfloat16),
                    pltpu.SemaphoreType.DMA((row_blocks,)),
                ],
            )(base, gate_row, *arrived)

    in_specs = (
        P(("groups", "patch"), ("head", "sub")),
        P("groups", ("head", "sub")),
        P("groups", ("head", "sub")),
        P(("groups", "patch"), ("head", "sub")),
        P(("groups", "patch"), ("head", "sub")),
        P(("head", "sub"), None),
        P(("groups", "patch"), ("head", "sub")),
        P(("groups", "head", "sub")),
    )
    out_specs = P(("groups", "patch"), ("head", "sub"))
    return jax.shard_map(
        per_device, mesh=mesh, in_specs=in_specs, out_specs=out_specs, check_vma=False
    )
```

```python
import functools
import math

import jax
import jax.numpy as jnp
from jax import lax
from jax.experimental import pallas as pl
from jax.experimental.pallas import tpu as pltpu
from jax.sharding import PartitionSpec as P

HD = 128
LANES = 128
ROW_TILE = 16
VMEM_LIMIT = 12 * 1024 * 1024
EARLY = 256

IN_VMEM = pl.BlockSpec(memory_space=pltpu.VMEM)
ANYWHERE = pl.BlockSpec(memory_space=pl.ANY)


def call(
    kernel,
    out_shape,
    in_specs,
    out_specs,
    name,
    flops=0,
    moved=0,
    scratch_shapes=(),
    vmem=VMEM_LIMIT,
):
    return pl.pallas_call(
        kernel,
        out_shape=out_shape,
        in_specs=in_specs,
        out_specs=out_specs,
        scratch_shapes=scratch_shapes,
        name=name,
        cost_estimate=pl.CostEstimate(flops=flops, bytes_accessed=moved, transcendentals=0),
        compiler_params=pltpu.CompilerParams(vmem_limit_bytes=vmem),
    )


def in_hbm(array):
    return pltpu.with_memory_space_constraint(array, pltpu.HBM)


def shift(array, axis, size, step):
    return lax.ppermute(array, axis, [(i, (i + step) % size) for i in range(size)])


LINE_OF_FOUR = (
    ((2, 0, 3, 1), (1, 0, 3, 2)),
    ((3, 2, 1, 0), (2, 3, 0, 1)),
    ((1, 3, 0, 2), (3, 2, 1, 0)),
)


def gather_targets(patches, subs):
    if patches == 4 and subs == 2:
        return LINE_OF_FOUR
    return [
        [[(i + step) % patches for i in range(patches)]] * subs
        for step in range(patches - 1, 0, -1)
    ]


def gather(own, patches, subs):
    blocks = [own]
    for targets in gather_targets(patches, subs):
        pairs = [
            (place * subs + sub, targets[sub][place] * subs + sub)
            for place in range(patches)
            for sub in range(subs)
        ]
        blocks.append(lax.ppermute(own, ("patch", "sub"), pairs))
    return blocks


def gather_sources(patches, subs):
    place, core = lax.axis_index("patch"), lax.axis_index("sub")
    sources = [place]
    for targets in gather_targets(patches, subs):
        value = jnp.int32(0)
        for sub in range(subs):
            for source, target in enumerate(targets[sub]):
                here = jnp.logical_and(place == target, core == sub)
                value = jnp.where(here, jnp.int32(source), value)
        sources.append(value)
    return sources


def early_weight_kernel(subs, columns, early, weight_ref, out_ref, sems):
    chip = (1 - lax.axis_index("head")) * subs
    copies = []
    for sub in range(subs):
        at = pl.multiple_of((chip + sub) * columns, LANES)
        copies.append(
            pltpu.make_async_copy(
                weight_ref.at[:, pl.ds(at, early)],
                out_ref.at[:, pl.ds(sub * early, early)],
                sems.at[sub],
            )
        )
    for copy in copies:
        copy.start()
    for copy in copies:
        copy.wait()


def stage_kernel(
    patches, subs, q_hbm, held_k_hbm, held_v_hbm, q_ref, products_ref, values_ref, keys_ref, sems
):
    rows, width = q_ref.shape
    sources = gather_sources(patches, subs)
    copies = [pltpu.make_async_copy(q_hbm, q_ref, sems.at[0])]
    for i, source in enumerate(sources):
        at = pl.multiple_of(source * rows, rows)
        for n, (held, ref) in enumerate(((held_k_hbm, keys_ref), (held_v_hbm, values_ref))):
            copies.append(
                pltpu.make_async_copy(
                    held.at[pl.ds(at, rows), :],
                    ref.at[i * rows : (i + 1) * rows, :],
                    sems.at[1 + 2 * i + n],
                )
            )
    for copy in copies:
        copy.start()
    for copy in copies:
        copy.wait()
    for head in range(width // HD):
        cols = slice(head * HD, (head + 1) * HD)
        products_ref[head] = dot_transposed(q_ref[:, cols], keys_ref[:, cols])


def dot_transposed(a, b):
    return lax.dot_general(
        a, b, (((1,), (1,)), ((), ())), preferred_element_type=jnp.float32
    )


def attention_kernel(scale, q_ref, products_ref, values_ref, *refs):
    block_refs, out_ref = refs[:-1], refs[-1]
    rows, width = q_ref.shape
    blocks = jnp.concatenate([ref[...] for ref in block_refs], axis=0)
    heads = [slice(at, at + HD) for at in range(0, width, HD)]
    products = [
        products_ref[n] + dot_transposed(q_ref[:, cols], blocks[:, cols])
        for n, cols in enumerate(heads)
    ]
    highest = [jnp.max(p, axis=1, keepdims=True) for p in products]
    weights = [jnp.exp((p - h) * scale) for p, h in zip(products, highest)]
    totals = [jnp.sum(w, axis=1, keepdims=True) for w in weights]
    high = [w.astype(jnp.bfloat16) for w in weights]
    low = [(w - h.astype(jnp.float32)).astype(jnp.bfloat16) for w, h in zip(weights, high)]
    sums = [
        jnp.dot(
            jnp.concatenate([high[n], low[n]], axis=0),
            jnp.concatenate(
                [values_ref[:, cols], blocks[:, width + cols.start : width + cols.stop]], axis=1
            ),
            preferred_element_type=jnp.float32,
        )
        for n, cols in enumerate(heads)
    ]
    for cols, total, both in zip(heads, totals, sums):
        both = both[:rows] + both[rows:]
        out_ref[:, cols] = ((both[:, :HD] + both[:, HD:]) / total).astype(jnp.bfloat16)


def block_dot(a_ref, weight_ref, start, columns):
    if start is None:
        weight = weight_ref[...]
    else:
        weight = weight_ref[:, pl.ds(pl.multiple_of(start, LANES), columns)]
    return jnp.dot(a_ref[...], weight, preferred_element_type=jnp.float32)


def products(start, columns, refs):
    total = 0.0
    for attended_ref, weight_ref in zip(refs[::2], refs[1::2]):
        total = total + block_dot(attended_ref, weight_ref, start, columns)
    return total


def sent_term_kernel(start, *refs):
    out_ref = refs[-1]
    total = products(start(), out_ref.shape[1], refs[:-1])
    out_ref[...] = total.astype(jnp.bfloat16)


def base_kernel(start, hidden_ref, gate_ref, *refs):
    out_ref = refs[-1]
    total = products(start(), out_ref.shape[1], refs[:-1])
    out_ref[...] = hidden_ref[...].astype(jnp.float32) + gate_ref[...] * total


def final_kernel(early, blocks, base_ref, gate_ref, *refs):
    arrived_refs, (out_ref, result, sems) = refs[:-3], refs[-3:]
    rows = base_ref.shape[0] // blocks
    copies = []
    for n in range(blocks):
        at = slice(n * rows, (n + 1) * rows)
        total = 0.0
        for ref in arrived_refs:
            total = total + ref[at, :].astype(jnp.float32)
        if early:
            result[at, :early] = base_ref[at, :early].astype(jnp.bfloat16)
        total = base_ref[at, early:] + gate_ref[:, early:] * total
        result[at, early:] = total.astype(jnp.bfloat16)
        copies.append(pltpu.make_async_copy(result.at[at, :], out_ref.at[at, :], sems.at[n]))
        copies[n].start()
    for copy in copies:
        copy.wait()


def pack_kernel(early, attended_ref, weight_ref, out_ref):
    rows, width = attended_ref.shape
    other = pl.multiple_of((1 - lax.axis_index("sub")) * early, LANES)
    out_ref[:rows, :width] = attended_ref[...]
    out_ref[rows:, :early] = weight_ref[:, pl.ds(other, early)]


def early_kernel(early, base_ref, gate_ref, attended_ref, weight_ref, packed_ref, out_ref):
    rows, width = attended_ref.shape
    mine = pl.multiple_of(lax.axis_index("sub") * early, LANES)
    total = jnp.dot(
        attended_ref[...],
        weight_ref[:, pl.ds(mine, early)],
        preferred_element_type=jnp.float32,
    ) + jnp.dot(
        packed_ref[:rows, :width], packed_ref[rows:, :early], preferred_element_type=jnp.float32
    )
    out_ref[...] = base_ref[...]
    out_ref[:, :early] = base_ref[:, :early] + gate_ref[:, :early] * total


def solution(mesh):
    patches, heads, subs = mesh.shape["patch"], mesh.shape["head"], mesh.shape["sub"]

    def per_device(
        queries, held_keys, held_values, key_change, value_change, out_weight, hidden_in, gate
    ):
        rows, width = queries.shape
        columns = hidden_in.shape[1]

        early = EARLY if heads == 2 and columns % LANES == 0 and columns > 4 * LANES else 0
        if early:
            with jax.named_scope("early_weight"):
                early_weight = call(
                    functools.partial(early_weight_kernel, subs, columns, early),
                    jax.ShapeDtypeStruct((width, subs * early), jnp.bfloat16),
                    [ANYWHERE],
                    IN_VMEM,
                    "early_weight",
                    moved=4 * width * subs * early,
                    scratch_shapes=[pltpu.SemaphoreType.DMA((subs,))],
                )(in_hbm(out_weight))
                key_change, value_change, early_weight = lax.optimization_barrier(
                    (key_change, value_change, early_weight)
                )

        with jax.named_scope("residual_gather"):
            low = jnp.float32(-jnp.inf)
            residual = jnp.maximum(
                lax.pad(key_change, low, ((0, 0, 0), (0, width, 0))),
                lax.pad(value_change, low, ((0, 0, 0), (width, 0, 0))),
            ).astype(jnp.bfloat16)
            blocks = gather(residual, patches, subs)

        with jax.named_scope("weight_swap"):
            weights = [out_weight] + [shift(out_weight, "sub", subs, i) for i in range(1, subs)]

        if early:
            with jax.named_scope("early_weight"):
                early_weight = shift(early_weight, "head", heads, 1)

        def weight_and_start(i, step, skip=0):
            def start():
                to = lax.rem(lax.axis_index("head") + step, heads) * subs + lax.axis_index("sub")
                return to * columns + skip

            if columns % LANES == 0:
                return weights[i], start
            return lax.dynamic_slice(weights[i], (0, start()), (width, columns)), lambda: None

        def pairs_and_start(step, skip=0):
            pairs = [
                x
                for i in range(subs)
                for x in (attended_parts[i], weight_and_start(i, step, skip)[0])
            ]
            return pairs, weight_and_start(0, step, skip)[1]

        tokens = rows * patches
        with jax.named_scope("attention"):
            staged_queries, products, values = call(
                functools.partial(stage_kernel, patches, subs),
                [
                    jax.ShapeDtypeStruct((rows, width), jnp.bfloat16),
                    jax.ShapeDtypeStruct((width // HD, rows, tokens), jnp.float32),
                    jax.ShapeDtypeStruct((tokens, width), jnp.bfloat16),
                ],
                [ANYWHERE] * 3,
                [IN_VMEM] * 3,
                "stage",
                flops=2_000_000_000,
                scratch_shapes=[
                    pltpu.VMEM((tokens, width), jnp.bfloat16),
                    pltpu.SemaphoreType.DMA((1 + 2 * patches,)),
                ],
            )(in_hbm(queries), in_hbm(held_keys), in_hbm(held_values))
            attended = call(
                functools.partial(attention_kernel, 1.0 / math.sqrt(HD)),
                jax.ShapeDtypeStruct((rows, width), jnp.bfloat16),
                [IN_VMEM] * (3 + len(blocks)),
                IN_VMEM,
                "attention",
                flops=2_000_000_000,
            )(staged_queries, products, values, *blocks)

        with jax.named_scope("attended_swap"):
            attended_parts = [attended] + [
                shift(attended, "sub", subs, i) for i in range(1, subs)
            ]
            if early:
                other_attended = shift(attended, "head", heads, 1)

        term = jax.ShapeDtypeStruct((rows, columns), jnp.float32)
        sent = jax.ShapeDtypeStruct((rows, columns - early), jnp.bfloat16)
        product_flops = 2 * rows * width * columns
        with jax.named_scope("projection"):
            arrived = []
            for step in range(1, heads):
                pairs, start = pairs_and_start(step, early)
                total = call(
                    functools.partial(sent_term_kernel, start),
                    sent,
                    [IN_VMEM] * len(pairs),
                    IN_VMEM,
                    "sent_term",
                    2 * product_flops,
                )(*pairs)
                arrived.append(shift(total, "head", heads, step))
            gate_row = gate.reshape(1, columns)
            pairs, start = pairs_and_start(0)
            base = call(
                functools.partial(base_kernel, start),
                term,
                [IN_VMEM] * (2 + len(pairs)),
                IN_VMEM,
                "base",
                2 * product_flops,
            )(hidden_in, gate_row, *pairs)
            if early:
                packed = call(
                    functools.partial(pack_kernel, early),
                    jax.ShapeDtypeStruct((rows + width, max(early, width)), jnp.bfloat16),
                    [IN_VMEM] * 2,
                    IN_VMEM,
                    "pack",
                )(other_attended, early_weight)
                packed = shift(packed, "sub", subs, 1)
                base = call(
                    functools.partial(early_kernel, early),
                    term,
                    [IN_VMEM] * 5,
                    IN_VMEM,
                    "early",
                    product_flops // 2,
                )(base, gate_row, other_attended, early_weight, packed)
            row_blocks = 3 if rows % (3 * ROW_TILE) == 0 else 1
            return call(
                functools.partial(final_kernel, early, row_blocks),
                jax.ShapeDtypeStruct((rows, columns), jnp.bfloat16),
                [IN_VMEM] * (2 + len(arrived)),
                ANYWHERE,
                "final",
                moved=rows * columns * 8,
                scratch_shapes=[
                    pltpu.VMEM((rows, columns), jnp.bfloat16),
                    pltpu.SemaphoreType.DMA((row_blocks,)),
                ],
            )(base, gate_row, *arrived)

    in_specs = (
        P(("groups", "patch"), ("head", "sub")),
        P("groups", ("head", "sub")),
        P("groups", ("head", "sub")),
        P(("groups", "patch"), ("head", "sub")),
        P(("groups", "patch"), ("head", "sub")),
        P(("head", "sub"), None),
        P(("groups", "patch"), ("head", "sub")),
        P(("groups", "head", "sub")),
    )
    out_specs = P(("groups", "patch"), ("head", "sub"))
    return jax.shard_map(
        per_device, mesh=mesh, in_specs=in_specs, out_specs=out_specs, check_vma=False
    )
```
